32 devices in a mesh: dp: 16 (over z, y, x), head: 2 (over core).
Axes of the slice: x: 2, y: 2, z: 4, core: 2. Of those that a mesh axis runs over, the one named last changes fastest.
Arguments:
- tokens: bfloat16 [256, 32, 32, 128], P('dp'), may hold values from -6 to 6
- cotangent: bfloat16 [256, 32, 32, 128], P('dp'), may hold values from -6 to 6
- resolution: int32 [256], P('dp'), may hold values from 8 to 16, as said below
- live_images: int32 [256], P('dp'), may hold values from 1 to 16, as said below
- entry_weight: float32 [3, 128, 128], P(None, 'dp', 'head'), may hold values from -0.5 to 0.5
- entry_momentum: float32 [3, 128, 128], P(None, 'dp', 'head'), may hold values from -320 to 320
- entry_average: float32 [3, 128, 128], P(None, 'dp', 'head'), may hold values from -1.25 to 1.25
- mixing_weight: float32 [128, 128], P('head', 'dp'), may hold values from -1 to 1
- mixing_momentum: float32 [128, 128], P('head', 'dp'), may hold values from -1536 to 1536
- mixing_average: float32 [128, 128], P('head', 'dp'), may hold values from -2.5 to 2.5
- expand_weight: float32 [128, 1024], P('dp', 'head'), may hold values from -0.5 to 0.5
- expand_momentum: float32 [128, 1024], P('dp', 'head'), may hold values from -768 to 768
- expand_average: float32 [128, 1024], P('dp', 'head'), may hold values from -1.25 to 1.25
- shrink_weight: float32 [1024, 128], P('head', 'dp'), may hold values from -0.25 to 0.25
- shrink_momentum: float32 [1024, 128], P('head', 'dp'), may hold values from -1536 to 1536
- shrink_average: float32 [1024, 128], P('head', 'dp'), may hold values from -0.625 to 0.625
- reduce_weight: float32 [2560, 128], P('dp', 'head'), may hold values from -0.1875 to 0.1875
- reduce_momentum: float32 [2560, 128], P('dp', 'head'), may hold values from -160 to 160
- reduce_average: float32 [2560, 128], P('dp', 'head'), may hold values from -0.5 to 0.5
- norm_params: float32 [2, 4, 128], replicated, may hold values from -1.2 to 1.5
- norm_momentum: float32 [2, 4, 128], replicated, may hold values from -1536 to 1536
- norm_average: float32 [2, 4, 128], replicated, may hold values from -6 to 6
- value_filter: float32 [2, 9, 64], P(None, None, 'head'), may hold values from -2 to 2
- value_momentum: float32 [2, 9, 64], P(None, None, 'head'), may hold values from -768 to 768
- value_average: float32 [2, 9, 64], P(None, None, 'head'), may hold values from -5 to 5
- hidden_filter: float32 [9, 1024], P(None, 'head'), may hold values from -2 to 2
- hidden_momentum: float32 [9, 1024], P(None, 'head'), may hold values from -640 to 640
- hidden_average: float32 [9, 1024], P(None, 'head'), may hold values from -5 to 5
Outputs:
- output: bfloat16 [256, 32, 32, 128], P('dp')
- input_grad: float32 [256, 32, 32, 128], P('dp')
- entry_velocity: float32 [3, 128, 128], P(None, 'dp', 'head')
- entry_updated: float32 [3, 128, 128], P(None, 'dp', 'head')
- entry_smoothed: float32 [3, 128, 128], P(None, 'dp', 'head')
- mixing_velocity: float32 [128, 128], P('head', 'dp')
- mixing_updated: float32 [128, 128], P('head', 'dp')
- mixing_smoothed: float32 [128, 128], P('head', 'dp')
- expand_velocity: float32 [128, 1024], P('dp', 'head')
- expand_updated: float32 [128, 1024], P('dp', 'head')
- expand_smoothed: float32 [128, 1024], P('dp', 'head')
- shrink_velocity: float32 [1024, 128], P('head', 'dp')
- shrink_updated: float32 [1024, 128], P('head', 'dp')
- shrink_smoothed: float32 [1024, 128], P('head', 'dp')
- reduce_velocity: float32 [2560, 128], P('dp', 'head')
- reduce_updated: float32 [2560, 128], P('dp', 'head')
- reduce_smoothed: float32 [2560, 128], P('dp', 'head')
- norm_velocity: float32 [2, 4, 128], replicated
- norm_updated: float32 [2, 4, 128], replicated
- norm_smoothed: float32 [2, 4, 128], replicated
- value_velocity: float32 [2, 9, 64], P(None, None, 'head')
- value_updated: float32 [2, 9, 64], P(None, None, 'head')
- value_smoothed: float32 [2, 9, 64], P(None, None, 'head')
- hidden_velocity: float32 [9, 1024], P(None, 'head')
- hidden_updated: float32 [9, 1024], P(None, 'head')
- hidden_smoothed: float32 [9, 1024], P(None, 'head')
The draws below stay inside these ranges and needn't reach their ends.
Inputs may be any that keep to these rules, and one draw needn't show every extreme that they name: `resolution`: 32 is a multiple of it; every image of a grid is a square of resolution x resolution patches, numbered in raster order. `live_images`: the images that hold data are the first ones in raster order; at most (32 // resolution) ** 2.
All inputs are finite; a program needn't handle non-finite values.
Results may differ from the reference program's by a relative error of at most 0.019.
Values may be sent and summed in bfloat16 or wider, within the bound.
A program may use at most 704 MiB of HBM per device.

```python
import jax
import jax.numpy as jnp
from jax import lax

D = 128
FF = 1024
SR_WIDE = 4
SR_NARROW = 2
GRID_SIDE = 32
GRIDS_DEV = 16
GRIDS = 256
TOKENS = 262144


def grid_resolution(key):
    key = jax.random.fold_in(key, 11)
    choose = jax.random.randint(key, (GRIDS,), 0, 2)
    index = jnp.arange(GRIDS, dtype=jnp.int32)
    choose = jnp.where(index == GRIDS - 1, 0, choose)
    choose = jnp.where(index == 0, 1, choose)
    return (8 + 8 * choose).astype(jnp.int32)


def draw_resolution(key, part):
    return grid_resolution(key)


def draw_live_images(key, part):
    sides = grid_resolution(key)
    key = jax.random.fold_in(key, 13)
    index = jnp.arange(GRIDS, dtype=jnp.int32)
    images = (GRID_SIDE // sides) ** 2
    base = images * (GRIDS + 2 * index) // (3 * GRIDS)
    jitter = jax.random.randint(key, (GRIDS,), -1, 2)
    living = jnp.clip(base + jitter, 1, images)
    living = jnp.where(index == GRIDS - 1, images, living)
    living = jnp.where(index == 0, 1, living)
    return living.astype(jnp.int32)


def draw_norm_params(key, part):
    key = jax.random.fold_in(key, 5)
    first_key, second_key = jax.random.split(key)
    gains = jax.random.uniform(first_key, (1, 4, D), jnp.float32, 0.5, 1.5)
    shifts = jnp.clip(0.3 * jax.random.normal(second_key, (1, 4, D), jnp.float32), -1.2, 1.2)
    return jnp.concatenate([gains, shifts], 0)


def steps_of(stream_key, extent, cuts, low, top_value):
    gain, own = 1.0, jax.random.fold_in(stream_key, 6)
    for position, shards_of in cuts:
        heights = jnp.exp(jax.random.uniform(jax.random.fold_in(own, position), (shards_of,), jnp.float32, low / len(cuts), top_value / len(cuts)))
        gain = gain * jnp.repeat(heights, extent[position] // shards_of).reshape([-1 if axis == position else 1 for axis in range(len(extent))])
    return gain


def noise(rng, extent, deviation, bound, cuts=(), held_as=jnp.bfloat16):
    drawn = deviation * jax.random.normal(rng, extent, jnp.float32)
    if cuts:
        drawn = drawn * steps_of(rng, extent, cuts, -0.22, 0.18)
    return jnp.clip(drawn, -bound, bound).astype(held_as)


def setup_inputs(seed: int = 0) -> dict:
    key_of = jax.random.split(jax.random.key(seed), 29)
    return {
        "tokens": noise(key_of[0], (GRIDS, GRID_SIDE, GRID_SIDE, D), 1.0, 6.0, ((0, 16),)),
        "cotangent": noise(key_of[1], (GRIDS, GRID_SIDE, GRID_SIDE, D), 1.0, 6.0, ((0, 16),)),
        "resolution": draw_resolution(jax.random.fold_in(key_of[28], 71), 0),
        "live_images": draw_live_images(jax.random.fold_in(key_of[28], 71), 0),
        "entry_weight": noise(key_of[4], (3, D, D), D ** -0.5, 0.5, ((1, 16), (2, 2)), jnp.float32),
        "entry_momentum": noise(key_of[5], (3, D, D), (0.1 * TOKENS ** 0.5), 320.0, ((1, 16), (2, 2)), jnp.float32),
        "entry_average": noise(key_of[6], (3, D, D), (D ** -0.5), 1.25, ((1, 16), (2, 2)), jnp.float32),
        "mixing_weight": noise(key_of[7], (D, D), (D // 4) ** -0.5, 1.0, ((0, 2), (1, 16)), jnp.float32),
        "mixing_momentum": noise(key_of[8], (D, D), (0.5 * TOKENS ** 0.5), 1536.0, ((0, 2), (1, 16)), jnp.float32),
        "mixing_average": noise(key_of[9], (D, D), (2 * D ** -0.5), 2.5, ((0, 2), (1, 16)), jnp.float32),
        "expand_weight": noise(key_of[10], (D, FF), D ** -0.5, 0.5, ((0, 16), (1, 2)), jnp.float32),
        "expand_momentum": noise(key_of[11], (D, FF), (0.25 * TOKENS ** 0.5), 768.0, ((0, 16), (1, 2)), jnp.float32),
        "expand_average": noise(key_of[12], (D, FF), (D ** -0.5), 1.25, ((0, 16), (1, 2)), jnp.float32),
        "shrink_weight": noise(key_of[13], (FF, D), (FF // 2) ** -0.5, 0.25, ((0, 2), (1, 16)), jnp.float32),
        "shrink_momentum": noise(key_of[14], (FF, D), (0.5 * TOKENS ** 0.5), 1536.0, ((0, 2), (1, 16)), jnp.float32),
        "shrink_average": noise(key_of[15], (FF, D), ((FF // 2) ** -0.5), 0.625, ((0, 2), (1, 16)), jnp.float32),
        "reduce_weight": noise(key_of[16], ((SR_WIDE ** 2 + SR_NARROW ** 2) * D, D), (SR_WIDE ** 2 * D // 2) ** -0.5, 0.1875, ((0, 16), (1, 2)), jnp.float32),
        "reduce_momentum": noise(key_of[17], ((SR_WIDE ** 2 + SR_NARROW ** 2) * D, D), (0.05 * TOKENS ** 0.5), 160.0, ((0, 16), (1, 2)), jnp.float32),
        "reduce_average": noise(key_of[18], ((SR_WIDE ** 2 + SR_NARROW ** 2) * D, D), ((SR_WIDE ** 2 * D // 2) ** -0.5), 0.5, ((0, 16), (1, 2)), jnp.float32),
        "norm_params": draw_norm_params(jax.random.fold_in(key_of[28], 71), 0),
        "norm_momentum": noise(key_of[20], (2, 4, D), (0.5 * TOKENS ** 0.5), 1536.0, (), jnp.float32),
        "norm_average": noise(key_of[21], (2, 4, D), 0.5, 6.0, (), jnp.float32),
        "value_filter": noise(key_of[22], (2, 9, D // 2), 9 ** -0.5, 2.0, ((2, 2),), jnp.float32),
        "value_momentum": noise(key_of[23], (2, 9, D // 2), (0.25 * TOKENS ** 0.5), 768.0, ((2, 2),), jnp.float32),
        "value_average": noise(key_of[24], (2, 9, D // 2), 0.33, 5.0, ((2, 2),), jnp.float32),
        "hidden_filter": noise(key_of[25], (9, FF), 9 ** -0.5, 2.0, ((1, 2),), jnp.float32),
        "hidden_momentum": noise(key_of[26], (9, FF), (0.2 * TOKENS ** 0.5), 640.0, ((1, 2),), jnp.float32),
        "hidden_average": noise(key_of[27], (9, FF), 0.33, 5.0, ((1, 2),), jnp.float32),
    }


PRECISE = lax.Precision.HIGHEST
NEGATIVE = -1000000000.0
EPSILON = 1e-06

@jax.custom_vjp
def low(v):
    return lax.optimization_barrier(v.astype(jnp.bfloat16)).astype(jnp.float32)

@jax.custom_vjp
def low_back(v):
    return v

def low_keep(v):
    return (low(v), None)

def low_pass(kept, grad):
    return (grad,)

def back_keep(v):
    return (v, None)

def back_low(kept, grad):
    return (low(grad),)
low.defvjp(low_keep, low_pass)
low_back.defvjp(back_keep, back_low)

def layer_norm(values, norm_gain, norm_shift):
    average = lax.optimization_barrier(jnp.mean(values, -1, keepdims=True))
    centred = values - average
    spread = lax.optimization_barrier(jnp.mean(centred * centred, -1, keepdims=True))
    return centred * lax.rsqrt(spread + EPSILON) * norm_gain + norm_shift

def image_ids(resolution, grid_side, stride):
    cells_side = grid_side // stride
    positions = jnp.arange(cells_side, dtype=jnp.int32) * stride
    across = (grid_side // resolution)[:, None, None]
    row_image = positions[None, :, None] // resolution[:, None, None]
    column_image = positions[None, None, :] // resolution[:, None, None]
    return row_image * across + column_image

def depthwise(values, image_map, weights):
    cells_side = values.shape[1]
    padded = jnp.pad(values, ((0, 0), (1, 1), (1, 1), (0, 0)))
    padded_map = jnp.pad(image_map, ((0, 0), (1, 1), (1, 1)), constant_values=-1)
    summed = jnp.zeros_like(values)
    for offset in range(9):
        row_shift = offset // 3
        column_shift = offset % 3
        same_image = (padded_map[:, row_shift:row_shift + cells_side, column_shift:column_shift + cells_side] == image_map).astype(values.dtype)
        summed = summed + padded[:, row_shift:row_shift + cells_side, column_shift:column_shift + cells_side, :] * same_image[..., None] * weights[offset]
    return summed

def dense(left_side, right_side):
    return jnp.einsum('...d,de->...e', left_side, right_side, precision=PRECISE)

def patch_rows(active, stride):
    count_grids = active.shape[0]
    cells_side = active.shape[1] // stride
    features = active.shape[3]
    blocks = active.reshape(count_grids, cells_side, stride, cells_side, stride, features)
    return blocks.transpose(0, 1, 3, 2, 4, 5).reshape(count_grids, cells_side, cells_side, stride * stride * features)

def forward(weights, inputs, resolution):
    entry_weight, mixing_weight, expand_weight, shrink_weight, reduce_weight, norm_params, value_filter, hidden_filter = weights
    count_grids = inputs.shape[0]
    grid_side = inputs.shape[1]
    features = inputs.shape[3]
    head_width = features // 4
    scaling = head_width ** (-0.5)
    positions = grid_side * grid_side
    image_map = image_ids(resolution, grid_side, 1)
    normed = low(layer_norm(inputs, norm_params[0, 0], norm_params[1, 0]))
    queries = low(low_back(dense(normed, low(entry_weight[0]))))
    queries = queries.reshape(count_grids, positions, 2, 2, head_width)
    results = []
    first_row = 0
    for group_index, stride in ((0, SR_WIDE), (1, SR_NARROW)):
        cells_side = grid_side // stride
        keys_count = cells_side * cells_side
        row_count = stride * stride * features
        cell_map = image_ids(resolution, grid_side, stride)
        reduced = low_back(dense(patch_rows(normed, stride), low(reduce_weight[first_row:first_row + row_count])))
        first_row = first_row + row_count
        reduced = low(jax.nn.gelu(layer_norm(reduced, norm_params[0, 1 + group_index], norm_params[1, 1 + group_index]), approximate=False))
        key_value = dense(reduced, low(entry_weight[1 + group_index])).reshape(count_grids, cells_side, cells_side, 2, 2, head_width)
        keys_low = low(low_back(key_value[..., 0, :])).reshape(count_grids, keys_count, 2, head_width)
        values_raw = low_back(key_value[..., 1, :].reshape(count_grids, cells_side, cells_side, 2 * head_width))
        enhanced = low(low_back(values_raw + depthwise(values_raw, cell_map, value_filter[group_index])))
        enhanced = enhanced.reshape(count_grids, keys_count, 2, head_width)
        scores = low_back(jnp.einsum('bqje,bkje->bjkq', queries[:, :, :, group_index, :], keys_low, precision=PRECISE))
        same_image = cell_map.reshape(count_grids, 1, keys_count, 1) == image_map.reshape(count_grids, 1, 1, positions)
        scores = jnp.where(same_image, scaling * scores, NEGATIVE)
        weights_soft = jax.nn.softmax(scores, axis=2)
        results.append(jnp.einsum('bjkq,bkje->bqje', low(weights_soft), enhanced, precision=PRECISE))
    mixed = jnp.stack(results, 3).reshape(count_grids, grid_side, grid_side, features)
    mixed = low(low_back(mixed))
    attended = low_back(dense(mixed, low(mixing_weight)))
    middle = inputs + attended
    second = low(layer_norm(middle, norm_params[0, 3], norm_params[1, 3]))
    hidden = low_back(dense(second, low(expand_weight)))
    hidden = hidden + depthwise(hidden, image_map, hidden_filter)
    activated = low(jax.nn.gelu(hidden, approximate=False))
    return middle + low_back(dense(activated, low(shrink_weight)))

def advance(weight, moment, average, gradient, step_rate, weight_decay):
    gradient = gradient + weight_decay * weight
    moment = 0.9 * moment + gradient
    weight = weight - step_rate * (gradient + 0.9 * moment)
    return (moment, weight, 0.8 * average + 0.2 * weight)

def add_trees(summed, addend):
    return summed + addend

def reference(tokens, cotangent, resolution, live_images, entry_weight, entry_momentum, entry_average, mixing_weight, mixing_momentum, mixing_average, expand_weight, expand_momentum, expand_average, shrink_weight, shrink_momentum, shrink_average, reduce_weight, reduce_momentum, reduce_average, norm_params, norm_momentum, norm_average, value_filter, value_momentum, value_average, hidden_filter, hidden_momentum, hidden_average):
    weights = (entry_weight, mixing_weight, expand_weight, shrink_weight, reduce_weight, norm_params, value_filter, hidden_filter)
    count_grids = tokens.shape[0]
    grid_side = tokens.shape[1]
    blocks_count = count_grids // GRIDS_DEV

    def to_blocks(array):
        return array.reshape((blocks_count, GRIDS_DEV) + array.shape[1:])
    inputs = to_blocks(tokens.astype(jnp.float32))
    cotangents = to_blocks(cotangent.astype(jnp.float32))
    resolutions = to_blocks(resolution)
    lives = to_blocks(live_images)
    zero_tree = jax.tree.map(jnp.zeros_like, weights)

    def visit(running, block_item):
        sums, live_total = running
        block_inputs, block_cotangent, block_resolution, block_live = block_item
        image_map = image_ids(block_resolution, grid_side, 1)
        live_mask = (image_map < block_live[:, None, None]).astype(block_cotangent.dtype)

        def local_forward(params, values):
            return forward(params, values, block_resolution)
        outputs, pullback = jax.vjp(local_forward, weights, block_inputs)
        weight_grads, input_grads = pullback(block_cotangent * live_mask[..., None])
        sums = jax.tree.map(add_trees, sums, weight_grads)
        return ((sums, live_total + jnp.sum(live_mask)), (outputs.astype(jnp.bfloat16), input_grads))
    (sums, live_total), (outputs, input_grads) = lax.scan(visit, (zero_tree, jnp.zeros((), jnp.float32)), (inputs, cotangents, resolutions, lives))
    factor = TOKENS / live_total
    output = outputs.reshape(tokens.shape)
    input_grad = factor * input_grads.reshape(tokens.shape)
    rate_unit = TOKENS ** (-0.5)
    entry_velocity, entry_updated, entry_smoothed = advance(entry_weight, entry_momentum, entry_average, factor * sums[0], 0.3 * rate_unit, 0.05)
    mixing_velocity, mixing_updated, mixing_smoothed = advance(mixing_weight, mixing_momentum, mixing_average, factor * sums[1], 0.12 * rate_unit, 0.05)
    expand_velocity, expand_updated, expand_smoothed = advance(expand_weight, expand_momentum, expand_average, factor * sums[2], 0.12 * rate_unit, 0.05)
    shrink_velocity, shrink_updated, shrink_smoothed = advance(shrink_weight, shrink_momentum, shrink_average, factor * sums[3], 0.03 * rate_unit, 0.05)
    reduce_velocity, reduce_updated, reduce_smoothed = advance(reduce_weight, reduce_momentum, reduce_average, factor * sums[4], 0.1 * rate_unit, 0.05)
    norm_velocity, norm_updated, norm_smoothed = advance(norm_params, norm_momentum, norm_average, factor * sums[5], 0.2 * rate_unit, 0.0)
    value_velocity, value_updated, value_smoothed = advance(value_filter, value_momentum, value_average, factor * sums[6], 0.4 * rate_unit, 0.05)
    hidden_velocity, hidden_updated, hidden_smoothed = advance(hidden_filter, hidden_momentum, hidden_average, factor * sums[7], 0.5 * rate_unit, 0.05)
    return (output, input_grad, entry_velocity, entry_updated, entry_smoothed, mixing_velocity, mixing_updated, mixing_smoothed, expand_velocity, expand_updated, expand_smoothed, shrink_velocity, shrink_updated, shrink_smoothed, reduce_velocity, reduce_updated, reduce_smoothed, norm_velocity, norm_updated, norm_smoothed, value_velocity, value_updated, value_smoothed, hidden_velocity, hidden_updated, hidden_smoothed)
```

```python
import math

import jax
import jax.numpy as jnp
import numpy as np
from jax import lax
from jax.experimental import pallas as pl
from jax.experimental.pallas import tpu as pltpu
from jax.sharding import PartitionSpec as P

BF = jnp.bfloat16
F32 = jnp.float32
EPSILON = 1e-06
HALF = 16
MASKED = -1e9
NN = (((1,), (0,)), ((), ()))
NT = (((1,), (1,)), ((), ()))
TN = (((0,), (0,)), ((), ()))


def mm(a, b, dims=NN):
    return lax.dot_general(a, b, dims, preferred_element_type=F32)


def block_of(a4, b4):
    return (a4 % 2) * 8 + (b4 % 2) * 4 + (a4 // 2) * 2 + b4 // 2


def place_of(block):
    return ((block >> 1) & 1) * 2 + (block >> 3), (block & 1) * 2 + ((block >> 2) & 1)


def order_matrix():
    perm = np.zeros((256, 256), np.float32)
    for block in range(16):
        a4, b4 = place_of(block)
        for ci in range(4):
            for ck in range(4):
                perm[block * 16 + ci * 4 + ck, (4 * ci + a4) * HALF + 4 * ck + b4] = 1
    return perm


def cell_shifts():
    places = []
    for ci in range(4):
        for ck in range(4):
            places.append((0, ci, ck, ci // 2, ck // 2))
    for ah in range(2):
        for bh in range(2):
            for ci in range(4):
                for ck in range(4):
                    places.append((1, 2 * ci + ah, 2 * ck + bh, ci // 2, ck // 2))
    index = {p[:3]: n for n, p in enumerate(places)}
    shifts = np.zeros((2, 9, 80, 80), np.float32)
    for n, (g, i, k, si, sk) in enumerate(places):
        for tap in range(9):
            other = index.get((g, i + tap // 3 - 1, k + tap % 3 - 1))
            if other is not None:
                shifts[0, tap, n, other] = 1
                if places[other][3:] == (si, sk):
                    shifts[1, tap, n, other] = 1
    return shifts.reshape(2, 720, 80)


def score_bias():
    rows = np.array([(n % 16) for _ in range(2) for n in list(range(16)) + list(range(64))])
    cols = np.arange(256) % 16

    def image(n):
        return (n // 8) * 2 + (n % 4) // 2

    return np.where(image(rows)[:, None] == image(cols)[None, :], 0.0, MASKED).astype(np.float32)


def shift_masks():
    masks = np.zeros((2, 4, 16, 128), np.float32)
    for fine in range(2):
        for ci in range(4):
            for ck in range(4):
                row = ci * 4 + ck
                for n, (d, e) in enumerate(((1, 0), (-1, 0), (0, 1), (0, -1))):
                    ni, nk = ci + d, ck + e
                    ok = 0 <= ni < 4 and 0 <= nk < 4
                    if fine:
                        ok = ok and ni // 2 == ci // 2 and nk // 2 == ck // 2
                    masks[fine, n, row] = ok
    return masks


def normalise(x):
    centred = x - jnp.mean(x, -1, keepdims=True)
    scale = lax.rsqrt(jnp.mean(centred * centred, -1, keepdims=True) + EPSILON)
    return centred * scale, scale


def normalise_back(grad, unit, scale):
    return scale * (
        grad
        - jnp.mean(grad, -1, keepdims=True)
        - unit * jnp.mean(grad * unit, -1, keepdims=True)
    )


def gelu_pair(h):
    density = jnp.exp(-0.5 * (h * h))
    t = 1.0 / (1.0 + (0.3275911 * math.sqrt(0.5)) * jnp.abs(h))
    poly = 1.061405429 * 0.5
    for c in (-1.453152027, 1.421413741, -0.284496736, 0.254829592):
        poly = poly * t + c * 0.5
    tail = poly * t * density
    below = jnp.where(h >= 0, 1.0 - tail, tail)
    return h * below, below + h * density * (1.0 / math.sqrt(2 * math.pi))


def block_kernel(
    info,
    tokens,
    cotangent,
    entry,
    mixing_t,
    expand,
    shrink_t,
    reduce_w,
    norms,
    value_filter,
    hidden_filter,
    perm,
    perm_t,
    shifts,
    bias,
    edge,
    out,
    input_grad,
    d_entry,
    d_mixing_t,
    d_expand,
    d_shrink_t,
    d_reduce,
    d_norm,
    d_value,
    d_hidden,
    conv_w,
    key_value_w,
    im2col,
    im2col_t,
    g_low,
    m_sum,
    folds,
    d_key_value,
    probs,
    normed_s,
    queries_s,
    *,
    steps,
):
    step = pl.program_id(0)
    ff = expand.shape[1]
    lane = lax.broadcasted_iota(jnp.int32, (128, 128), 1)
    first_lanes = lane % 64 < 32

    @pl.when(step == 0)
    def prepare():
        for tap in range(9):
            gain = hidden_filter[tap : tap + 1, :]
            if tap == 4:
                gain = gain + 1.0
            conv_w[tap * 128 : (tap + 1) * 128, :] = (expand[...].astype(F32) * gain).astype(BF)
        for g in range(2):
            w = entry[1 + g].astype(F32)
            if g == 0:
                keys, vals = w, pltpu.roll(w, 96, 1)
                keep = first_lanes
            else:
                keys, vals = pltpu.roll(w, 32, 1), w
                keep = jnp.logical_not(first_lanes)
            key_value_w[g, :, :128] = jnp.where(keep, keys, 0.0).astype(BF)
            key_value_w[g, :, 128:] = jnp.where(keep, vals, 0.0).astype(BF)
        for ref in (d_entry, d_mixing_t, d_shrink_t, d_reduce, d_norm, d_value, m_sum, d_key_value):
            ref[...] = jnp.zeros_like(ref)

    fine = info[0, step]
    alive = info[1, step]
    fine_f = fine.astype(F32)

    def ordered(ref):
        parts = [
            ref[0, a * 16 : a * 16 + 16, b * 16 : b * 16 + 16, :].reshape(256, 128)
            for a in range(2)
            for b in range(2)
        ]
        rows = mm(perm[...], jnp.concatenate(parts, 1))
        return jnp.stack(
            [rows[:, q * 128 : q * 128 + 128].reshape(16, 16, 128) for q in range(4)], 1
        ).reshape(1024, 128)

    def restore(value, ref):
        blocks = value.reshape(16, 4, 16, 128)
        rows = mm(
            perm_t[...],
            jnp.concatenate([blocks[:, q].reshape(256, 128) for q in range(4)], 1),
        ).astype(BF)
        for q in range(4):
            a, b = q // 2, q % 2
            ref[0, a * 16 : a * 16 + 16, b * 16 : b * 16 + 16, :] = rows[
                :, q * 128 : q * 128 + 128
            ].reshape(16, 16, 128)

    def of_quadrant(value, q, blocks):
        return value.reshape(blocks, 4, 16, 128)[:, q].reshape(blocks * 16, 128)

    def of_quadrants(parts, blocks):
        return jnp.stack([p.reshape(blocks, 16, 128) for p in parts], 1).reshape(
            blocks * 64, 128
        )

    def gain(n):
        return norms[0, n : n + 1, :]

    def shift_by(n):
        return norms[1, n : n + 1, :]

    def add_norm(n, grad, unit):
        d_norm[n : n + 1, :] += jnp.sum(grad * unit, 0, keepdims=True)
        d_norm[4 + n : 5 + n, :] += jnp.sum(grad, 0, keepdims=True)

    x = ordered(tokens)
    unit1, scale1 = normalise(x)
    normed = (unit1 * gain(0) + shift_by(0)).astype(BF)
    normed_s[...] = normed
    queries_s[...] = mm(normed, entry[0]).astype(BF)
    patches = (
        jnp.concatenate(
            [
                normed_s[block_of(t // 4, t % 4) * 64 : block_of(t // 4, t % 4) * 64 + 64, :]
                for t in range(16)
            ],
            1,
        ),
        jnp.concatenate([normed_s[t * 256 : t * 256 + 256, :] for t in range(4)], 1),
    )
    rows_of = (slice(0, 2048), slice(2048, 2560))
    cell_saved = []
    keys, values = [], []
    for g in range(2):
        reduced = mm(patches[g], reduce_w[rows_of[g], :])
        unit, scale = normalise(reduced)
        act, slope = gelu_pair(unit * gain(1 + g) + shift_by(1 + g))
        cell_low = act.astype(BF)
        pair = mm(cell_low, key_value_w[g])
        keys.append(pair[:, :128].astype(BF))
        values.append(pair[:, 128:])
        cell_saved.append((unit, scale, slope, cell_low))
    keys_all = [
        jnp.concatenate([keys[0][q * 16 : q * 16 + 16], of_quadrant(keys[1], q, 4)], 0)
        for q in range(4)
    ]
    values_all = jnp.concatenate(
        [
            jnp.concatenate([values[0][q * 16 : q * 16 + 16], of_quadrant(values[1], q, 4)], 0)
            for q in range(4)
        ],
        1,
    )
    moves = shifts[pl.ds(fine, 1)][0]
    high = values_all.astype(BF)
    rest = (values_all - high.astype(F32)).astype(BF)
    moved = mm(moves, high) + mm(moves, rest)
    taps4 = jnp.concatenate([value_filter[...]] * 4, 1)
    enhanced = values_all
    for tap in range(9):
        enhanced = enhanced + moved[tap * 80 : tap * 80 + 80] * taps4[tap : tap + 1]
    enhanced = enhanced.astype(BF)
    lane80 = lax.broadcasted_iota(jnp.int32, (80, 128), 1)
    zero80 = jnp.zeros((80, 128), BF)

    def both_heads(rows):
        return jnp.concatenate(
            [jnp.where(lane80 < 64, rows, zero80), jnp.where(lane80 < 64, zero80, rows)], 0
        )

    segments = ((0, 16), (16, 80), (80, 96), (96, 160))
    queries = queries_s[...]
    query_q = [of_quadrant(queries, q, 16) for q in range(4)]
    keys_q = [both_heads(keys_all[q]) for q in range(4)]
    enhanced_q = [both_heads(enhanced[:, q * 128 : q * 128 + 128]) for q in range(4)]
    mixed_parts = []
    scaling = 32**-0.5
    for q in range(4):
        scores = mm(keys_q[q], query_q[q], NT) * scaling + fine_f * bias[...]
        weights = []
        for lo, hi in segments:
            part = scores[lo:hi]
            part = jnp.exp(part - jnp.max(part, 0, keepdims=True))
            weights.append(part / jnp.sum(part, 0, keepdims=True))
        weights = jnp.concatenate(weights, 0)
        probs[q] = weights
        mixed_parts.append(mm(weights.astype(BF), enhanced_q[q], TN))
    mixed = of_quadrants(mixed_parts, 16).astype(BF)
    middle = x + mm(mixed, mixing_t[...], NT)
    unit2, scale2 = normalise(middle)
    second = unit2 * gain(3) + shift_by(3)
    second_low = second.astype(BF)
    second_f = second_low.astype(F32)

    def move(value, rows, columns):
        size = value.shape[0]
        if rows:
            n = 0 if rows > 0 else 1
            value = pltpu.roll(value, (-4 * rows) % size, 0)
            value = (
                value.reshape(size // 16, 16, 128) * edge[pl.ds(fine, 1), n : n + 1][0]
            ).reshape(size, 128)
        if columns:
            n = 2 if columns > 0 else 3
            value = pltpu.roll(value, (-columns) % size, 0)
            value = (
                value.reshape(size // 16, 16, 128) * edge[pl.ds(fine, 1), n : n + 1][0]
            ).reshape(size, 128)
        return value

    def wrap(a4, d):
        return (a4 + d) % 4, (a4 + d) // 4

    moved_blocks = {}
    for block in range(16):
        a4, b4 = place_of(block)
        for tap in range(9):
            na, wa = wrap(a4, tap // 3 - 1)
            nb, wb = wrap(b4, tap % 3 - 1)
            source = block_of(na, nb)
            key = (source, wa, wb)
            if key not in moved_blocks:
                rows = slice(source * 64, source * 64 + 64)
                if wa or wb:
                    moved_blocks[key] = move(second_f[rows], wa, wb).astype(BF)
                else:
                    moved_blocks[key] = second_low[rows]
            im2col[block * 64 : block * 64 + 64, tap * 128 : tap * 128 + 128] = moved_blocks[key]
    for tap in range(9):
        im2col_t[tap * 128 : tap * 128 + 128, :] = im2col[:, tap * 128 : tap * 128 + 128].T

    row16 = lax.broadcasted_iota(jnp.int32, (16, 128), 0)
    within = (row16 // 8) * 4 + (row16 % 4) // 2
    live = jnp.stack(
        [
            jnp.where(
                jnp.where(fine == 1, within + (q // 2) * 8 + (q % 2) * 2, q) < alive, 1.0, 0.0
            )
            for q in range(4)
        ],
        0,
    )
    upstream = (ordered(cotangent).reshape(16, 4, 16, 128) * live[None]).reshape(1024, 128)
    up_low = upstream.astype(BF)
    up_t = up_low.T

    feed = jnp.zeros((1024, 128), F32)
    wide = 256
    for c in range(0, ff, wide):
        cols = slice(c, c + wide)
        hidden = mm(im2col[...], conv_w[:, cols])
        act, slope = gelu_pair(hidden)
        act = act.astype(BF)
        grad = mm(up_low, shrink_t[:, cols]) * slope
        grad = grad.astype(BF)
        g_low[:, cols] = grad
        feed = feed + mm(act, shrink_t[:, cols], NT)
        d_shrink_t[:, cols] += mm(up_t, act)
        m_sum[:, cols] += mm(im2col_t[...], grad)
    restore((middle + feed).astype(BF), out)

    for t in range(0, 9, 2):
        rows = slice(t * 128, min(t + 2, 9) * 128)
        folds[:, rows] = mm(g_low[...], conv_w[rows, :], NT)
    sums = {}
    for block in range(16):
        a4, b4 = place_of(block)
        for tap in range(9):
            na, wa = wrap(a4, tap // 3 - 1)
            nb, wb = wrap(b4, tap % 3 - 1)
            key = (block_of(na, nb), wa, wb)
            sums.setdefault(key, []).append((block, tap))
    second_parts = []
    for block in range(16):
        total = None
        for (source, wa, wb), terms in sums.items():
            if source != block:
                continue
            part = None
            for other, tap in terms:
                term = folds[other * 64 : other * 64 + 64, tap * 128 : tap * 128 + 128]
                part = term if part is None else part + term
            if wa or wb:
                part = move(part, -wa, -wb)
            total = part if total is None else total + part
        second_parts.append(total)
    second_grad = jnp.concatenate(second_parts, 0)
    add_norm(3, second_grad, unit2)
    middle_grad = upstream + normalise_back(second_grad * gain(3), unit2, scale2)
    middle_low = middle_grad.astype(BF)
    d_mixing_t[...] += mm(middle_low, mixed, TN)
    mixed_grad = mm(middle_low, mixing_t[...]).astype(BF)

    query_parts, key_parts, enhanced_parts = [], [], []
    for q in range(4):
        out_grad = of_quadrant(mixed_grad, q, 16)
        weights = probs[q]
        prob_grad = mm(enhanced_q[q], out_grad, NT)
        product = weights * prob_grad
        score_grad = []
        for lo, hi in segments:
            score_grad.append(
                product[lo:hi] - weights[lo:hi] * jnp.sum(product[lo:hi], 0, keepdims=True)
            )
        score_low = (scaling * jnp.concatenate(score_grad, 0)).astype(BF)
        query_parts.append(mm(score_low, keys_q[q], TN))
        key_full = mm(score_low, query_q[q])
        enhanced_full = mm(weights.astype(BF), out_grad)
        key_parts.append(jnp.where(lane80 < 64, key_full[:80], key_full[80:]).astype(BF))
        enhanced_parts.append(
            jnp.where(lane80 < 64, enhanced_full[:80], enhanced_full[80:]).astype(BF)
        )
    query_low = of_quadrants(query_parts, 16).astype(BF)
    enhanced_grad = jnp.concatenate(enhanced_parts, 1)
    moved = mm(moves, enhanced_grad)
    value_grad = enhanced_grad.astype(F32)
    for tap in range(9):
        part = moved[(8 - tap) * 80 : (8 - tap) * 80 + 80]
        value_grad = value_grad + part * taps4[tap : tap + 1]
        row = jnp.sum(part * values_all, 0, keepdims=True)
        d_value[tap : tap + 1, :] += (
            row[:, :128] + row[:, 128:256] + row[:, 256:384] + row[:, 384:]
        )
    value_grad = value_grad.astype(BF)
    value_parts = [value_grad[:, q * 128 : q * 128 + 128] for q in range(4)]
    normed = normed_s[...]
    normed_grad = mm(query_low, entry[0], NT)
    d_entry[0] += mm(normed, query_low, TN)
    for g in range(2):
        if g == 0:
            sides = [jnp.concatenate([p[:16] for p in parts], 0) for parts in (key_parts, value_parts)]
        else:
            sides = [of_quadrants([p[16:] for p in parts], 4) for parts in (key_parts, value_parts)]
        pair = jnp.concatenate(sides, 1)
        unit, scale, slope, cell_low = cell_saved[g]
        d_key_value[g] += mm(cell_low, pair, TN)
        cell_grad = mm(pair, key_value_w[g], NT) * slope
        add_norm(1 + g, cell_grad, unit)
        reduced_low = normalise_back(cell_grad * gain(1 + g), unit, scale).astype(BF)
        d_reduce[rows_of[g], :] += mm(patches[g], reduced_low, TN)
        back = mm(reduced_low, reduce_w[rows_of[g], :], NT)
        if g == 0:
            order = [place_of(block) for block in range(16)]
            order = [a4 * 4 + b4 for a4, b4 in order]
        else:
            order = range(4)
        normed_grad = normed_grad + jnp.concatenate(
            [back[:, t * 128 : t * 128 + 128] for t in order], 0
        )
    add_norm(0, normed_grad, unit1)
    raw = middle_grad + normalise_back(normed_grad * gain(0), unit1, scale1)
    restore(raw.astype(BF), input_grad)

    @pl.when(step == steps - 1)
    def finish():
        weight = expand[...].astype(F32)
        total = None
        for tap in range(9):
            part = m_sum[tap * 128 : tap * 128 + 128, :]
            factor = hidden_filter[tap : tap + 1, :]
            if tap == 4:
                factor = factor + 1.0
            d_hidden[tap : tap + 1, :] = jnp.sum(part * weight, 0, keepdims=True)
            total = part * factor if total is None else total + part * factor
        d_expand[...] = total
        d_entry[1] = jnp.where(
            first_lanes, d_key_value[0, :, :128], pltpu.roll(d_key_value[0, :, 128:], 32, 1)
        )
        d_entry[2] = jnp.where(
            first_lanes, pltpu.roll(d_key_value[1, :, :128], 96, 1), d_key_value[1, :, 128:]
        )


def run_block(
    info,
    offset,
    tokens,
    cotangent,
    entry,
    mixing_t,
    expand,
    shrink_t,
    reduce_w,
    norms,
    value_filter,
    hidden_filter,
):
    steps = info.shape[1]
    ff = expand.shape[1]
    consts = [
        jnp.asarray(order_matrix(), BF),
        jnp.asarray(order_matrix().T, BF),
        jnp.asarray(cell_shifts(), BF),
        jnp.asarray(score_bias(), F32),
        jnp.asarray(shift_masks(), F32),
    ]
    whole = [entry, mixing_t, expand, shrink_t, reduce_w, norms, value_filter, hidden_filter] + consts

    def all_of(a):
        return pl.BlockSpec(a.shape, lambda i, *_: (0,) * a.ndim)

    grid_in = pl.BlockSpec((1, 32, 32, 128), lambda i, info, off: (off[0] + i, 0, 0, 0))
    grid_out = pl.BlockSpec((1, 32, 32, 128), lambda i, *_: (i, 0, 0, 0))
    sums = [(3, 128, 128), (128, 128), (128, ff), (128, ff), (2560, 128), (8, 128), (9, 128), (9, ff)]
    out_shape = [
        jax.ShapeDtypeStruct((steps, 32, 32, 128), BF),
        jax.ShapeDtypeStruct((steps, 32, 32, 128), BF),
    ] + [jax.ShapeDtypeStruct(s, F32) for s in sums]

    def kernel(info, off, *refs):
        block_kernel(info, *refs, steps=steps)

    return pl.pallas_call(
        kernel,
        out_shape=out_shape,
        grid_spec=pltpu.PrefetchScalarGridSpec(
            num_scalar_prefetch=2,
            grid=(steps,),
            in_specs=[grid_in, grid_in] + [all_of(a) for a in whole],
            out_specs=[grid_out, grid_out]
            + [pl.BlockSpec(s, lambda i, *_, n=len(s): (0,) * n) for s in sums],
            scratch_shapes=[
                pltpu.VMEM((1152, ff), BF),
                pltpu.VMEM((2, 128, 256), BF),
                pltpu.VMEM((1024, 1152), BF),
                pltpu.VMEM((1152, 1024), BF),
                pltpu.VMEM((1024, ff), BF),
                pltpu.VMEM((1152, ff), F32),
                pltpu.VMEM((1024, 1152), F32),
                pltpu.VMEM((2, 128, 256), F32),
                pltpu.VMEM((4, 160, 256), F32),
                pltpu.VMEM((1024, 128), BF),
                pltpu.VMEM((1024, 128), BF),
            ],
        ),
        compiler_params=pltpu.CompilerParams(
            dimension_semantics=("arbitrary",), vmem_limit_bytes=60 * 1024 * 1024
        ),
        name="block",
    )(info, offset, tokens, cotangent, *whole)


def advance(weight, moment, average, gradient, step_rate, weight_decay):
    gradient = gradient + weight_decay * weight
    moment = 0.9 * moment + gradient
    weight = weight - step_rate * (gradient + 0.9 * moment)
    return (moment, weight, 0.8 * average + 0.2 * weight)


def per_device(
    tokens,
    cotangent,
    resolution,
    live_images,
    entry_weight,
    entry_momentum,
    entry_average,
    mixing_weight,
    mixing_momentum,
    mixing_average,
    expand_weight,
    expand_momentum,
    expand_average,
    shrink_weight,
    shrink_momentum,
    shrink_average,
    reduce_weight,
    reduce_momentum,
    reduce_average,
    norm_params,
    norm_momentum,
    norm_average,
    value_filter,
    value_momentum,
    value_average,
    hidden_filter,
    hidden_momentum,
    hidden_average,
):
    devices = lax.axis_size("dp")
    head = lax.axis_index("head")
    swap = [(0, 1), (1, 0)]
    grids = tokens.shape[0]
    half = grids // 2
    ff = 2 * expand_weight.shape[1]

    def pair(own, axis):
        other = lax.ppermute(own, "head", swap)
        return jnp.where(
            head == 0, jnp.concatenate([own, other], axis), jnp.concatenate([other, own], axis)
        )

    shards = (entry_weight, mixing_weight.T, expand_weight, shrink_weight.T, reduce_weight)
    shapes = [s.shape for s in shards]
    sizes = [s.size for s in shards]
    starts = [sum(sizes[:n]) for n in range(6)]
    packed = jnp.concatenate([s.astype(BF).reshape(-1) for s in shards]).reshape(-1, 128)
    gathered = lax.all_gather(packed, ("dp", "head")).reshape(devices, 2, -1)
    parts = [
        gathered[:, :, starts[n] : starts[n + 1]].reshape((devices, 2) + shapes[n]) for n in range(5)
    ]
    entry = parts[0].transpose(2, 0, 3, 1, 4).reshape(3, 128, 128)
    mixing_t, expand, shrink_t, reduce_w = [
        p.transpose(0, 2, 1, 3).reshape(devices * p.shape[2], -1) for p in parts[1:]
    ]
    values_here = value_filter.transpose(1, 0, 2).reshape(9, 64)
    filters = pair(jnp.concatenate([values_here, hidden_filter], 1)[None], 0)
    values_full = filters[:, :, :64].transpose(1, 0, 2).reshape(9, 128)
    hidden_full = filters[:, :, 64:].transpose(1, 0, 2).reshape(9, ff)

    fine = (resolution == 8).astype(jnp.int32)
    info = lax.dynamic_slice_in_dim(jnp.stack([fine, live_images]), head * half, half, 1)
    offset = (head * half).reshape(1).astype(jnp.int32)
    (
        out_half,
        input_half,
        d_entry,
        d_mixing_t,
        d_expand,
        d_shrink_t,
        d_reduce,
        d_norm,
        d_value,
        d_hidden,
    ) = run_block(
        info,
        offset,
        tokens,
        cotangent,
        entry,
        mixing_t,
        expand,
        shrink_t,
        reduce_w,
        norm_params,
        values_full,
        hidden_full,
    )
    live_here = jnp.sum(info[1] * jnp.where(info[0] == 1, 64, 256)).astype(F32)

    small = jnp.concatenate(
        [d_norm.reshape(-1), d_value.reshape(-1), d_hidden.reshape(-1), live_here.reshape(1)]
    )
    small = lax.psum(small, ("dp", "head"))
    norm_grad = small[:1024].reshape(2, 4, 128)
    value_grad = small[1024 : 1024 + 1152].reshape(9, 2, 2, 32)
    value_grad = lax.dynamic_index_in_dim(value_grad, head, 1, False).transpose(1, 0, 2)
    hidden_grad = small[2176 : 2176 + 9 * ff].reshape(9, 2, ff // 2)
    hidden_grad = lax.dynamic_index_in_dim(hidden_grad, head, 1, False)
    live_total = small[-1]

    d_entry = d_entry.reshape(3, devices, -1, 2, 64).transpose(3, 1, 0, 2, 4)
    d_rest = [
        d.reshape(devices, -1, 2, d.shape[1] // 2).transpose(2, 0, 1, 3)
        for d in (d_mixing_t, d_expand, d_shrink_t, d_reduce)
    ]
    grads = jnp.concatenate([d.reshape(2, devices, -1) for d in [d_entry] + d_rest], 2)
    mine = lax.dynamic_index_in_dim(grads, head, 0, False)
    theirs = lax.dynamic_index_in_dim(grads, 1 - head, 0, False)
    mine = mine + lax.ppermute(theirs, "head", swap)
    mine = lax.psum_scatter(mine.reshape(devices, -1, 128), "dp", scatter_dimension=0)
    mine = mine.reshape(-1)
    entry_grad, mixing_grad, expand_grad, shrink_grad, reduce_grad = [
        mine[starts[n] : starts[n + 1]].reshape(shapes[n]) for n in range(5)
    ]
    mixing_grad, shrink_grad = mixing_grad.T, shrink_grad.T

    output = pair(out_half, 0)
    input_raw = pair(input_half, 0)
    tokens_all = devices * grids * tokens.shape[1] * tokens.shape[2]
    factor = tokens_all / live_total
    rate_unit = tokens_all ** (-0.5)
    input_grad = factor * input_raw.astype(F32)
    results = []
    for weight, moment, average, grad, rate, decay in (
        (entry_weight, entry_momentum, entry_average, entry_grad, 0.3, 0.05),
        (mixing_weight, mixing_momentum, mixing_average, mixing_grad, 0.12, 0.05),
        (expand_weight, expand_momentum, expand_average, expand_grad, 0.12, 0.05),
        (shrink_weight, shrink_momentum, shrink_average, shrink_grad, 0.03, 0.05),
        (reduce_weight, reduce_momentum, reduce_average, reduce_grad, 0.1, 0.05),
        (norm_params, norm_momentum, norm_average, norm_grad, 0.2, 0.0),
        (value_filter, value_momentum, value_average, value_grad, 0.4, 0.05),
        (hidden_filter, hidden_momentum, hidden_average, hidden_grad, 0.5, 0.05),
    ):
        results.extend(advance(weight, moment, average, factor * grad, rate * rate_unit, decay))
    return (output, input_grad, *results)


def solution(mesh):
    in_specs = (
        P("dp", None, None, None),
        P("dp", None, None, None),
        P("dp"),
        P("dp"),
        P(None, "dp", "head"),
        P(None, "dp", "head"),
        P(None, "dp", "head"),
        P("head", "dp"),
        P("head", "dp"),
        P("head", "dp"),
        P("dp", "head"),
        P("dp", "head"),
        P("dp", "head"),
        P("head", "dp"),
        P("head", "dp"),
        P("head", "dp"),
        P("dp", "head"),
        P("dp", "head"),
        P("dp", "head"),
        P(),
        P(),
        P(),
        P(None, None, "head"),
        P(None, None, "head"),
        P(None, None, "head"),
        P(None, "head"),
        P(None, "head"),
        P(None, "head"),
    )
    out_specs = (
        P("dp", None, None, None),
        P("dp", None, None, None),
        P(None, "dp", "head"),
        P(None, "dp", "head"),
        P(None, "dp", "head"),
        P("head", "dp"),
        P("head", "dp"),
        P("head", "dp"),
        P("dp", "head"),
        P("dp", "head"),
        P("dp", "head"),
        P("head", "dp"),
        P("head", "dp"),
        P("head", "dp"),
        P("dp", "head"),
        P("dp", "head"),
        P("dp", "head"),
        P(),
        P(),
        P(),
        P(None, None, "head"),
        P(None, None, "head"),
        P(None, None, "head"),
        P(None, "head"),
        P(None, "head"),
        P(None, "head"),
    )
    return jax.shard_map(
        per_device, mesh=mesh, in_specs=in_specs, out_specs=out_specs, check_vma=False
    )
```

```python
import math

import jax
import jax.numpy as jnp
import numpy as np
from jax import lax
from jax.experimental import pallas as pl
from jax.experimental.pallas import tpu as pltpu
from jax.sharding import PartitionSpec as P

BF = jnp.bfloat16
F32 = jnp.float32
EPSILON = 1e-06
HALF = 16
MASKED = -1e9
NN = (((1,), (0,)), ((), ()))
NT = (((1,), (1,)), ((), ()))
TN = (((0,), (0,)), ((), ()))
MESH = pl.DeviceIdType.MESH
SMALL = 64
LIMIT = 60 * 1024 * 1024


def mm(a, b, dims=NN):
    return lax.dot_general(a, b, dims, preferred_element_type=F32)


def block_of(a4, b4):
    return (a4 % 2) * 8 + (b4 % 2) * 4 + (a4 // 2) * 2 + b4 // 2


def place_of(block):
    return ((block >> 1) & 1) * 2 + (block >> 3), (block & 1) * 2 + ((block >> 2) & 1)


def order_matrix():
    perm = np.zeros((256, 256), np.float32)
    for block in range(16):
        a4, b4 = place_of(block)
        for ci in range(4):
            for ck in range(4):
                perm[block * 16 + ci * 4 + ck, (4 * ci + a4) * HALF + 4 * ck + b4] = 1
    return perm


def cell_shifts():
    places = []
    for ci in range(4):
        for ck in range(4):
            places.append((0, ci, ck, ci // 2, ck // 2))
    for ah in range(2):
        for bh in range(2):
            for ci in range(4):
                for ck in range(4):
                    places.append((1, 2 * ci + ah, 2 * ck + bh, ci // 2, ck // 2))
    index = {p[:3]: n for n, p in enumerate(places)}
    shifts = np.zeros((2, 9, 80, 80), np.float32)
    for n, (g, i, k, si, sk) in enumerate(places):
        for tap in range(9):
            other = index.get((g, i + tap // 3 - 1, k + tap % 3 - 1))
            if other is not None:
                shifts[0, tap, n, other] = 1
                if places[other][3:] == (si, sk):
                    shifts[1, tap, n, other] = 1
    return shifts.reshape(2, 720, 80)


def score_bias():
    rows = np.array([(n % 16) for _ in range(2) for n in list(range(16)) + list(range(64))])
    cols = np.arange(256) % 16

    def image(n):
        return (n // 8) * 2 + (n % 4) // 2

    return np.where(image(rows)[:, None] == image(cols)[None, :], 0.0, MASKED).astype(np.float32)


def shift_masks():
    masks = np.zeros((2, 4, 16, 128), np.float32)
    for fine in range(2):
        for ci in range(4):
            for ck in range(4):
                row = ci * 4 + ck
                for n, (d, e) in enumerate(((1, 0), (-1, 0), (0, 1), (0, -1))):
                    ni, nk = ci + d, ck + e
                    ok = 0 <= ni < 4 and 0 <= nk < 4
                    if fine:
                        ok = ok and ni // 2 == ci // 2 and nk // 2 == ck // 2
                    masks[fine, n, row] = ok
    return masks


def normalise(x):
    centred = x - jnp.mean(x, -1, keepdims=True)
    scale = lax.rsqrt(jnp.mean(centred * centred, -1, keepdims=True) + EPSILON)
    return centred * scale, scale


def normalise_back(grad, unit, scale):
    return scale * (
        grad
        - jnp.mean(grad, -1, keepdims=True)
        - unit * jnp.mean(grad * unit, -1, keepdims=True)
    )


def gelu_pair(h):
    density = jnp.exp(-0.5 * (h * h))
    t = 1.0 / (1.0 + (0.3275911 * math.sqrt(0.5)) * jnp.abs(h))
    poly = 1.061405429 * 0.5
    for c in (-1.453152027, 1.421413741, -0.284496736, 0.254829592):
        poly = poly * t + c * 0.5
    tail = poly * t * density
    below = jnp.where(h >= 0, 1.0 - tail, tail)
    return h * below, below + h * density * (1.0 / math.sqrt(2 * math.pi))


def block_kernel(
    resolution,
    live_images,
    head,
    tokens,
    cotangent,
    packed,
    filters,
    norms,
    perm,
    perm_t,
    shifts,
    bias,
    edge,
    out,
    input_grad,
    mine,
    theirs,
    small_mine,
    small_theirs,
    entry,
    mixing_t,
    expand,
    shrink_t,
    reduce_w,
    value_filter,
    hidden_filter,
    wide_s,
    square_s,
    d_entry,
    d_mixing_t,
    d_shrink_t,
    d_reduce,
    d_norm,
    d_value,
    conv_w,
    key_value_w,
    im2col,
    im2col_t,
    g_low,
    m_sum,
    folds,
    d_key_value,
    probs,
    normed_s,
    queries_s,
    reduce_low,
    *,
    steps,
):
    step = pl.program_id(0)
    devices = packed.shape[0] // 2
    width = 128 // devices
    ff = expand.shape[1]
    lane = lax.broadcasted_iota(jnp.int32, (128, 128), 1)
    first_lanes = lane % 64 < 32

    def left(rows):
        return lax.broadcasted_iota(jnp.int32, (rows, 128), 1) < 64

    @pl.when(step == 0)
    def prepare():
        top, chunk = 12 * width, ff // 256
        for d in range(devices):
            one, two = [packed[2 * d + h].astype(F32) for h in range(2)]
            mask = left(top)
            reduce_w[20 * width * d : 20 * width * d + top, :] = jnp.where(
                mask, one[:top], pltpu.roll(two[:top], 64, 1)
            )
            rest = jnp.where(mask, pltpu.roll(one[:top], 64, 1), two[:top])
            reduce_w[20 * width * d + top : 20 * width * (d + 1), :] = rest[: 8 * width]
            rows = slice(width * d, width * d + width)
            for e in range(4):
                square_s[e, rows, :] = rest[(8 + e) * width : (9 + e) * width]
            for h, part in enumerate((one, two)):
                for u in range(chunk):
                    cols = slice((h * chunk + u) * 128, (h * chunk + u + 1) * 128)
                    wide_s[0, rows, cols] = part[top + u * width : top + (u + 1) * width]
                    wide_s[1, rows, cols] = part[
                        top + (chunk + u) * width : top + (chunk + u + 1) * width
                    ]
        reduce_low[...] = reduce_w[...].astype(BF)
        entry[...] = square_s[:3].astype(BF)
        mixing_t[...] = square_s[3].astype(BF)
        expand[...] = wide_s[0]
        shrink_t[...] = wide_s[1].astype(BF)
        for h in range(2):
            hidden_filter[:, h * (ff // 2) : (h + 1) * (ff // 2)] = filters[h, :9, : ff // 2]
        value_filter[...] = jnp.where(
            left(9),
            filters[0, :9, ff // 2 :],
            pltpu.roll(filters[1, :9, ff // 2 :], 64, 1),
        )
        for tap in range(9):
            gain = hidden_filter[tap : tap + 1, :]
            if tap == 4:
                gain = gain + 1.0
            conv_w[tap * 128 : (tap + 1) * 128, :] = (expand[...] * gain).astype(BF)
        for g in range(2):
            w = entry[1 + g].astype(F32)
            if g == 0:
                keys, vals = w, pltpu.roll(w, 96, 1)
                keep = first_lanes
            else:
                keys, vals = pltpu.roll(w, 32, 1), w
                keep = jnp.logical_not(first_lanes)
            key_value_w[g, :, :128] = jnp.where(keep, keys, 0.0).astype(BF)
            key_value_w[g, :, 128:] = jnp.where(keep, vals, 0.0).astype(BF)
        for ref in (d_entry, d_mixing_t, d_shrink_t, d_reduce, d_norm, d_value, m_sum, d_key_value):
            ref[...] = jnp.zeros_like(ref)

    grid = head[0] * steps + step
    fine = (resolution[grid] == 8).astype(jnp.int32)
    alive = live_images[grid]
    fine_f = fine.astype(F32)

    def ordered(ref):
        parts = [
            ref[0, a * 16 : a * 16 + 16, b * 16 : b * 16 + 16, :].reshape(256, 128)
            for a in range(2)
            for b in range(2)
        ]
        rows = mm(perm[...], jnp.concatenate(parts, 1))
        return jnp.stack(
            [rows[:, q * 128 : q * 128 + 128].reshape(16, 16, 128) for q in range(4)], 1
        ).reshape(1024, 128)

    def restore(value, ref):
        blocks = value.reshape(16, 4, 16, 128)
        rows = mm(
            perm_t[...],
            jnp.concatenate([blocks[:, q].reshape(256, 128) for q in range(4)], 1),
        ).astype(BF)
        for q in range(4):
            a, b = q // 2, q % 2
            ref[0, a * 16 : a * 16 + 16, b * 16 : b * 16 + 16, :] = rows[
                :, q * 128 : q * 128 + 128
            ].reshape(16, 16, 128)

    def of_quadrant(value, q, blocks):
        return value.reshape(blocks, 4, 16, 128)[:, q].reshape(blocks * 16, 128)

    def of_quadrants(parts, blocks):
        return jnp.stack([p.reshape(blocks, 16, 128) for p in parts], 1).reshape(
            blocks * 64, 128
        )

    def gain(n):
        return norms[0, n : n + 1, :]

    def shift_by(n):
        return norms[1, n : n + 1, :]

    def add_norm(n, grad, unit):
        d_norm[n : n + 1, :] += jnp.sum(grad * unit, 0, keepdims=True)
        d_norm[4 + n : 5 + n, :] += jnp.sum(grad, 0, keepdims=True)

    x = ordered(tokens)
    unit1, scale1 = normalise(x)
    normed = (unit1 * gain(0) + shift_by(0)).astype(BF)
    normed_s[...] = normed
    queries_s[...] = mm(normed, entry[0]).astype(BF)
    patches = (
        jnp.concatenate(
            [
                normed_s[block_of(t // 4, t % 4) * 64 : block_of(t // 4, t % 4) * 64 + 64, :]
                for t in range(16)
            ],
            1,
        ),
        jnp.concatenate([normed_s[t * 256 : t * 256 + 256, :] for t in range(4)], 1),
    )
    rows_of = (slice(0, 2048), slice(2048, 2560))
    cell_saved = []
    keys, values = [], []
    for g in range(2):
        reduced = mm(patches[g], reduce_low[rows_of[g], :])
        unit, scale = normalise(reduced)
        act, slope = gelu_pair(unit * gain(1 + g) + shift_by(1 + g))
        cell_low = act.astype(BF)
        pair = mm(cell_low, key_value_w[g])
        keys.append(pair[:, :128].astype(BF))
        values.append(pair[:, 128:])
        cell_saved.append((unit, scale, slope, cell_low))
    keys_all = [
        jnp.concatenate([keys[0][q * 16 : q * 16 + 16], of_quadrant(keys[1], q, 4)], 0)
        for q in range(4)
    ]
    values_all = jnp.concatenate(
        [
            jnp.concatenate([values[0][q * 16 : q * 16 + 16], of_quadrant(values[1], q, 4)], 0)
            for q in range(4)
        ],
        1,
    )
    moves = shifts[pl.ds(fine, 1)][0]
    high = values_all.astype(BF)
    rest = (values_all - high.astype(F32)).astype(BF)
    moved = mm(moves, high) + mm(moves, rest)
    taps4 = jnp.concatenate([value_filter[...]] * 4, 1)
    enhanced = values_all
    for tap in range(9):
        enhanced = enhanced + moved[tap * 80 : tap * 80 + 80] * taps4[tap : tap + 1]
    enhanced = enhanced.astype(BF)
    lane80 = lax.broadcasted_iota(jnp.int32, (80, 128), 1)
    zero80 = jnp.zeros((80, 128), BF)

    def both_heads(rows):
        return jnp.concatenate(
            [jnp.where(lane80 < 64, rows, zero80), jnp.where(lane80 < 64, zero80, rows)], 0
        )

    segments = ((0, 16), (16, 80), (80, 96), (96, 160))
    queries = queries_s[...]
    query_q = [of_quadrant(queries, q, 16) for q in range(4)]
    keys_q = [both_heads(keys_all[q]) for q in range(4)]
    enhanced_q = [both_heads(enhanced[:, q * 128 : q * 128 + 128]) for q in range(4)]
    mixed_parts = []
    scaling = 32**-0.5
    for q in range(4):
        scores = mm(keys_q[q], query_q[q], NT) * scaling + fine_f * bias[...]
        weights = []
        for lo, hi in segments:
            part = scores[lo:hi]
            part = jnp.exp(part - jnp.max(part, 0, keepdims=True))
            weights.append(part / jnp.sum(part, 0, keepdims=True))
        weights = jnp.concatenate(weights, 0)
        probs[q] = weights
        mixed_parts.append(mm(weights.astype(BF), enhanced_q[q], TN))
    mixed = of_quadrants(mixed_parts, 16).astype(BF)
    middle = x + mm(mixed, mixing_t[...], NT)
    unit2, scale2 = normalise(middle)
    second = unit2 * gain(3) + shift_by(3)
    second_low = second.astype(BF)
    second_f = second_low.astype(F32)

    def move(value, rows, columns):
        size = value.shape[0]
        if rows:
            n = 0 if rows > 0 else 1
            value = pltpu.roll(value, (-4 * rows) % size, 0)
            value = (
                value.reshape(size // 16, 16, 128) * edge[pl.ds(fine, 1), n : n + 1][0]
            ).reshape(size, 128)
        if columns:
            n = 2 if columns > 0 else 3
            value = pltpu.roll(value, (-columns) % size, 0)
            value = (
                value.reshape(size // 16, 16, 128) * edge[pl.ds(fine, 1), n : n + 1][0]
            ).reshape(size, 128)
        return value

    def wrap(a4, d):
        return (a4 + d) % 4, (a4 + d) // 4

    moved_blocks = {}
    for block in range(16):
        a4, b4 = place_of(block)
        for tap in range(9):
            na, wa = wrap(a4, tap // 3 - 1)
            nb, wb = wrap(b4, tap % 3 - 1)
            source = block_of(na, nb)
            key = (source, wa, wb)
            if key not in moved_blocks:
                rows = slice(source * 64, source * 64 + 64)
                if wa or wb:
                    moved_blocks[key] = move(second_f[rows], wa, wb).astype(BF)
                else:
                    moved_blocks[key] = second_low[rows]
            im2col[block * 64 : block * 64 + 64, tap * 128 : tap * 128 + 128] = moved_blocks[key]
    for tap in range(9):
        im2col_t[tap * 128 : tap * 128 + 128, :] = im2col[:, tap * 128 : tap * 128 + 128].T

    row16 = lax.broadcasted_iota(jnp.int32, (16, 128), 0)
    within = (row16 // 8) * 4 + (row16 % 4) // 2
    live = jnp.stack(
        [
            jnp.where(
                jnp.where(fine == 1, within + (q // 2) * 8 + (q % 2) * 2, q) < alive, 1.0, 0.0
            )
            for q in range(4)
        ],
        0,
    )
    upstream = (ordered(cotangent).reshape(16, 4, 16, 128) * live[None]).reshape(1024, 128)
    up_low = upstream.astype(BF)
    up_t = up_low.T

    feed = jnp.zeros((1024, 128), F32)
    wide = 256
    for c in range(0, ff, wide):
        cols = slice(c, c + wide)
        hidden = mm(im2col[...], conv_w[:, cols])
        act, slope = gelu_pair(hidden)
        act = act.astype(BF)
        grad = mm(up_low, shrink_t[:, cols]) * slope
        grad = grad.astype(BF)
        g_low[:, cols] = grad
        feed = feed + mm(act, shrink_t[:, cols], NT)
        d_shrink_t[:, cols] += mm(up_t, act)
        m_sum[:, cols] += mm(im2col_t[...], grad)
    restore((middle + feed).astype(BF), out)

    for t in range(0, 9, 2):
        rows = slice(t * 128, min(t + 2, 9) * 128)
        folds[:, rows] = mm(g_low[...], conv_w[rows, :], NT)
    sums = {}
    for block in range(16):
        a4, b4 = place_of(block)
        for tap in range(9):
            na, wa = wrap(a4, tap // 3 - 1)
            nb, wb = wrap(b4, tap % 3 - 1)
            key = (block_of(na, nb), wa, wb)
            sums.setdefault(key, []).append((block, tap))
    second_parts = []
    for block in range(16):
        total = None
        for (source, wa, wb), terms in sums.items():
            if source != block:
                continue
            part = None
            for other, tap in terms:
                term = folds[other * 64 : other * 64 + 64, tap * 128 : tap * 128 + 128]
                part = term if part is None else part + term
            if wa or wb:
                part = move(part, -wa, -wb)
            total = part if total is None else total + part
        second_parts.append(total)
    second_grad = jnp.concatenate(second_parts, 0)
    add_norm(3, second_grad, unit2)
    middle_grad = upstream + normalise_back(second_grad * gain(3), unit2, scale2)
    middle_low = middle_grad.astype(BF)
    d_mixing_t[...] += mm(middle_low, mixed, TN)
    mixed_grad = mm(middle_low, mixing_t[...]).astype(BF)

    query_parts, key_parts, enhanced_parts = [], [], []
    for q in range(4):
        out_grad = of_quadrant(mixed_grad, q, 16)
        weights = probs[q]
        prob_grad = mm(enhanced_q[q], out_grad, NT)
        product = weights * prob_grad
        score_grad = []
        for lo, hi in segments:
            score_grad.append(
                product[lo:hi] - weights[lo:hi] * jnp.sum(product[lo:hi], 0, keepdims=True)
            )
        score_low = (scaling * jnp.concatenate(score_grad, 0)).astype(BF)
        query_parts.append(mm(score_low, keys_q[q], TN))
        key_full = mm(score_low, query_q[q])
        enhanced_full = mm(weights.astype(BF), out_grad)
        key_parts.append(jnp.where(lane80 < 64, key_full[:80], key_full[80:]).astype(BF))
        enhanced_parts.append(
            jnp.where(lane80 < 64, enhanced_full[:80], enhanced_full[80:]).astype(BF)
        )
    query_low = of_quadrants(query_parts, 16).astype(BF)
    enhanced_grad = jnp.concatenate(enhanced_parts, 1)
    moved = mm(moves, enhanced_grad)
    value_grad = enhanced_grad.astype(F32)
    for tap in range(9):
        part = moved[(8 - tap) * 80 : (8 - tap) * 80 + 80]
        value_grad = value_grad + part * taps4[tap : tap + 1]
        row = jnp.sum(part * values_all, 0, keepdims=True)
        d_value[tap : tap + 1, :] += (
            row[:, :128] + row[:, 128:256] + row[:, 256:384] + row[:, 384:]
        )
    value_grad = value_grad.astype(BF)
    value_parts = [value_grad[:, q * 128 : q * 128 + 128] for q in range(4)]
    normed = normed_s[...]
    normed_grad = mm(query_low, entry[0], NT)
    d_entry[0] += mm(normed, query_low, TN)
    for g in range(2):
        if g == 0:
            sides = [jnp.concatenate([p[:16] for p in parts], 0) for parts in (key_parts, value_parts)]
        else:
            sides = [of_quadrants([p[16:] for p in parts], 4) for parts in (key_parts, value_parts)]
        pair = jnp.concatenate(sides, 1)
        unit, scale, slope, cell_low = cell_saved[g]
        d_key_value[g] += mm(cell_low, pair, TN)
        cell_grad = mm(pair, key_value_w[g], NT) * slope
        add_norm(1 + g, cell_grad, unit)
        reduced_low = normalise_back(cell_grad * gain(1 + g), unit, scale).astype(BF)
        d_reduce[rows_of[g], :] += mm(patches[g], reduced_low, TN)
        back = mm(reduced_low, reduce_low[rows_of[g], :], NT)
        if g == 0:
            order = [place_of(block) for block in range(16)]
            order = [a4 * 4 + b4 for a4, b4 in order]
        else:
            order = range(4)
        normed_grad = normed_grad + jnp.concatenate(
            [back[:, t * 128 : t * 128 + 128] for t in order], 0
        )
    add_norm(0, normed_grad, unit1)
    raw = middle_grad + normalise_back(normed_grad * gain(0), unit1, scale1)
    restore(raw.astype(BF), input_grad)

    @pl.when(step == steps - 1)
    def finish():
        weight = expand[...]
        total = None
        for tap in range(9):
            part = m_sum[tap * 128 : tap * 128 + 128, :]
            factor = hidden_filter[tap : tap + 1, :]
            if tap == 4:
                factor = factor + 1.0
            hidden_filter[tap : tap + 1, :] = jnp.sum(part * weight, 0, keepdims=True)
            total = part * factor if total is None else total + part * factor
        wide_s[0] = total
        wide_s[1] = d_shrink_t[...]
        d_entry[1] = jnp.where(
            first_lanes, d_key_value[0, :, :128], pltpu.roll(d_key_value[0, :, 128:], 32, 1)
        )
        d_entry[2] = jnp.where(
            first_lanes, pltpu.roll(d_key_value[1, :, :128], 96, 1), d_key_value[1, :, 128:]
        )
        is_second = head[0] == 1
        top, chunk = 12 * width, ff // 256
        planes, lines = mine.shape[0], mine.shape[1]

        def put(d, rows, first, second):
            place = (d % planes, d // planes, rows)
            mine[place] = jnp.where(is_second, second, first)
            theirs[place] = jnp.where(is_second, first, second).astype(BF)

        for d in range(devices):
            rows = slice(width * d, width * d + width)
            upper = d_reduce[20 * width * d : 20 * width * d + top, :]
            lower = jnp.concatenate(
                [d_reduce[20 * width * d + top : 20 * width * (d + 1), :]]
                + [d_entry[e, rows, :] for e in range(3)]
                + [d_mixing_t[rows, :]],
                0,
            )
            firsts = [jnp.where(left(top), upper, pltpu.roll(lower, 64, 1))]
            seconds = [jnp.where(left(top), pltpu.roll(upper, 64, 1), lower)]
            for n in range(2):
                for h, parts in enumerate((firsts, seconds)):
                    for u in range(chunk):
                        cols = slice((h * chunk + u) * 128, (h * chunk + u + 1) * 128)
                        parts.append(wide_s[n, rows, cols])
            pad = mine.shape[2] - 20 * width
            if pad:
                firsts.append(jnp.zeros((pad, 128), F32))
                seconds.append(jnp.zeros((pad, 128), F32))
            put(d, slice(None), jnp.concatenate(firsts, 0), jnp.concatenate(seconds, 0))
        count = jnp.int32(0)
        for n in range(steps):
            side = resolution[head[0] * steps + n]
            count = count + side * side * live_images[head[0] * steps + n]
        halves = [
            jnp.concatenate(
                [
                    hidden_filter[:, (h * chunk + u) * 128 : (h * chunk + u + 1) * 128]
                    for u in range(chunk)
                ],
                0,
            )
            for h in range(2)
        ]
        for ref, flip in ((small_mine, False), (small_theirs, True)):
            ref[...] = jnp.zeros_like(ref)
            ref[:8, :] = d_norm[...]
            ref[8:17, :] = d_value[...]
            ref[17:18, :] = jnp.full((1, 128), count, jnp.int32).astype(F32)
            second = jnp.logical_not(is_second) if flip else is_second
            ref[18 : 18 + 9 * chunk, :] = jnp.where(second, halves[1], halves[0])


def run_block(resolution, live_images, head, tokens, cotangent, packed, filters, norms):
    steps = tokens.shape[0] // 2
    devices, rows = packed.shape[0] // 2, packed.shape[1]
    ff = 2 * (filters.shape[2] - 128)
    lines = line_of(devices)
    consts = [
        jnp.asarray(order_matrix(), BF),
        jnp.asarray(order_matrix().T, BF),
        jnp.asarray(cell_shifts(), BF),
        jnp.asarray(score_bias(), F32),
        jnp.asarray(shift_masks(), F32),
    ]
    whole = [packed, filters, norms] + consts

    def all_of(a):
        return pl.BlockSpec(a.shape, lambda i, *_, n=a.ndim: (0,) * n)

    grid_in = pl.BlockSpec((1, 32, 32, 128), lambda i, res, live, head: (head[0] * steps + i, 0, 0, 0))
    grid_out = pl.BlockSpec((1, 32, 32, 128), lambda i, *_: (i, 0, 0, 0))
    out_shape = [
        jax.ShapeDtypeStruct((steps, 32, 32, 128), BF),
        jax.ShapeDtypeStruct((steps, 32, 32, 128), BF),
        jax.ShapeDtypeStruct((devices // lines, lines, rows, 128), F32),
        jax.ShapeDtypeStruct((devices // lines, lines, rows, 128), BF),
        jax.ShapeDtypeStruct((SMALL, 128), F32),
        jax.ShapeDtypeStruct((SMALL, 128), F32),
    ]

    def kernel(*refs):
        block_kernel(*refs, steps=steps)

    return pl.pallas_call(
        kernel,
        out_shape=out_shape,
        grid_spec=pltpu.PrefetchScalarGridSpec(
            num_scalar_prefetch=3,
            grid=(steps,),
            in_specs=[grid_in, grid_in] + [all_of(a) for a in whole],
            out_specs=[grid_out, grid_out] + [all_of(a) for a in out_shape[2:]],
            scratch_shapes=[
                pltpu.VMEM((3, 128, 128), BF),
                pltpu.VMEM((128, 128), BF),
                pltpu.VMEM((128, ff), F32),
                pltpu.VMEM((128, ff), BF),
                pltpu.VMEM((2560, 128), F32),
                pltpu.VMEM((9, 128), F32),
                pltpu.VMEM((9, ff), F32),
                pltpu.VMEM((2, 128, ff), F32),
                pltpu.VMEM((4, 128, 128), F32),
                pltpu.VMEM((3, 128, 128), F32),
                pltpu.VMEM((128, 128), F32),
                pltpu.VMEM((128, ff), F32),
                pltpu.VMEM((2560, 128), F32),
                pltpu.VMEM((8, 128), F32),
                pltpu.VMEM((9, 128), F32),
                pltpu.VMEM((1152, ff), BF),
                pltpu.VMEM((2, 128, 256), BF),
                pltpu.VMEM((1024, 1152), BF),
                pltpu.VMEM((1152, 1024), BF),
                pltpu.VMEM((1024, ff), BF),
                pltpu.VMEM((1152, ff), F32),
                pltpu.VMEM((1024, 1152), F32),
                pltpu.VMEM((2, 128, 256), F32),
                pltpu.VMEM((4, 160, 256), F32),
                pltpu.VMEM((1024, 128), BF),
                pltpu.VMEM((1024, 128), BF),
                pltpu.VMEM((2560, 128), BF),
            ],
        ),
        compiler_params=pltpu.CompilerParams(
            dimension_semantics=("arbitrary",), vmem_limit_bytes=LIMIT
        ),
        name="block",
    )(resolution, live_images, head, tokens, cotangent, *whole)


def line_of(devices):
    return 4 if devices % 4 == 0 else 1


def rows_of_block(devices):
    return -(-20 * (128 // devices) // 16) * 16


def pack_kernel(entry, mixing, expand, shrink, reduce_w, values, hidden, block, filters, held):
    width, ff = expand.shape
    top, chunk = 12 * width, ff // 128
    held[...] = jnp.zeros_like(held)
    held[:top, :64] = reduce_w[:top, :]
    held[: 8 * width, 64:] = reduce_w[top:, :]
    for e in range(3):
        held[(8 + e) * width : (9 + e) * width, 64:] = entry[e]
    held[11 * width : top, 64:] = mixing[...].T
    turned = shrink[...].T
    for u in range(chunk):
        cols = slice(u * 128, (u + 1) * 128)
        held[top + u * width : top + (u + 1) * width, :] = expand[:, cols]
        held[top + (chunk + u) * width : top + (chunk + u + 1) * width, :] = turned[:, cols]
    block[...] = held[...].astype(BF)
    filters[...] = jnp.zeros_like(filters)
    filters[:9, :ff] = hidden[...]
    for g in range(2):
        filters[:9, ff + 32 * g : ff + 32 * g + 32] = values[g]


def run_pack(devices, entry, mixing, expand, shrink, reduce_w, values, hidden):
    rows = rows_of_block(devices)
    return pl.pallas_call(
        pack_kernel,
        out_shape=[
            jax.ShapeDtypeStruct((rows, 128), BF),
            jax.ShapeDtypeStruct((16, hidden.shape[1] + 128), F32),
        ],
        scratch_shapes=[pltpu.VMEM((rows, 128), F32)],
        compiler_params=pltpu.CompilerParams(vmem_limit_bytes=LIMIT),
        name="pack",
    )(entry, mixing, expand, shrink, reduce_w, values, hidden)


def greet(peers):
    barrier = pltpu.get_barrier_semaphore()
    for peer in peers:
        pl.semaphore_signal(barrier, inc=1, device_id=peer, device_id_type=MESH)
    pl.semaphore_wait(barrier, len(peers))


def places(devices):
    lines = line_of(devices)
    planes = devices // lines
    me, head = lax.axis_index("dp"), lax.axis_index("head")
    z, p = me // planes, me % planes
    line_peers = [((z + k) % lines) for k in range(1, lines)]
    plane_peers = [((p + k) % planes) for k in range(1, planes)]
    return lines, planes, z, p, head, line_peers, plane_peers


def gather_kernel(devices, block, filters, blocks, both, send_sem, recv_sem, filter_sem, local_sem):
    lines, planes, z, p, head, line_peers, plane_peers = places(devices)

    def slot(line, plane, core):
        return (line * planes + plane) * 2 + core

    def at(line, plane, core):
        return (line * planes + plane, core)

    sibling = at(z, p, 1 - head)
    greet(
        [at(k, p, head) for k in line_peers] + [at(z, k, head) for k in plane_peers] + [sibling]
    )
    sends = []

    def send(source, index, target):
        copy = pltpu.make_async_remote_copy(
            src_ref=source,
            dst_ref=blocks.at[index],
            send_sem=send_sem.at[len(sends)],
            recv_sem=recv_sem.at[index],
            device_id=target,
            device_id_type=MESH,
        )
        copy.start()
        sends.append(copy)

    def arrived(index):
        pltpu.make_async_remote_copy(
            src_ref=block,
            dst_ref=blocks.at[index],
            send_sem=send_sem.at[0],
            recv_sem=recv_sem.at[index],
            device_id=sibling,
            device_id_type=MESH,
        ).wait_recv()

    own = slot(z, p, head)
    for k in line_peers:
        send(block, own, at(k, p, head))
    for k in plane_peers:
        send(block, own, at(z, k, head))
    send(block, own, sibling)
    swap = pltpu.make_async_remote_copy(
        src_ref=filters,
        dst_ref=both.at[head],
        send_sem=filter_sem.at[0],
        recv_sem=filter_sem.at[1],
        device_id=sibling,
        device_id_type=MESH,
    )
    swap.start()
    keep = [
        pltpu.make_async_copy(block, blocks.at[own], local_sem.at[0]),
        pltpu.make_async_copy(filters, both.at[head], local_sem.at[1]),
    ]
    for copy in keep:
        copy.start()
    for k in line_peers:
        index = slot(k, p, head)
        arrived(index)
        for j in plane_peers:
            send(blocks.at[index], index, at(z, j, head))
        send(blocks.at[index], index, sibling)
    for line in [z] + line_peers:
        for j in plane_peers:
            index = slot(line, j, head)
            arrived(index)
            send(blocks.at[index], index, sibling)
    for line in [z] + line_peers:
        for j in [p] + plane_peers:
            arrived(slot(line, j, 1 - head))
    for copy in sends:
        copy.wait_send()
    swap.wait_send()
    pltpu.make_async_remote_copy(
        src_ref=filters,
        dst_ref=both.at[1 - head],
        send_sem=filter_sem.at[0],
        recv_sem=filter_sem.at[1],
        device_id=sibling,
        device_id_type=MESH,
    ).wait_recv()
    for copy in keep:
        copy.wait()


def run_gather(devices, block, filters):
    lines = line_of(devices)
    planes = devices // lines
    copies = (lines - 1) + lines * (planes - 1) + lines * planes
    anywhere = pl.BlockSpec(memory_space=pl.ANY)

    def kernel(*refs):
        gather_kernel(devices, *refs)

    return pl.pallas_call(
        kernel,
        out_shape=[
            jax.ShapeDtypeStruct((2 * devices,) + block.shape, BF),
            jax.ShapeDtypeStruct((2,) + filters.shape, F32),
        ],
        in_specs=[anywhere, anywhere],
        out_specs=[anywhere, anywhere],
        scratch_shapes=[
            pltpu.SemaphoreType.DMA((copies,)),
            pltpu.SemaphoreType.DMA((2 * devices,)),
            pltpu.SemaphoreType.DMA((2,)),
            pltpu.SemaphoreType.DMA((2,)),
        ],
        compiler_params=pltpu.CompilerParams(collective_id=0, has_side_effects=True),
        name="gather",
    )(block, filters)


def reduce_kernel(
    devices,
    mine,
    theirs,
    small_mine,
    small_theirs,
    out_half,
    input_half,
    grad,
    small,
    out_other,
    input_other,
    core_in,
    core_small,
    plane_out,
    plane_in,
    plane_small,
    line_sum,
    line_out,
    line_in,
    line_small,
    core_send,
    core_recv,
    plane_send,
    plane_recv,
    line_send,
    line_recv,
):
    lines, planes, z, p, head, line_peers, plane_peers = places(devices)

    def at(line, plane, core):
        return (line * planes + plane, core)

    sibling = at(z, p, 1 - head)
    greet(
        [at(k, p, head) for k in line_peers] + [at(z, k, head) for k in plane_peers] + [sibling]
    )

    def remote(source, target, send, recv, device):
        return pltpu.make_async_remote_copy(
            src_ref=source,
            dst_ref=target,
            send_sem=send,
            recv_sem=recv,
            device_id=device,
            device_id_type=MESH,
        )

    started = []

    def go(*args):
        copy = remote(*args)
        copy.start()
        started.append(copy)

    go(small_theirs, core_small, core_send.at[planes], core_recv.at[planes], sibling)
    for k in plane_peers + [p]:
        go(theirs.at[k], core_in.at[k], core_send.at[k], core_recv.at[k], sibling)
    remote(
        small_theirs, core_small, core_send.at[planes], core_recv.at[planes], sibling
    ).wait_recv()
    plane_small[pl.ds(p, 1)] = (small_mine[...] + core_small[...])[None]
    for n, k in enumerate(plane_peers):
        go(
            plane_small.at[p],
            plane_small.at[p],
            plane_send.at[planes + n],
            plane_recv.at[planes + p],
            at(z, k, head),
        )
    for n, k in enumerate(plane_peers):
        remote(
            theirs.at[k], core_in.at[k], core_send.at[k], core_recv.at[k], sibling
        ).wait_recv()
        plane_out[pl.ds(k, 1)] = (mine[pl.ds(k, 1)] + core_in[pl.ds(k, 1)].astype(F32)).astype(BF)
        go(plane_out.at[k], plane_in.at[p], plane_send.at[n], plane_recv.at[p], at(z, k, head))
    remote(theirs.at[p], core_in.at[p], core_send.at[p], core_recv.at[p], sibling).wait_recv()
    go(out_half, out_other, core_send.at[planes + 1], core_recv.at[planes + 1], sibling)
    go(input_half, input_other, core_send.at[planes + 2], core_recv.at[planes + 2], sibling)
    total = mine[pl.ds(p, 1)][0] + core_in[pl.ds(p, 1)][0].astype(F32)
    for k in plane_peers:
        remote(
            plane_out.at[k], plane_in.at[k], plane_send.at[0], plane_recv.at[k], sibling
        ).wait_recv()
        total = total + plane_in[pl.ds(k, 1)][0].astype(F32)
    line_sum[...] = total
    for n, k in enumerate(line_peers):
        line_out[pl.ds(k, 1)] = line_sum[pl.ds(k, 1)].astype(BF)
        go(line_out.at[k], line_in.at[z], line_send.at[n], line_recv.at[z], at(k, p, head))
    for k in plane_peers:
        remote(
            plane_small.at[p],
            plane_small.at[k],
            plane_send.at[0],
            plane_recv.at[planes + k],
            sibling,
        ).wait_recv()
    part = plane_small[0]
    for k in range(1, planes):
        part = part + plane_small[k]
    line_small[pl.ds(z, 1)] = part[None]
    for n, k in enumerate(line_peers):
        go(
            line_small.at[z],
            line_small.at[z],
            line_send.at[lines + n],
            line_recv.at[lines + z],
            at(k, p, head),
        )
    own = line_sum[pl.ds(z, 1)][0]
    for k in line_peers:
        remote(
            line_out.at[k], line_in.at[k], line_send.at[0], line_recv.at[k], sibling
        ).wait_recv()
        own = own + line_in[pl.ds(k, 1)][0].astype(F32)
    grad[...] = own
    for k in line_peers:
        remote(
            line_small.at[z],
            line_small.at[k],
            line_send.at[0],
            line_recv.at[lines + k],
            sibling,
        ).wait_recv()
    part = line_small[0]
    for k in range(1, lines):
        part = part + line_small[k]
    small[...] = part
    remote(
        out_half, out_other, core_send.at[planes + 1], core_recv.at[planes + 1], sibling
    ).wait_recv()
    remote(
        input_half, input_other, core_send.at[planes + 2], core_recv.at[planes + 2], sibling
    ).wait_recv()
    for copy in started:
        copy.wait_send()


def run_reduce(devices, mine, theirs, small_mine, small_theirs, out_half, input_half):
    planes, lines, rows = mine.shape[:3]
    anywhere = pl.BlockSpec(memory_space=pl.ANY)
    vmem = pl.BlockSpec(memory_space=pltpu.VMEM)
    sem = pltpu.SemaphoreType.DMA

    def kernel(*refs):
        reduce_kernel(devices, *refs)

    return pl.pallas_call(
        kernel,
        out_shape=[
            jax.ShapeDtypeStruct((rows, 128), F32),
            jax.ShapeDtypeStruct((SMALL, 128), F32),
            jax.ShapeDtypeStruct(out_half.shape, BF),
            jax.ShapeDtypeStruct(input_half.shape, BF),
        ],
        in_specs=[vmem] * 4 + [anywhere] * 2,
        out_specs=[vmem] * 2 + [anywhere] * 2,
        scratch_shapes=[
            pltpu.VMEM((planes, lines, rows, 128), BF),
            pltpu.VMEM((SMALL, 128), F32),
            pltpu.VMEM((planes, lines, rows, 128), BF),
            pltpu.VMEM((planes, lines, rows, 128), BF),
            pltpu.VMEM((planes, SMALL, 128), F32),
            pltpu.VMEM((lines, rows, 128), F32),
            pltpu.VMEM((lines, rows, 128), BF),
            pltpu.VMEM((lines, rows, 128), BF),
            pltpu.VMEM((lines, SMALL, 128), F32),
            sem((planes + 3,)),
            sem((planes + 3,)),
            sem((2 * planes,)),
            sem((2 * planes,)),
            sem((2 * lines,)),
            sem((2 * lines,)),
        ],
        compiler_params=pltpu.CompilerParams(
            collective_id=1, has_side_effects=True, vmem_limit_bytes=LIMIT
        ),
        name="reduce",
    )(mine, theirs, small_mine, small_theirs, out_half, input_half)


def advance(weight, moment, average, gradient, step_rate, weight_decay):
    gradient = gradient + weight_decay * weight
    moment = 0.9 * moment + gradient
    weight = weight - step_rate * (gradient + 0.9 * moment)
    return (moment, weight, 0.8 * average + 0.2 * weight)


RATES = (0.3, 0.12, 0.12, 0.03, 0.1, 0.2, 0.4, 0.5)


def update_kernel(head, *refs, tokens_all):
    out_own, out_other, in_own, in_other, grad, small = refs[:6]
    state = refs[6:30]
    output, input_grad = refs[30:32]
    results = refs[32:]
    step = pl.program_id(0)
    half = pl.num_programs(0) // 2
    factor = tokens_all / small[17:18, :]
    is_own = (step // half) == head[0]

    @pl.when(is_own)
    def own():
        output[...] = out_own[...]
        input_grad[...] = in_own[...].astype(F32) * factor

    @pl.when(jnp.logical_not(is_own))
    def other():
        output[...] = out_other[...]
        input_grad[...] = in_other[...].astype(F32) * factor

    @pl.when(step == 0)
    def update():
        width, ff = state[6].shape
        top, chunk = 12 * width, ff // 128
        rate_unit = tokens_all**-0.5

        def apply(n, place, raw, scale):
            new = advance(
                state[3 * n][place],
                state[3 * n + 1][place],
                state[3 * n + 2][place],
                scale * raw,
                RATES[n] * rate_unit,
                0.0 if n == 5 else 0.05,
            )
            for k in range(3):
                results[3 * n + k][place] = new[k]

        scale = factor[:, :64]
        for e in range(3):
            apply(0, e, grad[(8 + e) * width : (9 + e) * width, 64:], scale)
        apply(1, Ellipsis, grad[11 * width : top, 64:].T, factor[:, :width])
        for u in range(chunk):
            cols = slice(u * 128, (u + 1) * 128)
            apply(2, (slice(None), cols), grad[top + u * width : top + (u + 1) * width, :], factor)
            apply(
                3,
                (cols, slice(None)),
                grad[top + (chunk + u) * width : top + (chunk + u + 1) * width, :].T,
                factor[:, :width],
            )
        apply(4, (slice(0, top), slice(None)), grad[:top, :64], scale)
        apply(4, (slice(top, 20 * width), slice(None)), grad[: 8 * width, 64:], scale)
        for n in range(2):
            apply(5, n, small[4 * n : 4 * n + 4, :], factor)
        values = small[8:17, :]
        values = jnp.where(head[0] == 1, pltpu.roll(values, 64, 1), values)
        for g in range(2):
            apply(6, g, values[:, 32 * g : 32 * g + 32], factor[:, :32])
        for u in range(chunk):
            apply(
                7,
                (slice(None), slice(u * 128, (u + 1) * 128)),
                small[18 + 9 * u : 27 + 9 * u, :],
                factor,
            )


def run_update(tokens_all, head, out_own, out_other, in_own, in_other, grad, small, state):
    half = out_own.shape[0]

    def all_of(a):
        return pl.BlockSpec(a.shape, lambda i, *_, n=a.ndim: (0,) * n)

    block = (1,) + out_own.shape[1:]
    own = pl.BlockSpec(block, lambda i, head: (jnp.clip(i - head[0] * half, 0, half - 1), 0, 0, 0))
    other = pl.BlockSpec(
        block, lambda i, head: (jnp.clip(i - (1 - head[0]) * half, 0, half - 1), 0, 0, 0)
    )
    final = pl.BlockSpec(block, lambda i, *_: (i, 0, 0, 0))
    whole = (2 * half,) + out_own.shape[1:]

    def kernel(*refs):
        update_kernel(*refs, tokens_all=tokens_all)

    return pl.pallas_call(
        kernel,
        out_shape=[jax.ShapeDtypeStruct(whole, BF), jax.ShapeDtypeStruct(whole, F32)]
        + [jax.ShapeDtypeStruct(a.shape, F32) for a in state],
        grid_spec=pltpu.PrefetchScalarGridSpec(
            num_scalar_prefetch=1,
            grid=(2 * half,),
            in_specs=[own, other, own, other, all_of(grad), all_of(small)]
            + [all_of(a) for a in state],
            out_specs=[final, final] + [all_of(a) for a in state],
        ),
        compiler_params=pltpu.CompilerParams(
            dimension_semantics=("arbitrary",), vmem_limit_bytes=LIMIT
        ),
        name="update",
    )(head, out_own, out_other, in_own, in_other, grad, small, *state)


def per_device(
    tokens,
    cotangent,
    resolution,
    live_images,
    entry_weight,
    entry_momentum,
    entry_average,
    mixing_weight,
    mixing_momentum,
    mixing_average,
    expand_weight,
    expand_momentum,
    expand_average,
    shrink_weight,
    shrink_momentum,
    shrink_average,
    reduce_weight,
    reduce_momentum,
    reduce_average,
    norm_params,
    norm_momentum,
    norm_average,
    value_filter,
    value_momentum,
    value_average,
    hidden_filter,
    hidden_momentum,
    hidden_average,
):
    devices = lax.axis_size("dp")
    head = lax.axis_index("head").reshape(1).astype(jnp.int32)
    block, filters = run_pack(
        devices,
        entry_weight,
        mixing_weight,
        expand_weight,
        shrink_weight,
        reduce_weight,
        value_filter,
        hidden_filter,
    )
    blocks, filters = run_gather(devices, block, filters)
    out_half, input_half, mine, theirs, small_mine, small_theirs = run_block(
        resolution, live_images, head, tokens, cotangent, blocks, filters, norm_params
    )
    grad, small, out_other, input_other = run_reduce(
        devices, mine, theirs, small_mine, small_theirs, out_half, input_half
    )
    state = (
        entry_weight,
        entry_momentum,
        entry_average,
        mixing_weight,
        mixing_momentum,
        mixing_average,
        expand_weight,
        expand_momentum,
        expand_average,
        shrink_weight,
        shrink_momentum,
        shrink_average,
        reduce_weight,
        reduce_momentum,
        reduce_average,
        norm_params,
        norm_momentum,
        norm_average,
        value_filter,
        value_momentum,
        value_average,
        hidden_filter,
        hidden_momentum,
        hidden_average,
    )
    tokens_all = devices * tokens.shape[0] * tokens.shape[1] * tokens.shape[2]
    return tuple(
        run_update(
            tokens_all, head, out_half, out_other, input_half, input_other, grad, small, state
        )
    )


def solution(mesh):
    in_specs = (
        P("dp", None, None, None),
        P("dp", None, None, None),
        P("dp"),
        P("dp"),
        P(None, "dp", "head"),
        P(None, "dp", "head"),
        P(None, "dp", "head"),
        P("head", "dp"),
        P("head", "dp"),
        P("head", "dp"),
        P("dp", "head"),
        P("dp", "head"),
        P("dp", "head"),
        P("head", "dp"),
        P("head", "dp"),
        P("head", "dp"),
        P("dp", "head"),
        P("dp", "head"),
        P("dp", "head"),
        P(),
        P(),
        P(),
        P(None, None, "head"),
        P(None, None, "head"),
        P(None, None, "head"),
        P(None, "head"),
        P(None, "head"),
        P(None, "head"),
    )
    out_specs = (
        P("dp", None, None, None),
        P("dp", None, None, None),
        P(None, "dp", "head"),
        P(None, "dp", "head"),
        P(None, "dp", "head"),
        P("head", "dp"),
        P("head", "dp"),
        P("head", "dp"),
        P("dp", "head"),
        P("dp", "head"),
        P("dp", "head"),
        P("head", "dp"),
        P("head", "dp"),
        P("head", "dp"),
        P("dp", "head"),
        P("dp", "head"),
        P("dp", "head"),
        P(),
        P(),
        P(),
        P(None, None, "head"),
        P(None, None, "head"),
        P(None, None, "head"),
        P(None, "head"),
        P(None, "head"),
        P(None, "head"),
    )
    return jax.shard_map(
        per_device, mesh=mesh, in_specs=in_specs, out_specs=out_specs, check_vma=False
    )
```

```python
import math

import jax
import jax.numpy as jnp
import numpy as np
from jax import lax
from jax.experimental import pallas as pl
from jax.experimental.pallas import tpu as pltpu
from jax.sharding import PartitionSpec as P

BF = jnp.bfloat16
F32 = jnp.float32
EPSILON = 1e-06
HALF = 16
MASKED = -1e9
NN = (((1,), (0,)), ((), ()))
NT = (((1,), (1,)), ((), ()))
TN = (((0,), (0,)), ((), ()))
MESH = pl.DeviceIdType.MESH
SMALL = 64
PAIR = 2
LIMIT = 60 * 1024 * 1024
ROOT = math.sqrt(0.5)


def mm(a, b, dims=NN):
    return lax.dot_general(a, b, dims, preferred_element_type=F32)


def block_of(a4, b4):
    return (a4 % 2) * 8 + (b4 % 2) * 4 + (a4 // 2) * 2 + b4 // 2


def place_of(block):
    return ((block >> 1) & 1) * 2 + (block >> 3), (block & 1) * 2 + ((block >> 2) & 1)


def order_matrix():
    perm = np.zeros((256, 256), np.float32)
    for block in range(16):
        a4, b4 = place_of(block)
        for ci in range(4):
            for ck in range(4):
                perm[block * 16 + ci * 4 + ck, (4 * ci + a4) * HALF + 4 * ck + b4] = 1
    return perm


def cell_shifts():
    places = []
    for ci in range(4):
        for ck in range(4):
            places.append((0, ci, ck, ci // 2, ck // 2))
    for ah in range(2):
        for bh in range(2):
            for ci in range(4):
                for ck in range(4):
                    places.append((1, 2 * ci + ah, 2 * ck + bh, ci // 2, ck // 2))
    index = {p[:3]: n for n, p in enumerate(places)}
    shifts = np.zeros((2, 9, 80, 80), np.float32)
    for n, (g, i, k, si, sk) in enumerate(places):
        for tap in range(9):
            other = index.get((g, i + tap // 3 - 1, k + tap % 3 - 1))
            if other is not None:
                shifts[0, tap, n, other] = 1
                if places[other][3:] == (si, sk):
                    shifts[1, tap, n, other] = 1
    shifts = shifts.reshape(2, 720, 80)
    return np.concatenate([shifts, shifts], 2)


def score_bias():
    rows = np.array([(n % 16) for _ in range(2) for n in list(range(16)) + list(range(64))])
    cols = np.arange(256) % 16

    def image(n):
        return (n // 8) * 2 + (n % 4) // 2

    return np.where(image(rows)[:, None] == image(cols)[None, :], 0.0, MASKED).astype(np.float32)


def shift_masks():
    masks = np.zeros((2, 4, 16, 128), np.float32)
    for fine in range(2):
        for ci in range(4):
            for ck in range(4):
                row = ci * 4 + ck
                for n, (d, e) in enumerate(((1, 0), (-1, 0), (0, 1), (0, -1))):
                    ni, nk = ci + d, ck + e
                    ok = 0 <= ni < 4 and 0 <= nk < 4
                    if fine:
                        ok = ok and ni // 2 == ci // 2 and nk // 2 == ck // 2
                    masks[fine, n, row] = ok
    return masks


def normalise(x):
    centred = x - jnp.mean(x, -1, keepdims=True)
    scale = lax.rsqrt(jnp.mean(centred * centred, -1, keepdims=True) + EPSILON)
    return centred * scale, scale


def normalise_back(grad, unit, scale):
    return scale * (
        grad
        - jnp.mean(grad, -1, keepdims=True)
        - unit * jnp.mean(grad * unit, -1, keepdims=True)
    )


def gelu_pair(h):
    below = 0.5 + 0.5 * lax.erf(h * math.sqrt(0.5))
    density = jnp.exp2(h * h * (-0.5 * math.log2(math.e)))
    return h * below, below + h * density * (1.0 / math.sqrt(2 * math.pi))


def scaled_gelu_pair(u):
    below = math.sqrt(0.5) + math.sqrt(0.5) * lax.erf(u)
    density = jnp.exp2(u * u * (-math.log2(math.e)))
    return u * below, below + u * density * (2.0 / math.sqrt(2 * math.pi))


def block_kernel(
    resolution,
    live_images,
    head,
    tokens,
    cotangent,
    packed,
    filters,
    norms,
    perm,
    perm_t,
    shifts,
    bias,
    edge,
    out,
    input_grad,
    mine,
    theirs,
    small_mine,
    small_theirs,
    entry,
    mixing_t,
    expand,
    shrink_t,
    reduce_w,
    value_filter,
    hidden_filter,
    wide_s,
    square_s,
    d_entry,
    d_mixing_t,
    d_shrink_t,
    d_reduce_t,
    d_norm,
    d_value,
    conv_w,
    key_value_w,
    g_low,
    m_sum,
    folds,
    d_key_value,
    reduce_low,
    im2col,
    im2col_t,
    middle_s,
    up_s,
    unit1_s,
    scale1_s,
    unit2_s,
    scale2_s,
    normed_s,
    queries_s,
    mixed_s,
    probs,
    keys_s,
    enhanced_s,
    values_s,
    wide_cells,
    wide_scale,
    narrow_cells,
    narrow_scale,
    second_grad_s,
    *,
    steps,
):
    step = pl.program_id(0)
    last = pl.num_programs(0) - 1
    first_grid = head[0] * steps
    devices = packed.shape[0] // 2
    width = 128 // devices
    ff = expand.shape[1]
    lane = lax.broadcasted_iota(jnp.int32, (128, 128), 1)
    first_lanes = lane % 64 < 32

    def left(rows):
        return lax.broadcasted_iota(jnp.int32, (rows, 128), 1) < 64

    @pl.when(step == 0)
    def prepare():
        top, chunk = 12 * width, ff // 256
        for d in range(devices):
            one, two = [packed[2 * d + h].astype(F32) for h in range(2)]
            mask = left(top)
            reduce_w[20 * width * d : 20 * width * d + top, :] = jnp.where(
                mask, one[:top], pltpu.roll(two[:top], 64, 1)
            )
            rest = jnp.where(mask, pltpu.roll(one[:top], 64, 1), two[:top])
            reduce_w[20 * width * d + top : 20 * width * (d + 1), :] = rest[: 8 * width]
            rows = slice(width * d, width * d + width)
            for e in range(4):
                square_s[e, rows, :] = rest[(8 + e) * width : (9 + e) * width]
            for h, part in enumerate((one, two)):
                for u in range(chunk):
                    cols = slice((h * chunk + u) * 128, (h * chunk + u + 1) * 128)
                    wide_s[0, rows, cols] = part[top + u * width : top + (u + 1) * width]
                    wide_s[1, rows, cols] = part[
                        top + (chunk + u) * width : top + (chunk + u + 1) * width
                    ]
        reduce_low[...] = reduce_w[...].astype(BF)
        entry[...] = square_s[:3].astype(BF)
        mixing_t[...] = square_s[3].astype(BF)
        expand[...] = wide_s[0]
        shrink_t[...] = wide_s[1].astype(BF)
        for h in range(2):
            hidden_filter[:, h * (ff // 2) : (h + 1) * (ff // 2)] = filters[h, :9, : ff // 2]
        value_filter[...] = jnp.where(
            left(9),
            filters[0, :9, ff // 2 :],
            pltpu.roll(filters[1, :9, ff // 2 :], 64, 1),
        )
        for tap in range(9):
            gain = hidden_filter[tap : tap + 1, :]
            if tap == 4:
                gain = gain + 1.0
            conv_w[tap * 128 : (tap + 1) * 128, :] = (expand[...] * (gain * ROOT)).astype(BF)
        for g in range(2):
            w = entry[1 + g].astype(F32)
            if g == 0:
                keys, vals = w, pltpu.roll(w, 96, 1)
                keep = first_lanes
            else:
                keys, vals = pltpu.roll(w, 32, 1), w
                keep = jnp.logical_not(first_lanes)
            key_value_w[g, :, :128] = jnp.where(keep, keys, 0.0).astype(BF)
            key_value_w[g, :, 128:] = jnp.where(keep, vals, 0.0).astype(BF)
        for ref in (d_entry, d_mixing_t, d_shrink_t, d_reduce_t, d_norm, d_value, m_sum, d_key_value):
            ref[...] = jnp.zeros_like(ref)

    def ordered(ref, place):
        parts = [
            ref[place, a * 16 : a * 16 + 16, b * 16 : b * 16 + 16, :].reshape(256, 128)
            for a in range(2)
            for b in range(2)
        ]
        rows = mm(perm[...], jnp.concatenate(parts, 1))
        return jnp.stack(
            [rows[:, q * 128 : q * 128 + 128].reshape(16, 16, 128) for q in range(4)], 1
        ).reshape(1024, 128)

    def restore(value, ref, place):
        blocks = value.reshape(16, 4, 16, 128)
        rows = mm(
            perm_t[...],
            jnp.concatenate([blocks[:, q].reshape(256, 128) for q in range(4)], 1),
        ).astype(BF)
        for q in range(4):
            a, b = q // 2, q % 2
            ref[pl.ds(place, 1), a * 16 : a * 16 + 16, b * 16 : b * 16 + 16, :] = rows[
                :, q * 128 : q * 128 + 128
            ].reshape(1, 16, 16, 128)

    def of_quadrant(value, q, blocks):
        return value.reshape(blocks, 4, 16, 128)[:, q].reshape(blocks * 16, 128)

    def of_quadrants(parts, blocks):
        return jnp.stack([p.reshape(blocks, 16, 128) for p in parts], 1).reshape(
            blocks * 64, 128
        )

    def gain(n):
        return norms[0, n : n + 1, :]

    def shift_by(n):
        return norms[1, n : n + 1, :]

    def add_norm(n, grad, unit):
        d_norm[n : n + 1, :] += jnp.sum(grad * unit, 0, keepdims=True)
        d_norm[4 + n : 5 + n, :] += jnp.sum(grad, 0, keepdims=True)

    lane80 = lax.broadcasted_iota(jnp.int32, (80, 128), 1)
    zero80 = jnp.zeros((80, 128), BF)
    segments = ((0, 16), (16, 80), (80, 96), (96, 160))
    scaling = 32**-0.5
    rows_of = (slice(0, 2048), slice(2048, 2560))
    cells_f = (wide_cells, narrow_cells)
    cells_scale = (wide_scale, narrow_scale)

    def fine_of(grid):
        return (resolution[first_grid + grid] == 8).astype(jnp.int32)

    def patches_of(slot, g):
        if g == 0:
            blocks = [block_of(t // 4, t % 4) for t in range(16)]
            parts = [normed_s[slot, b * 64 : b * 64 + 64, :] for b in blocks]
        else:
            parts = [normed_s[slot, t * 256 : t * 256 + 256, :] for t in range(4)]
        return jnp.concatenate(parts, 1)

    def move(value, fine, rows, columns):
        size = value.shape[0]
        if rows:
            n = 0 if rows > 0 else 1
            value = pltpu.roll(value, (-4 * rows) % size, 0)
            value = (
                value.reshape(size // 16, 16, 128) * edge[pl.ds(fine, 1), n : n + 1][0]
            ).reshape(size, 128)
        if columns:
            n = 2 if columns > 0 else 3
            value = pltpu.roll(value, (-columns) % size, 0)
            value = (
                value.reshape(size // 16, 16, 128) * edge[pl.ds(fine, 1), n : n + 1][0]
            ).reshape(size, 128)
        return value

    def wrap(a4, d):
        return (a4 + d) % 4, (a4 + d) // 4

    def attend(slot, grid):
        fine = fine_of(grid)
        alive = live_images[first_grid + grid]
        x = ordered(tokens, slot)
        unit1, scale1 = normalise(x)
        unit1_s[slot] = unit1
        scale1_s[slot] = scale1
        normed = (unit1 * gain(0) + shift_by(0)).astype(BF)
        normed_s[slot] = normed
        yield
        queries_s[slot] = mm(normed, entry[0]).astype(BF)
        keys, values = [], []
        for g in range(2):
            reduced = mm(patches_of(slot, g), reduce_low[rows_of[g], :])
            unit, scale = normalise(reduced)
            act, slope = gelu_pair(unit * gain(1 + g) + shift_by(1 + g))
            cells_f[g][slot, 0] = unit
            cells_f[g][slot, 1] = slope
            cells_f[g][slot, 2] = act
            cells_scale[g][slot] = scale
            pair = mm(act.astype(BF), key_value_w[g])
            keys.append(pair[:, :128].astype(BF))
            values.append(pair[:, 128:])
            yield
        keys_all = [
            jnp.concatenate([keys[0][q * 16 : q * 16 + 16], of_quadrant(keys[1], q, 4)], 0)
            for q in range(4)
        ]
        values_all = jnp.concatenate(
            [
                jnp.concatenate(
                    [values[0][q * 16 : q * 16 + 16], of_quadrant(values[1], q, 4)], 0
                )
                for q in range(4)
            ],
            1,
        )
        values_s[slot] = values_all
        moves = shifts[pl.ds(fine, 1)][0]
        high = values_all.astype(BF)
        rest = (values_all - high.astype(F32)).astype(BF)
        moved = mm(moves, jnp.concatenate([high, rest], 0))
        taps4 = jnp.concatenate([value_filter[...]] * 4, 1)
        enhanced = values_all
        for tap in range(9):
            enhanced = enhanced + moved[tap * 80 : tap * 80 + 80] * taps4[tap : tap + 1]
        enhanced = enhanced.astype(BF)
        yield

        def both_heads(rows):
            return jnp.concatenate(
                [jnp.where(lane80 < 64, rows, zero80), jnp.where(lane80 < 64, zero80, rows)], 0
            )

        queries = queries_s[slot]
        scores = []
        for q in range(4):
            keys_s[slot, q] = both_heads(keys_all[q])
            enhanced_s[slot, q] = both_heads(enhanced[:, q * 128 : q * 128 + 128])
            scores.append(mm(keys_s[slot, q], of_quadrant(queries, q, 16), NT))
        yield
        for q in range(4):
            biased = scores[q] * scaling + fine.astype(F32) * bias[...]
            for lo, hi in segments:
                part = biased[lo:hi]
                part = jnp.exp(part - jnp.max(part, 0, keepdims=True))
                probs[slot, q, lo:hi, :] = part * (1.0 / jnp.sum(part, 0, keepdims=True))
        yield
        mixed_parts = [
            mm(probs[slot, q].astype(BF), enhanced_s[slot, q], TN) for q in range(4)
        ]
        yield
        mixed = of_quadrants(mixed_parts, 16).astype(BF)
        mixed_s[slot] = mixed
        middle = x + mm(mixed, mixing_t[...], NT)
        middle_s[slot] = middle
        yield
        unit2, scale2 = normalise(middle)
        unit2_s[slot] = unit2
        scale2_s[slot] = scale2
        second_low = (unit2 * gain(3) + shift_by(3)).astype(BF)
        second_f = second_low.astype(F32)
        yield
        moved_blocks = {}
        for block in range(16):
            a4, b4 = place_of(block)
            for tap in range(9):
                na, wa = wrap(a4, tap // 3 - 1)
                nb, wb = wrap(b4, tap % 3 - 1)
                source = block_of(na, nb)
                key = (source, wa, wb)
                if key not in moved_blocks:
                    rows = slice(source * 64, source * 64 + 64)
                    if wa or wb:
                        moved_blocks[key] = move(second_f[rows], fine, wa, wb).astype(BF)
                    else:
                        moved_blocks[key] = second_low[rows]
                im2col[slot, block * 64 : block * 64 + 64, tap * 128 : tap * 128 + 128] = (
                    moved_blocks[key]
                )
            yield
        row16 = lax.broadcasted_iota(jnp.int32, (16, 128), 0)
        within = (row16 // 8) * 4 + (row16 % 4) // 2
        live = jnp.stack(
            [
                jnp.where(
                    jnp.where(fine == 1, within + (q // 2) * 8 + (q % 2) * 2, q) < alive, 1.0, 0.0
                )
                for q in range(4)
            ],
            0,
        )
        up_low = (
            (ordered(cotangent, slot).reshape(16, 4, 16, 128) * live[None])
            .reshape(1024, 128)
            .astype(BF)
        )
        up_s[slot] = up_low
        yield

    def feed(slot, grid):
        fine = fine_of(grid)
        total = middle_s[slot]
        wide = 256
        held = None
        for c in range(0, ff + wide, wide):
            if c < ff:
                cols = slice(c, c + wide)
                hidden = mm(im2col[slot], conv_w[:, cols])
                grad = mm(up_s[slot], shrink_t[:, cols])
            if c == 0:
                for tap in range(9):
                    im2col_t[tap * 128 : tap * 128 + 128, :] = im2col[
                        slot, :, tap * 128 : tap * 128 + 128
                    ].T
                up_t = up_s[slot].T
            if held:
                before, act, back = held
                total = total + mm(act, shrink_t[:, before], NT)
                d_shrink_t[:, before] += mm(up_t, act)
                m_sum[:, before] += mm(im2col_t[...], back)
            if c < ff:
                act, slope = scaled_gelu_pair(hidden)
                act = act.astype(BF)
                grad = (grad * slope).astype(BF)
                g_low[:, cols] = grad
                held = (cols, act, grad)
        restore(total.astype(BF), out, slot)
        for t in range(0, 9, 2):
            rows = slice(t * 128, min(t + 2, 9) * 128)
            folds[:, rows] = mm(g_low[...], conv_w[rows, :], NT)
        sums = {}
        for block in range(16):
            a4, b4 = place_of(block)
            for tap in range(9):
                na, wa = wrap(a4, tap // 3 - 1)
                nb, wb = wrap(b4, tap % 3 - 1)
                key = (block_of(na, nb), wa, wb)
                sums.setdefault(key, []).append((block, tap))
        for block in range(16):
            total = None
            for (source, wa, wb), terms in sums.items():
                if source != block:
                    continue
                part = None
                for other, tap in terms:
                    term = folds[other * 64 : other * 64 + 64, tap * 128 : tap * 128 + 128]
                    part = term if part is None else part + term
                if wa or wb:
                    part = move(part, fine, -wa, -wb)
                total = part if total is None else total + part
            second_grad_s[slot, block * 64 : block * 64 + 64, :] = total

    def back(slot, grid):
        fine = fine_of(grid)
        second_grad = second_grad_s[slot]
        unit2 = unit2_s[slot]
        add_norm(3, second_grad, unit2)
        middle_grad = up_s[slot].astype(F32) + normalise_back(
            second_grad * gain(3), unit2, scale2_s[slot]
        )
        middle_low = middle_grad.astype(BF)
        yield
        mixed = mixed_s[slot]
        d_mixing_t[...] += mm(middle_low, mixed, TN)
        mixed_grad = mm(middle_low, mixing_t[...]).astype(BF)
        queries = queries_s[slot]
        yield
        out_grads = [of_quadrant(mixed_grad, q, 16) for q in range(4)]
        prob_grads = [mm(enhanced_s[slot, q], out_grads[q], NT) for q in range(4)]
        yield
        enhanced_parts = []
        for q in range(4):
            full = mm(probs[slot, q].astype(BF), out_grads[q])
            enhanced_parts.append(jnp.where(lane80 < 64, full[:80], full[80:]).astype(BF))
        yield
        score_lows = []
        for q in range(4):
            weights = probs[slot, q]
            product = weights * prob_grads[q]
            score_grad = []
            for lo, hi in segments:
                score_grad.append(
                    product[lo:hi] - weights[lo:hi] * jnp.sum(product[lo:hi], 0, keepdims=True)
                )
            score_lows.append((scaling * jnp.concatenate(score_grad, 0)).astype(BF))
        yield
        query_parts = [mm(score_lows[q], keys_s[slot, q], TN) for q in range(4)]
        yield
        key_parts = []
        for q in range(4):
            full = mm(score_lows[q], of_quadrant(queries, q, 16))
            key_parts.append(jnp.where(lane80 < 64, full[:80], full[80:]).astype(BF))
        yield
        query_low = of_quadrants(query_parts, 16).astype(BF)
        enhanced_grad = jnp.concatenate(enhanced_parts, 1)
        moved = mm(shifts[pl.ds(fine, 1)][0][:, :80], enhanced_grad)
        taps4 = jnp.concatenate([value_filter[...]] * 4, 1)
        value_grad = enhanced_grad.astype(F32)
        values_all = values_s[slot]
        for tap in range(9):
            part = moved[(8 - tap) * 80 : (8 - tap) * 80 + 80]
            value_grad = value_grad + part * taps4[tap : tap + 1]
            row = jnp.sum(part * values_all, 0, keepdims=True)
            d_value[tap : tap + 1, :] += (
                row[:, :128] + row[:, 128:256] + row[:, 256:384] + row[:, 384:]
            )
        value_grad = value_grad.astype(BF)
        value_parts = [value_grad[:, q * 128 : q * 128 + 128] for q in range(4)]
        yield
        normed = normed_s[slot]
        normed_grad = mm(query_low, entry[0], NT)
        d_entry[0] += mm(normed, query_low, TN)
        yield
        for g in range(2):
            if g == 0:
                sides = [
                    jnp.concatenate([p[:16] for p in parts], 0)
                    for parts in (key_parts, value_parts)
                ]
            else:
                sides = [
                    of_quadrants([p[16:] for p in parts], 4) for parts in (key_parts, value_parts)
                ]
            pair = jnp.concatenate(sides, 1)
            unit, slope = cells_f[g][slot, 0], cells_f[g][slot, 1]
            cell_low = cells_f[g][slot, 2].astype(BF)
            d_key_value[g] += mm(cell_low, pair, TN)
            cell_grad = mm(pair, key_value_w[g], NT) * slope
            add_norm(1 + g, cell_grad, unit)
            reduced_low = normalise_back(
                cell_grad * gain(1 + g), unit, cells_scale[g][slot]
            ).astype(BF)
            d_reduce_t[:, rows_of[g]] += mm(reduced_low, patches_of(slot, g), TN)
            spread = mm(reduced_low, reduce_low[rows_of[g], :], NT)
            if g == 0:
                order = [place_of(block) for block in range(16)]
                order = [a4 * 4 + b4 for a4, b4 in order]
            else:
                order = range(4)
            normed_grad = normed_grad + jnp.concatenate(
                [spread[:, t * 128 : t * 128 + 128] for t in order], 0
            )
            yield
        unit1 = unit1_s[slot]
        add_norm(0, normed_grad, unit1)
        raw = middle_grad + normalise_back(normed_grad * gain(0), unit1, scale1_s[slot])
        restore(raw.astype(BF), input_grad, slot)
        yield

    def together(*parts):
        parts = list(parts)
        while parts:
            parts = [part for part in parts if next(part, parts) is not parts]

    first = PAIR * step
    together(*[attend(k, first + k) for k in range(PAIR)])

    def feed_one(k, carry):
        feed(k, first + k)
        return carry

    lax.fori_loop(0, PAIR, feed_one, 0)
    together(*[back(k, first + k) for k in range(PAIR)])

    @pl.when(step == last)
    def finish():
        for c in range(0, ff, 256):
            cols = slice(c, c + 256)
            weight = expand[:, cols]
            total = None
            for tap in range(9):
                part = m_sum[tap * 128 : tap * 128 + 128, cols] * ROOT
                factor = hidden_filter[tap : tap + 1, cols]
                if tap == 4:
                    factor = factor + 1.0
                hidden_filter[tap : tap + 1, cols] = jnp.sum(part * weight, 0, keepdims=True)
                total = part * factor if total is None else total + part * factor
            wide_s[0, :, cols] = total
        wide_s[1] = d_shrink_t[...]
        d_entry[1] = jnp.where(
            first_lanes, d_key_value[0, :, :128], pltpu.roll(d_key_value[0, :, 128:], 32, 1)
        )
        d_entry[2] = jnp.where(
            first_lanes, pltpu.roll(d_key_value[1, :, :128], 96, 1), d_key_value[1, :, 128:]
        )
        is_second = head[0] == 1
        d_reduce = reduce_w
        for n in range(20):
            rows = slice(n * 128, n * 128 + 128)
            d_reduce[rows, :] = d_reduce_t[:, rows].T
        top, chunk = 12 * width, ff // 256
        planes, lines = mine.shape[0], mine.shape[1]

        def put(d, rows, first, second):
            place = (d % planes, d // planes, rows)
            mine[place] = jnp.where(is_second, second, first)
            theirs[place] = jnp.where(is_second, first, second).astype(BF)

        for d in range(devices):
            rows = slice(width * d, width * d + width)
            upper = d_reduce[20 * width * d : 20 * width * d + top, :]
            lower = jnp.concatenate(
                [d_reduce[20 * width * d + top : 20 * width * (d + 1), :]]
                + [d_entry[e, rows, :] for e in range(3)]
                + [d_mixing_t[rows, :]],
                0,
            )
            firsts = [jnp.where(left(top), upper, pltpu.roll(lower, 64, 1))]
            seconds = [jnp.where(left(top), pltpu.roll(upper, 64, 1), lower)]
            for n in range(2):
                for h, parts in enumerate((firsts, seconds)):
                    for u in range(chunk):
                        cols = slice((h * chunk + u) * 128, (h * chunk + u + 1) * 128)
                        parts.append(wide_s[n, rows, cols])
            pad = mine.shape[2] - 20 * width
            if pad:
                firsts.append(jnp.zeros((pad, 128), F32))
                seconds.append(jnp.zeros((pad, 128), F32))
            put(d, slice(None), jnp.concatenate(firsts, 0), jnp.concatenate(seconds, 0))
        count = jnp.int32(0)
        for n in range(steps):
            side = resolution[head[0] * steps + n]
            count = count + side * side * live_images[head[0] * steps + n]
        halves = [
            jnp.concatenate(
                [
                    hidden_filter[:, (h * chunk + u) * 128 : (h * chunk + u + 1) * 128]
                    for u in range(chunk)
                ],
                0,
            )
            for h in range(2)
        ]
        for ref, flip in ((small_mine, False), (small_theirs, True)):
            ref[...] = jnp.zeros_like(ref)
            ref[:8, :] = d_norm[...]
            ref[8:17, :] = d_value[...]
            ref[17:18, :] = jnp.full((1, 128), count, jnp.int32).astype(F32)
            second = jnp.logical_not(is_second) if flip else is_second
            ref[18 : 18 + 9 * chunk, :] = jnp.where(second, halves[1], halves[0])


def run_block(resolution, live_images, head, tokens, cotangent, packed, filters, norms):
    steps = tokens.shape[0] // 2
    devices, rows = packed.shape[0] // 2, packed.shape[1]
    ff = 2 * (filters.shape[2] - 128)
    lines = line_of(devices)
    consts = [
        jnp.asarray(order_matrix(), BF),
        jnp.asarray(order_matrix().T, BF),
        jnp.asarray(cell_shifts(), BF),
        jnp.asarray(score_bias(), F32),
        jnp.asarray(shift_masks(), F32),
    ]
    whole = [packed, filters, norms] + consts

    def all_of(a):
        return pl.BlockSpec(a.shape, lambda i, *_, n=a.ndim: (0,) * n)

    grid_in = pl.BlockSpec(
        (PAIR, 32, 32, 128), lambda i, res, live, head: (head[0] * (steps // PAIR) + i, 0, 0, 0)
    )
    grid_out = pl.BlockSpec((PAIR, 32, 32, 128), lambda i, *_: (i, 0, 0, 0))
    out_shape = [
        jax.ShapeDtypeStruct((steps, 32, 32, 128), BF),
        jax.ShapeDtypeStruct((steps, 32, 32, 128), BF),
        jax.ShapeDtypeStruct((devices // lines, lines, rows, 128), F32),
        jax.ShapeDtypeStruct((devices // lines, lines, rows, 128), BF),
        jax.ShapeDtypeStruct((SMALL, 128), F32),
        jax.ShapeDtypeStruct((SMALL, 128), F32),
    ]

    def kernel(*refs):
        block_kernel(*refs, steps=steps)

    return pl.pallas_call(
        kernel,
        out_shape=out_shape,
        grid_spec=pltpu.PrefetchScalarGridSpec(
            num_scalar_prefetch=3,
            grid=(steps // PAIR,),
            in_specs=[grid_in, grid_in] + [all_of(a) for a in whole],
            out_specs=[grid_out, grid_out] + [all_of(a) for a in out_shape[2:]],
            scratch_shapes=[
                pltpu.VMEM((3, 128, 128), BF),
                pltpu.VMEM((128, 128), BF),
                pltpu.VMEM((128, ff), F32),
                pltpu.VMEM((128, ff), BF),
                pltpu.VMEM((2560, 128), F32),
                pltpu.VMEM((9, 128), F32),
                pltpu.VMEM((9, ff), F32),
                pltpu.VMEM((2, 128, ff), F32),
                pltpu.VMEM((4, 128, 128), F32),
                pltpu.VMEM((3, 128, 128), F32),
                pltpu.VMEM((128, 128), F32),
                pltpu.VMEM((128, ff), F32),
                pltpu.VMEM((128, 2560), F32),
                pltpu.VMEM((8, 128), F32),
                pltpu.VMEM((9, 128), F32),
                pltpu.VMEM((1152, ff), BF),
                pltpu.VMEM((2, 128, 256), BF),
                pltpu.VMEM((1024, ff), BF),
                pltpu.VMEM((1152, ff), F32),
                pltpu.VMEM((1024, 1152), F32),
                pltpu.VMEM((2, 128, 256), F32),
                pltpu.VMEM((2560, 128), BF),
                pltpu.VMEM((2, 1024, 1152), BF),
                pltpu.VMEM((1152, 1024), BF),
                pltpu.VMEM((2, 1024, 128), F32),
                pltpu.VMEM((2, 1024, 128), BF),
                pltpu.VMEM((2, 1024, 128), F32),
                pltpu.VMEM((2, 1024, 1), F32),
                pltpu.VMEM((2, 1024, 128), F32),
                pltpu.VMEM((2, 1024, 1), F32),
                pltpu.VMEM((2, 1024, 128), BF),
                pltpu.VMEM((2, 1024, 128), BF),
                pltpu.VMEM((2, 1024, 128), BF),
                pltpu.VMEM((2, 4, 160, 256), F32),
                pltpu.VMEM((2, 4, 160, 128), BF),
                pltpu.VMEM((2, 4, 160, 128), BF),
                pltpu.VMEM((2, 80, 512), F32),
                pltpu.VMEM((2, 3, 64, 128), F32),
                pltpu.VMEM((2, 64, 1), F32),
                pltpu.VMEM((2, 3, 256, 128), F32),
                pltpu.VMEM((2, 256, 1), F32),
                pltpu.VMEM((2, 1024, 128), F32),
            ],
        ),
        compiler_params=pltpu.CompilerParams(
            dimension_semantics=("arbitrary",), vmem_limit_bytes=LIMIT
        ),
        name="block",
    )(resolution, live_images, head, tokens, cotangent, *whole)


def line_of(devices):
    return 4 if devices % 4 == 0 else 1


def rows_of_block(devices):
    return -(-20 * (128 // devices) // 16) * 16


def pack_kernel(entry, mixing_t, expand, shrink_t, reduce_t, values, hidden, block, filters, held):
    width, ff = expand.shape
    top, chunk = 12 * width, ff // 128
    held[...] = jnp.zeros_like(held)
    rows = reduce_t[...].T
    held[:top, :64] = rows[:top, :]
    held[: 8 * width, 64:] = rows[top:, :]
    for e in range(3):
        held[(8 + e) * width : (9 + e) * width, 64:] = entry[e]
    held[11 * width : top, 64:] = mixing_t[...]
    for u in range(chunk):
        cols = slice(u * 128, (u + 1) * 128)
        held[top + u * width : top + (u + 1) * width, :] = expand[:, cols]
        held[top + (chunk + u) * width : top + (chunk + u + 1) * width, :] = shrink_t[:, cols]
    block[...] = held[...].astype(BF)
    filters[...] = jnp.zeros_like(filters)
    filters[:9, :ff] = hidden[...]
    for g in range(2):
        filters[:9, ff + 32 * g : ff + 32 * g + 32] = values[:, g]


def run_pack(devices, entry, mixing_t, expand, shrink_t, reduce_t, values, hidden):
    rows = rows_of_block(devices)
    return pl.pallas_call(
        pack_kernel,
        out_shape=[
            jax.ShapeDtypeStruct((rows, 128), BF),
            jax.ShapeDtypeStruct((16, hidden.shape[1] + 128), F32),
        ],
        scratch_shapes=[pltpu.VMEM((rows, 128), F32)],
        compiler_params=pltpu.CompilerParams(vmem_limit_bytes=LIMIT),
        name="pack",
    )(entry, mixing_t, expand, shrink_t, reduce_t, values, hidden)


def greet(peers):
    barrier = pltpu.get_barrier_semaphore()
    for peer in peers:
        pl.semaphore_signal(barrier, inc=1, device_id=peer, device_id_type=MESH)
    pl.semaphore_wait(barrier, len(peers))


def places(devices):
    lines = line_of(devices)
    planes = devices // lines
    me, head = lax.axis_index("dp"), lax.axis_index("head")
    z, p = me // planes, me % planes
    line_peers = [((z + k) % lines) for k in range(1, lines)]
    plane_peers = [((p + k) % planes) for k in range(1, planes)]
    return lines, planes, z, p, head, line_peers, plane_peers


def gather_kernel(devices, block, filters, blocks, both, send_sem, recv_sem, filter_sem, local_sem):
    lines, planes, z, p, head, line_peers, plane_peers = places(devices)

    def slot(line, plane, core):
        return (line * planes + plane) * 2 + core

    def at(line, plane, core):
        return (line * planes + plane, core)

    sibling = at(z, p, 1 - head)
    greet(
        [at(k, p, head) for k in line_peers] + [at(z, k, head) for k in plane_peers] + [sibling]
    )
    sends = []

    def send(source, index, target):
        copy = pltpu.make_async_remote_copy(
            src_ref=source,
            dst_ref=blocks.at[index],
            send_sem=send_sem.at[len(sends)],
            recv_sem=recv_sem.at[index],
            device_id=target,
            device_id_type=MESH,
        )
        copy.start()
        sends.append(copy)

    def arrived(index):
        pltpu.make_async_remote_copy(
            src_ref=block,
            dst_ref=blocks.at[index],
            send_sem=send_sem.at[0],
            recv_sem=recv_sem.at[index],
            device_id=sibling,
            device_id_type=MESH,
        ).wait_recv()

    own = slot(z, p, head)
    for k in line_peers:
        send(block, own, at(k, p, head))
    for k in plane_peers:
        send(block, own, at(z, k, head))
    send(block, own, sibling)
    swap = pltpu.make_async_remote_copy(
        src_ref=filters,
        dst_ref=both.at[head],
        send_sem=filter_sem.at[0],
        recv_sem=filter_sem.at[1],
        device_id=sibling,
        device_id_type=MESH,
    )
    swap.start()
    keep = [
        pltpu.make_async_copy(block, blocks.at[own], local_sem.at[0]),
        pltpu.make_async_copy(filters, both.at[head], local_sem.at[1]),
    ]
    for copy in keep:
        copy.start()
    for k in line_peers:
        index = slot(k, p, head)
        arrived(index)
        for j in plane_peers:
            send(blocks.at[index], index, at(z, j, head))
        send(blocks.at[index], index, sibling)
    for line in [z] + line_peers:
        for j in plane_peers:
            index = slot(line, j, head)
            arrived(index)
            send(blocks.at[index], index, sibling)
    for line in [z] + line_peers:
        for j in [p] + plane_peers:
            arrived(slot(line, j, 1 - head))
    for copy in sends:
        copy.wait_send()
    swap.wait_send()
    pltpu.make_async_remote_copy(
        src_ref=filters,
        dst_ref=both.at[1 - head],
        send_sem=filter_sem.at[0],
        recv_sem=filter_sem.at[1],
        device_id=sibling,
        device_id_type=MESH,
    ).wait_recv()
    for copy in keep:
        copy.wait()


def run_gather(devices, block, filters):
    lines = line_of(devices)
    planes = devices // lines
    copies = (lines - 1) + lines * (planes - 1) + lines * planes
    anywhere = pl.BlockSpec(memory_space=pl.ANY)

    def kernel(*refs):
        gather_kernel(devices, *refs)

    return pl.pallas_call(
        kernel,
        out_shape=[
            jax.ShapeDtypeStruct((2 * devices,) + block.shape, BF),
            jax.ShapeDtypeStruct((2,) + filters.shape, F32),
        ],
        in_specs=[anywhere, anywhere],
        out_specs=[anywhere, anywhere],
        scratch_shapes=[
            pltpu.SemaphoreType.DMA((copies,)),
            pltpu.SemaphoreType.DMA((2 * devices,)),
            pltpu.SemaphoreType.DMA((2,)),
            pltpu.SemaphoreType.DMA((2,)),
        ],
        compiler_params=pltpu.CompilerParams(collective_id=0, has_side_effects=True),
        name="gather",
    )(block, filters)


def reduce_kernel(
    devices,
    mine,
    theirs,
    small_mine,
    small_theirs,
    out_half,
    input_half,
    grad,
    small,
    out_other,
    input_other,
    core_in,
    core_small,
    plane_out,
    plane_in,
    plane_small,
    line_sum,
    line_out,
    line_in,
    line_small,
    core_send,
    core_recv,
    plane_send,
    plane_recv,
    line_send,
    line_recv,
):
    lines, planes, z, p, head, line_peers, plane_peers = places(devices)

    def at(line, plane, core):
        return (line * planes + plane, core)

    sibling = at(z, p, 1 - head)
    greet(
        [at(k, p, head) for k in line_peers] + [at(z, k, head) for k in plane_peers] + [sibling]
    )

    def remote(source, target, send, recv, device):
        return pltpu.make_async_remote_copy(
            src_ref=source,
            dst_ref=target,
            send_sem=send,
            recv_sem=recv,
            device_id=device,
            device_id_type=MESH,
        )

    started = []

    def go(*args):
        copy = remote(*args)
        copy.start()
        started.append(copy)

    go(small_theirs, core_small, core_send.at[planes], core_recv.at[planes], sibling)
    for k in plane_peers + [p]:
        go(theirs.at[k], core_in.at[k], core_send.at[k], core_recv.at[k], sibling)
    remote(
        small_theirs, core_small, core_send.at[planes], core_recv.at[planes], sibling
    ).wait_recv()
    plane_small[pl.ds(p, 1)] = (small_mine[...] + core_small[...])[None]
    for n, k in enumerate(plane_peers):
        go(
            plane_small.at[p],
            plane_small.at[p],
            plane_send.at[planes + n],
            plane_recv.at[planes + p],
            at(z, k, head),
        )
    for n, k in enumerate(plane_peers):
        remote(
            theirs.at[k], core_in.at[k], core_send.at[k], core_recv.at[k], sibling
        ).wait_recv()
        plane_out[pl.ds(k, 1)] = (mine[pl.ds(k, 1)] + core_in[pl.ds(k, 1)].astype(F32)).astype(BF)
        go(plane_out.at[k], plane_in.at[p], plane_send.at[n], plane_recv.at[p], at(z, k, head))
    remote(theirs.at[p], core_in.at[p], core_send.at[p], core_recv.at[p], sibling).wait_recv()
    go(out_half, out_other, core_send.at[planes + 1], core_recv.at[planes + 1], sibling)
    go(input_half, input_other, core_send.at[planes + 2], core_recv.at[planes + 2], sibling)
    total = mine[pl.ds(p, 1)][0] + core_in[pl.ds(p, 1)][0].astype(F32)
    for k in plane_peers:
        remote(
            plane_out.at[k], plane_in.at[k], plane_send.at[0], plane_recv.at[k], sibling
        ).wait_recv()
        total = total + plane_in[pl.ds(k, 1)][0].astype(F32)
    line_sum[...] = total
    for n, k in enumerate(line_peers):
        line_out[pl.ds(k, 1)] = line_sum[pl.ds(k, 1)].astype(BF)
        go(line_out.at[k], line_in.at[z], line_send.at[n], line_recv.at[z], at(k, p, head))
    for k in plane_peers:
        remote(
            plane_small.at[p],
            plane_small.at[k],
            plane_send.at[0],
            plane_recv.at[planes + k],
            sibling,
        ).wait_recv()
    part = plane_small[0]
    for k in range(1, planes):
        part = part + plane_small[k]
    line_small[pl.ds(z, 1)] = part[None]
    for n, k in enumerate(line_peers):
        go(
            line_small.at[z],
            line_small.at[z],
            line_send.at[lines + n],
            line_recv.at[lines + z],
            at(k, p, head),
        )
    own = line_sum[pl.ds(z, 1)][0]
    for k in line_peers:
        remote(
            line_out.at[k], line_in.at[k], line_send.at[0], line_recv.at[k], sibling
        ).wait_recv()
        own = own + line_in[pl.ds(k, 1)][0].astype(F32)
    grad[...] = own
    for k in line_peers:
        remote(
            line_small.at[z],
            line_small.at[k],
            line_send.at[0],
            line_recv.at[lines + k],
            sibling,
        ).wait_recv()
    part = line_small[0]
    for k in range(1, lines):
        part = part + line_small[k]
    small[...] = part
    remote(
        out_half, out_other, core_send.at[planes + 1], core_recv.at[planes + 1], sibling
    ).wait_recv()
    remote(
        input_half, input_other, core_send.at[planes + 2], core_recv.at[planes + 2], sibling
    ).wait_recv()
    for copy in started:
        copy.wait_send()


def run_reduce(devices, mine, theirs, small_mine, small_theirs, out_half, input_half):
    planes, lines, rows = mine.shape[:3]
    anywhere = pl.BlockSpec(memory_space=pl.ANY)
    vmem = pl.BlockSpec(memory_space=pltpu.VMEM)
    sem = pltpu.SemaphoreType.DMA

    def kernel(*refs):
        reduce_kernel(devices, *refs)

    return pl.pallas_call(
        kernel,
        out_shape=[
            jax.ShapeDtypeStruct((rows, 128), F32),
            jax.ShapeDtypeStruct((SMALL, 128), F32),
            jax.ShapeDtypeStruct(out_half.shape, BF),
            jax.ShapeDtypeStruct(input_half.shape, BF),
        ],
        in_specs=[vmem] * 4 + [anywhere] * 2,
        out_specs=[vmem] * 2 + [anywhere] * 2,
        scratch_shapes=[
            pltpu.VMEM((planes, lines, rows, 128), BF),
            pltpu.VMEM((SMALL, 128), F32),
            pltpu.VMEM((planes, lines, rows, 128), BF),
            pltpu.VMEM((planes, lines, rows, 128), BF),
            pltpu.VMEM((planes, SMALL, 128), F32),
            pltpu.VMEM((lines, rows, 128), F32),
            pltpu.VMEM((lines, rows, 128), BF),
            pltpu.VMEM((lines, rows, 128), BF),
            pltpu.VMEM((lines, SMALL, 128), F32),
            sem((planes + 3,)),
            sem((planes + 3,)),
            sem((2 * planes,)),
            sem((2 * planes,)),
            sem((2 * lines,)),
            sem((2 * lines,)),
        ],
        compiler_params=pltpu.CompilerParams(
            collective_id=1, has_side_effects=True, vmem_limit_bytes=LIMIT
        ),
        name="reduce",
    )(mine, theirs, small_mine, small_theirs, out_half, input_half)


def advance(weight, moment, average, gradient, step_rate, weight_decay):
    gradient = gradient + weight_decay * weight
    moment = 0.9 * moment + gradient
    weight = weight - step_rate * (gradient + 0.9 * moment)
    return (moment, weight, 0.8 * average + 0.2 * weight)


RATES = (0.3, 0.12, 0.12, 0.03, 0.1, 0.2, 0.4, 0.5)


def update_kernel(head, *refs, tokens_all):
    out_own, out_other, in_own, in_other, grad, small = refs[:6]
    state = refs[6:30]
    output, input_grad = refs[30:32]
    results = refs[32:]
    step = pl.program_id(0)
    half = pl.num_programs(0) // 2
    factor = tokens_all / small[17:18, :]
    is_own = (step // half) == head[0]

    @pl.when(is_own)
    def own():
        output[...] = out_own[...]
        input_grad[...] = in_own[...].astype(F32) * factor

    @pl.when(jnp.logical_not(is_own))
    def other():
        output[...] = out_other[...]
        input_grad[...] = in_other[...].astype(F32) * factor

    @pl.when(step == 0)
    def update():
        width, ff = state[6].shape
        top, chunk = 12 * width, ff // 128
        rate_unit = tokens_all**-0.5

        def apply(n, place, raw, scale):
            new = advance(
                state[3 * n][place],
                state[3 * n + 1][place],
                state[3 * n + 2][place],
                scale * raw,
                RATES[n] * rate_unit,
                0.0 if n == 5 else 0.05,
            )
            for k in range(3):
                results[3 * n + k][place] = new[k]

        scale = factor[:, :64]
        for e in range(3):
            apply(0, e, grad[(8 + e) * width : (9 + e) * width, 64:], scale)
        apply(1, Ellipsis, grad[11 * width : top, 64:], scale)
        for u in range(chunk):
            cols = slice(u * 128, (u + 1) * 128)
            apply(2, (slice(None), cols), grad[top + u * width : top + (u + 1) * width, :], factor)
            apply(
                3,
                (slice(None), cols),
                grad[top + (chunk + u) * width : top + (chunk + u + 1) * width, :],
                factor,
            )
        turned = grad[:top, :].T
        apply(4, (slice(None), slice(0, top)), turned[:64, :], factor[:, :1])
        apply(4, (slice(None), slice(top, 20 * width)), turned[64:, : 8 * width], factor[:, :1])
        for n in range(2):
            apply(5, n, small[4 * n : 4 * n + 4, :], factor)
        values = small[8:17, :]
        values = jnp.where(head[0] == 1, pltpu.roll(values, 64, 1), values)
        for g in range(2):
            apply(6, (slice(None), g), values[:, 32 * g : 32 * g + 32], factor[:, :32])
        for u in range(chunk):
            apply(
                7,
                (slice(None), slice(u * 128, (u + 1) * 128)),
                small[18 + 9 * u : 27 + 9 * u, :],
                factor,
            )


def run_update(tokens_all, head, out_own, out_other, in_own, in_other, grad, small, state):
    half = out_own.shape[0]

    def all_of(a):
        return pl.BlockSpec(a.shape, lambda i, *_, n=a.ndim: (0,) * n)

    block = (1,) + out_own.shape[1:]
    own = pl.BlockSpec(block, lambda i, head: (jnp.clip(i - head[0] * half, 0, half - 1), 0, 0, 0))
    other = pl.BlockSpec(
        block, lambda i, head: (jnp.clip(i - (1 - head[0]) * half, 0, half - 1), 0, 0, 0)
    )
    final = pl.BlockSpec(block, lambda i, *_: (i, 0, 0, 0))
    whole = (2 * half,) + out_own.shape[1:]

    def kernel(*refs):
        update_kernel(*refs, tokens_all=tokens_all)

    return pl.pallas_call(
        kernel,
        out_shape=[jax.ShapeDtypeStruct(whole, BF), jax.ShapeDtypeStruct(whole, F32)]
        + [jax.ShapeDtypeStruct(a.shape, F32) for a in state],
        grid_spec=pltpu.PrefetchScalarGridSpec(
            num_scalar_prefetch=1,
            grid=(2 * half,),
            in_specs=[own, other, own, other, all_of(grad), all_of(small)]
            + [all_of(a) for a in state],
            out_specs=[final, final] + [all_of(a) for a in state],
        ),
        compiler_params=pltpu.CompilerParams(
            dimension_semantics=("arbitrary",), vmem_limit_bytes=LIMIT
        ),
        name="update",
    )(head, out_own, out_other, in_own, in_other, grad, small, *state)


def per_device(
    tokens,
    cotangent,
    resolution,
    live_images,
    entry_weight,
    entry_momentum,
    entry_average,
    mixing_weight,
    mixing_momentum,
    mixing_average,
    expand_weight,
    expand_momentum,
    expand_average,
    shrink_weight,
    shrink_momentum,
    shrink_average,
    reduce_weight,
    reduce_momentum,
    reduce_average,
    norm_params,
    norm_momentum,
    norm_average,
    value_filter,
    value_momentum,
    value_average,
    hidden_filter,
    hidden_momentum,
    hidden_average,
):
    devices = lax.axis_size("dp")
    head = lax.axis_index("head").reshape(1).astype(jnp.int32)
    turns = ((1, 0), (1, 0), (1, 0), (1, 0, 2))
    mixing, shrink, reduced, values = [
        tuple(a.transpose(turn) for a in arrays)
        for turn, arrays in zip(
            turns,
            (
                (mixing_weight, mixing_momentum, mixing_average),
                (shrink_weight, shrink_momentum, shrink_average),
                (reduce_weight, reduce_momentum, reduce_average),
                (value_filter, value_momentum, value_average),
            ),
        )
    ]
    block, filters = run_pack(
        devices,
        entry_weight,
        mixing[0],
        expand_weight,
        shrink[0],
        reduced[0],
        values[0],
        hidden_filter,
    )
    blocks, filters = run_gather(devices, block, filters)
    out_half, input_half, mine, theirs, small_mine, small_theirs = run_block(
        resolution, live_images, head, tokens, cotangent, blocks, filters, norm_params
    )
    grad, small, out_other, input_other = run_reduce(
        devices, mine, theirs, small_mine, small_theirs, out_half, input_half
    )
    state = (
        entry_weight,
        entry_momentum,
        entry_average,
        *mixing,
        expand_weight,
        expand_momentum,
        expand_average,
        *shrink,
        *reduced,
        norm_params,
        norm_momentum,
        norm_average,
        *values,
        hidden_filter,
        hidden_momentum,
        hidden_average,
    )
    tokens_all = devices * tokens.shape[0] * tokens.shape[1] * tokens.shape[2]
    results = list(
        run_update(
            tokens_all, head, out_half, out_other, input_half, input_other, grad, small, state
        )
    )
    for n, turn in zip((1, 3, 4, 6), turns):
        for k in range(2 + 3 * n, 5 + 3 * n):
            results[k] = results[k].transpose(turn)
    return tuple(results)


def solution(mesh):
    in_specs = (
        P("dp", None, None, None),
        P("dp", None, None, None),
        P("dp"),
        P("dp"),
        P(None, "dp", "head"),
        P(None, "dp", "head"),
        P(None, "dp", "head"),
        P("head", "dp"),
        P("head", "dp"),
        P("head", "dp"),
        P("dp", "head"),
        P("dp", "head"),
        P("dp", "head"),
        P("head", "dp"),
        P("head", "dp"),
        P("head", "dp"),
        P("dp", "head"),
        P("dp", "head"),
        P("dp", "head"),
        P(),
        P(),
        P(),
        P(None, None, "head"),
        P(None, None, "head"),
        P(None, None, "head"),
        P(None, "head"),
        P(None, "head"),
        P(None, "head"),
    )
    out_specs = (
        P("dp", None, None, None),
        P("dp", None, None, None),
        P(None, "dp", "head"),
        P(None, "dp", "head"),
        P(None, "dp", "head"),
        P("head", "dp"),
        P("head", "dp"),
        P("head", "dp"),
        P("dp", "head"),
        P("dp", "head"),
        P("dp", "head"),
        P("head", "dp"),
        P("head", "dp"),
        P("head", "dp"),
        P("dp", "head"),
        P("dp", "head"),
        P("dp", "head"),
        P(),
        P(),
        P(),
        P(None, None, "head"),
        P(None, None, "head"),
        P(None, None, "head"),
        P(None, "head"),
        P(None, "head"),
        P(None, "head"),
    )
    return jax.shard_map(
        per_device, mesh=mesh, in_specs=in_specs, out_specs=out_specs, check_vma=False
    )
```

```python
import math

import jax
import jax.numpy as jnp
import numpy as np
from jax import lax
from jax.experimental import pallas as pl
from jax.experimental.pallas import tpu as pltpu
from jax.sharding import PartitionSpec as P

BF = jnp.bfloat16
F32 = jnp.float32
EPSILON = 1e-06
HALF = 16
MASKED = -1e9
NN = (((1,), (0,)), ((), ()))
NT = (((1,), (1,)), ((), ()))
TN = (((0,), (0,)), ((), ()))
MESH = pl.DeviceIdType.MESH
SMALL = 64
PAIR = 2
LIMIT = 60 * 1024 * 1024
ROOT = math.sqrt(0.5)


def mm(a, b, dims=NN):
    return lax.dot_general(a, b, dims, preferred_element_type=F32)


def block_of(a4, b4):
    return (a4 % 2) * 8 + (b4 % 2) * 4 + (a4 // 2) * 2 + b4 // 2


def place_of(block):
    return ((block >> 1) & 1) * 2 + (block >> 3), (block & 1) * 2 + ((block >> 2) & 1)


def order_matrix():
    perm = np.zeros((256, 256), np.float32)
    for block in range(16):
        a4, b4 = place_of(block)
        for ci in range(4):
            for ck in range(4):
                perm[block * 16 + ci * 4 + ck, (4 * ci + a4) * HALF + 4 * ck + b4] = 1
    return perm


def cell_shifts():
    places = []
    for ci in range(4):
        for ck in range(4):
            places.append((0, ci, ck, ci // 2, ck // 2))
    for ah in range(2):
        for bh in range(2):
            for ci in range(4):
                for ck in range(4):
                    places.append((1, 2 * ci + ah, 2 * ck + bh, ci // 2, ck // 2))
    index = {p[:3]: n for n, p in enumerate(places)}
    shifts = np.zeros((2, 9, 80, 80), np.float32)
    for n, (g, i, k, si, sk) in enumerate(places):
        for tap in range(9):
            other = index.get((g, i + tap // 3 - 1, k + tap % 3 - 1))
            if other is not None:
                shifts[0, tap, n, other] = 1
                if places[other][3:] == (si, sk):
                    shifts[1, tap, n, other] = 1
    shifts = shifts.reshape(2, 720, 80)
    return np.concatenate([shifts, shifts], 2)


def score_bias():
    rows = np.array([(n % 16) for _ in range(2) for n in list(range(16)) + list(range(64))])
    cols = np.arange(256) % 16

    def image(n):
        return (n // 8) * 2 + (n % 4) // 2

    return np.where(image(rows)[:, None] == image(cols)[None, :], 0.0, MASKED).astype(np.float32)


def shift_masks():
    masks = np.zeros((2, 4, 16, 128), np.float32)
    for fine in range(2):
        for ci in range(4):
            for ck in range(4):
                row = ci * 4 + ck
                for n, (d, e) in enumerate(((1, 0), (-1, 0), (0, 1), (0, -1))):
                    ni, nk = ci + d, ck + e
                    ok = 0 <= ni < 4 and 0 <= nk < 4
                    if fine:
                        ok = ok and ni // 2 == ci // 2 and nk // 2 == ck // 2
                    masks[fine, n, row] = ok
    return masks


def normalise(x):
    centred = x - jnp.mean(x, -1, keepdims=True)
    scale = lax.rsqrt(jnp.mean(centred * centred, -1, keepdims=True) + EPSILON)
    return centred * scale, scale


def normalise_back(grad, unit, scale):
    return scale * (
        grad
        - jnp.mean(grad, -1, keepdims=True)
        - unit * jnp.mean(grad * unit, -1, keepdims=True)
    )


def gelu_pair(h):
    below = 0.5 + 0.5 * lax.erf(h * math.sqrt(0.5))
    density = jnp.exp2(h * h * (-0.5 * math.log2(math.e)))
    return h * below, below + h * density * (1.0 / math.sqrt(2 * math.pi))


def scaled_gelu_pair(u):
    below = math.sqrt(0.5) + math.sqrt(0.5) * lax.erf(u)
    density = jnp.exp2(u * u * (-math.log2(math.e)))
    return u * below, below + u * density * (2.0 / math.sqrt(2 * math.pi))


def block_kernel(
    resolution,
    live_images,
    head,
    tokens,
    cotangent,
    packed,
    filters,
    norms,
    perm,
    perm_t,
    shifts,
    bias,
    edge,
    out,
    input_grad,
    input_low,
    mine,
    theirs,
    small_mine,
    small_theirs,
    entry,
    mixing_t,
    expand,
    shrink_t,
    reduce_w,
    value_filter,
    hidden_filter,
    wide_s,
    square_s,
    d_entry,
    d_mixing_t,
    d_shrink_t,
    d_reduce_t,
    d_norm,
    d_value,
    conv_w,
    key_value_w,
    g_low,
    m_sum,
    folds,
    d_key_value,
    reduce_low,
    rows_in,
    rows_in_t,
    middle_s,
    up_s,
    unit1_s,
    scale1_s,
    unit2_s,
    scale2_s,
    normed_s,
    queries_s,
    mixed_s,
    probs,
    keys_s,
    enhanced_s,
    values_s,
    wide_cells,
    wide_scale,
    narrow_cells,
    narrow_scale,
    second_grad_s,
    factor_s,
    *,
    steps,
):
    step = pl.program_id(0)
    last = pl.num_programs(0) - 1
    first_grid = head[0] * steps
    devices = packed.shape[0] // 2
    width = 128 // devices
    ff = expand.shape[1]
    lane = lax.broadcasted_iota(jnp.int32, (128, 128), 1)
    first_lanes = lane % 64 < 32

    def left(rows):
        return lax.broadcasted_iota(jnp.int32, (rows, 128), 1) < 64

    @pl.when(step == 0)
    def prepare():
        top, chunk = 12 * width, ff // 256
        counts = jnp.zeros((1, 128), F32)
        last_rows = packed.shape[1] - 16
        for n in range(2 * devices):
            pair = packed[n, last_rows : last_rows + 16, :].astype(F32)
            counts = counts + (pair[:1] + 256.0 * pair[1:2])
        factor_s[...] = (devices * 2 * steps * 1024 / 64) / counts
        for d in range(devices):
            one, two = [packed[2 * d + h].astype(F32) for h in range(2)]
            mask = left(top)
            reduce_w[20 * width * d : 20 * width * d + top, :] = jnp.where(
                mask, one[:top], pltpu.roll(two[:top], 64, 1)
            )
            rest = jnp.where(mask, pltpu.roll(one[:top], 64, 1), two[:top])
            reduce_w[20 * width * d + top : 20 * width * (d + 1), :] = rest[: 8 * width]
            rows = slice(width * d, width * d + width)
            for e in range(4):
                square_s[e, rows, :] = rest[(8 + e) * width : (9 + e) * width]
            for h, part in enumerate((one, two)):
                for u in range(chunk):
                    cols = slice((h * chunk + u) * 128, (h * chunk + u + 1) * 128)
                    wide_s[0, rows, cols] = part[top + u * width : top + (u + 1) * width]
                    wide_s[1, rows, cols] = part[
                        top + (chunk + u) * width : top + (chunk + u + 1) * width
                    ]
        reduce_low[...] = reduce_w[...].astype(BF)
        entry[...] = square_s[:3].astype(BF)
        mixing_t[...] = square_s[3].astype(BF)
        expand[...] = wide_s[0]
        shrink_t[...] = wide_s[1].astype(BF)
        for h in range(2):
            hidden_filter[:, h * (ff // 2) : (h + 1) * (ff // 2)] = filters[h, :9, : ff // 2]
        value_filter[...] = jnp.where(
            left(9),
            filters[0, :9, ff // 2 :],
            pltpu.roll(filters[1, :9, ff // 2 :], 64, 1),
        )
        for column in range(3):
            top, mid, low = [
                hidden_filter[3 * a + column : 3 * a + column + 1, :] * ROOT for a in range(3)
            ]
            if column == 1:
                mid = mid + ROOT
            rows = slice(column * 128, column * 128 + 128)
            for n, gain in enumerate(
                (top, 0.5 * (top + mid + low), 0.5 * (top - mid + low), low)
            ):
                conv_w[n, rows, :] = (expand[...] * gain).astype(BF)
        for g in range(2):
            w = entry[1 + g].astype(F32)
            if g == 0:
                keys, vals = w, pltpu.roll(w, 96, 1)
                keep = first_lanes
            else:
                keys, vals = pltpu.roll(w, 32, 1), w
                keep = jnp.logical_not(first_lanes)
            key_value_w[g, :, :128] = jnp.where(keep, keys, 0.0).astype(BF)
            key_value_w[g, :, 128:] = jnp.where(keep, vals, 0.0).astype(BF)
        for ref in (d_entry, d_mixing_t, d_shrink_t, d_reduce_t, d_norm, d_value, m_sum, d_key_value):
            ref[...] = jnp.zeros_like(ref)

    def ordered(ref, place):
        parts = [
            ref[place, a * 16 : a * 16 + 16, b * 16 : b * 16 + 16, :].reshape(256, 128)
            for a in range(2)
            for b in range(2)
        ]
        rows = mm(perm[...], jnp.concatenate(parts, 1))
        return jnp.stack(
            [rows[:, q * 128 : q * 128 + 128].reshape(16, 16, 128) for q in range(4)], 1
        ).reshape(1024, 128)

    def restore(value, ref, place, wide=None):
        blocks = value.reshape(16, 4, 16, 128)
        rows = mm(
            perm_t[...],
            jnp.concatenate([blocks[:, q].reshape(256, 128) for q in range(4)], 1),
        )
        for q in range(4):
            a, b = q // 2, q % 2
            index = (pl.ds(place, 1), slice(a * 16, a * 16 + 16), slice(b * 16, b * 16 + 16))
            part = rows[:, q * 128 : q * 128 + 128]
            ref[index] = part.astype(BF).reshape(1, 16, 16, 128)
            if wide is not None:
                wide[index] = (part * factor_s[...]).reshape(1, 16, 16, 128)

    def of_quadrant(value, q, blocks):
        return value.reshape(blocks, 4, 16, 128)[:, q].reshape(blocks * 16, 128)

    def of_quadrants(parts, blocks):
        return jnp.stack([p.reshape(blocks, 16, 128) for p in parts], 1).reshape(
            blocks * 64, 128
        )

    def gain(n):
        return norms[0, n : n + 1, :]

    def shift_by(n):
        return norms[1, n : n + 1, :]

    def add_norm(n, grad, unit):
        d_norm[n : n + 1, :] += jnp.sum(grad * unit, 0, keepdims=True)
        d_norm[4 + n : 5 + n, :] += jnp.sum(grad, 0, keepdims=True)

    lane80 = lax.broadcasted_iota(jnp.int32, (80, 128), 1)
    zero80 = jnp.zeros((80, 128), BF)
    segments = ((0, 16), (16, 80), (80, 96), (96, 160))
    scaling = 32**-0.5
    rows_of = (slice(0, 2048), slice(2048, 2560))
    cells_f = (wide_cells, narrow_cells)
    cells_scale = (wide_scale, narrow_scale)

    def fine_of(grid):
        return (resolution[first_grid + grid] == 8).astype(jnp.int32)

    def patches_of(slot, g):
        if g == 0:
            blocks = [block_of(t // 4, t % 4) for t in range(16)]
            parts = [normed_s[slot, b * 64 : b * 64 + 64, :] for b in blocks]
        else:
            parts = [normed_s[slot, t * 256 : t * 256 + 256, :] for t in range(4)]
        return jnp.concatenate(parts, 1)

    def move(value, fine, rows, columns):
        size = value.shape[0]
        if rows:
            n = 0 if rows > 0 else 1
            value = pltpu.roll(value, (-4 * rows) % size, 0)
            value = (
                value.reshape(size // 16, 16, 128) * edge[pl.ds(fine, 1), n : n + 1][0]
            ).reshape(size, 128)
        if columns:
            n = 2 if columns > 0 else 3
            value = pltpu.roll(value, (-columns) % size, 0)
            value = (
                value.reshape(size // 16, 16, 128) * edge[pl.ds(fine, 1), n : n + 1][0]
            ).reshape(size, 128)
        return value

    def wrap(a4, d):
        return (a4 + d) % 4, (a4 + d) // 4

    def attend(slot, grid):
        fine = fine_of(grid)
        alive = live_images[first_grid + grid]
        x = ordered(tokens, slot)
        yield
        raised = ordered(cotangent, slot)
        yield
        unit1, scale1 = normalise(x)
        unit1_s[slot] = unit1
        scale1_s[slot] = scale1
        yield
        normed = (unit1 * gain(0) + shift_by(0)).astype(BF)
        normed_s[slot] = normed
        yield
        reduced = [mm(patches_of(slot, g), reduce_low[rows_of[g], :]) for g in range(2)]
        yield
        queries_s[slot] = mm(normed, entry[0]).astype(BF)
        yield
        cells = [normalise(reduced[g]) for g in range(2)]
        yield
        row16 = lax.broadcasted_iota(jnp.int32, (16, 128), 0)
        within = (row16 // 8) * 4 + (row16 % 4) // 2
        live = jnp.stack(
            [
                jnp.where(
                    jnp.where(fine == 1, within + (q // 2) * 8 + (q % 2) * 2, q) < alive, 1.0, 0.0
                )
                for q in range(4)
            ],
            0,
        )
        up_s[slot] = (raised.reshape(16, 4, 16, 128) * live[None]).reshape(1024, 128).astype(BF)
        yield
        acts = []
        for g in range(2):
            unit, scale = cells[g]
            act, slope = gelu_pair(unit * gain(1 + g) + shift_by(1 + g))
            cells_f[g][slot, 0] = unit
            cells_f[g][slot, 1] = slope
            cells_f[g][slot, 2] = act
            cells_scale[g][slot] = scale
            acts.append(act.astype(BF))
        yield
        pairs = [mm(acts[g], key_value_w[g]) for g in range(2)]
        yield
        keys = [pair[:, :128].astype(BF) for pair in pairs]
        values = [pair[:, 128:] for pair in pairs]
        keys_all = [
            jnp.concatenate([keys[0][q * 16 : q * 16 + 16], of_quadrant(keys[1], q, 4)], 0)
            for q in range(4)
        ]
        values_all = jnp.concatenate(
            [
                jnp.concatenate(
                    [values[0][q * 16 : q * 16 + 16], of_quadrant(values[1], q, 4)], 0
                )
                for q in range(4)
            ],
            1,
        )
        values_s[slot] = values_all
        moves = shifts[pl.ds(fine, 1)][0]
        high = values_all.astype(BF)
        rest = (values_all - high.astype(F32)).astype(BF)
        moved = mm(moves, jnp.concatenate([high, rest], 0))
        taps4 = jnp.concatenate([value_filter[...]] * 4, 1)
        enhanced = values_all
        for tap in range(9):
            enhanced = enhanced + moved[tap * 80 : tap * 80 + 80] * taps4[tap : tap + 1]
        enhanced = enhanced.astype(BF)
        yield

        def both_heads(rows):
            return jnp.concatenate(
                [jnp.where(lane80 < 64, rows, zero80), jnp.where(lane80 < 64, zero80, rows)], 0
            )

        queries = queries_s[slot]
        scores = []
        for q in range(4):
            keys_s[slot, q] = both_heads(keys_all[q])
            enhanced_s[slot, q] = both_heads(enhanced[:, q * 128 : q * 128 + 128])
            scores.append(mm(keys_s[slot, q], of_quadrant(queries, q, 16), NT))
        yield
        for q in range(4):
            biased = scores[q] * scaling + fine.astype(F32) * bias[...]
            for lo, hi in segments:
                part = biased[lo:hi]
                part = jnp.exp(part - jnp.max(part, 0, keepdims=True))
                probs[slot, q, lo:hi, :] = part * (1.0 / jnp.sum(part, 0, keepdims=True))
        yield
        mixed_parts = [
            mm(probs[slot, q].astype(BF), enhanced_s[slot, q], TN) for q in range(4)
        ]
        yield
        mixed = of_quadrants(mixed_parts, 16).astype(BF)
        mixed_s[slot] = mixed
        middle = x + mm(mixed, mixing_t[...], NT)
        middle_s[slot] = middle
        yield
        unit2, scale2 = normalise(middle)
        unit2_s[slot] = unit2
        scale2_s[slot] = scale2
        second_low = (unit2 * gain(3) + shift_by(3)).astype(BF)
        second_f = second_low.astype(F32)
        yield
        moved_blocks = {}

        def neighbour(block, down, across):
            a4, b4 = place_of(block)
            na, wa = wrap(a4, down)
            nb, wb = wrap(b4, across)
            key = (block_of(na, nb), wa, wb)
            if key not in moved_blocks:
                rows = second_f[key[0] * 64 : key[0] * 64 + 64]
                moved_blocks[key] = move(rows, fine, wa, wb) if wa or wb else rows
            return moved_blocks[key]

        for block in range(8):
            for column in range(3):
                above, first, second = [neighbour(block, d, column - 1) for d in (-1, 0, 1)]
                below = neighbour(block + 8, 1, column - 1)
                for n, part in enumerate(
                    (above - second, first + second, second - first, below - first)
                ):
                    rows_in[
                        slot, n, block * 64 : block * 64 + 64, column * 128 : column * 128 + 128
                    ] = part.astype(BF)
            yield
    def feed(slot, grid):
        fine = fine_of(grid)
        total = middle_s[slot]
        wide = 256
        held = None
        for c in range(0, ff + wide, wide):
            if c < ff:
                cols = slice(c, c + wide)
                m = [mm(rows_in[slot, n], conv_w[n, :, cols]) for n in range(4)]
                inner = m[1] + m[0]
                hidden = (inner + m[2], m[1] - m[2] + m[3])
                grads = [
                    mm(up_s[slot, h * 512 : h * 512 + 512, :], shrink_t[:, cols]) for h in range(2)
                ]
            if c == 0:
                for n in range(4):
                    for column in range(3):
                        rows = slice(column * 128, column * 128 + 128)
                        rows_in_t[n, rows, :] = rows_in[slot, n, :, rows].T
                up_t = up_s[slot].T
            if held:
                before, act, backs = held
                total = total + mm(act, shrink_t[:, before], NT)
                d_shrink_t[:, before] += mm(up_t, act)
                for n in range(4):
                    m_sum[n, :, before] += mm(rows_in_t[n], backs[n])
            if c < ff:
                acts, gs = [], []
                for h in range(2):
                    act, slope = scaled_gelu_pair(hidden[h])
                    acts.append(act.astype(BF))
                    gs.append(grads[h] * slope)
                act = jnp.concatenate(acts, 0)
                backs = [
                    v.astype(BF) for v in (gs[0], gs[0] + gs[1], gs[0] - gs[1], gs[1])
                ]
                for n in range(4):
                    g_low[n, :, cols] = backs[n]
                held = (cols, act, backs)
        restore(total.astype(BF), out, slot)
        for n in range(4):
            folds[n] = mm(g_low[n], conv_w[n], NT)
        sums = {}
        for block in range(8):
            for column in range(3):
                for down, other, terms in (
                    (-1, block, ((0, 1),)),
                    (0, block, ((1, 1), (2, -1), (3, -1))),
                    (1, block, ((1, 1), (2, 1), (0, -1))),
                    (1, block + 8, ((3, 1),)),
                ):
                    a4, b4 = place_of(other)
                    na, wa = wrap(a4, down)
                    nb, wb = wrap(b4, column - 1)
                    key = (block_of(na, nb), wa, wb)
                    sums.setdefault(key, []).extend((block, column, n, sign) for n, sign in terms)
        for block in range(16):
            total = None
            for (source, wa, wb), terms in sums.items():
                if source != block:
                    continue
                part = None
                for other, column, n, sign in terms:
                    term = folds[
                        n, other * 64 : other * 64 + 64, column * 128 : column * 128 + 128
                    ]
                    if part is None:
                        part = term if sign > 0 else -term
                    else:
                        part = part + term if sign > 0 else part - term
                if wa or wb:
                    part = move(part, fine, -wa, -wb)
                total = part if total is None else total + part
            second_grad_s[slot, block * 64 : block * 64 + 64, :] = total

    def back(slot, grid):
        fine = fine_of(grid)
        second_grad = second_grad_s[slot]
        unit2 = unit2_s[slot]
        add_norm(3, second_grad, unit2)
        middle_grad = up_s[slot].astype(F32) + normalise_back(
            second_grad * gain(3), unit2, scale2_s[slot]
        )
        middle_low = middle_grad.astype(BF)
        yield
        mixed_grad = mm(middle_low, mixing_t[...]).astype(BF)
        queries = queries_s[slot]
        yield
        d_mixing_t[...] += mm(middle_low, mixed_s[slot], TN)
        yield
        out_grads = [of_quadrant(mixed_grad, q, 16) for q in range(4)]
        prob_grads = [mm(enhanced_s[slot, q], out_grads[q], NT) for q in range(4)]
        yield
        enhanced_parts = []
        for q in range(4):
            full = mm(probs[slot, q].astype(BF), out_grads[q])
            enhanced_parts.append(jnp.where(lane80 < 64, full[:80], full[80:]).astype(BF))
        yield
        score_lows = []
        for q in range(4):
            weights = probs[slot, q]
            product = weights * prob_grads[q]
            score_grad = []
            for lo, hi in segments:
                score_grad.append(
                    product[lo:hi] - weights[lo:hi] * jnp.sum(product[lo:hi], 0, keepdims=True)
                )
            score_lows.append((scaling * jnp.concatenate(score_grad, 0)).astype(BF))
        yield
        query_parts = [mm(score_lows[q], keys_s[slot, q], TN) for q in range(4)]
        yield
        key_parts = []
        for q in range(4):
            full = mm(score_lows[q], of_quadrant(queries, q, 16))
            key_parts.append(jnp.where(lane80 < 64, full[:80], full[80:]).astype(BF))
        yield
        query_low = of_quadrants(query_parts, 16).astype(BF)
        enhanced_grad = jnp.concatenate(enhanced_parts, 1)
        moved = mm(shifts[pl.ds(fine, 1)][0][:, :80], enhanced_grad)
        taps4 = jnp.concatenate([value_filter[...]] * 4, 1)
        value_grad = enhanced_grad.astype(F32)
        values_all = values_s[slot]
        for tap in range(9):
            part = moved[(8 - tap) * 80 : (8 - tap) * 80 + 80]
            value_grad = value_grad + part * taps4[tap : tap + 1]
            row = jnp.sum(part * values_all, 0, keepdims=True)
            d_value[tap : tap + 1, :] += (
                row[:, :128] + row[:, 128:256] + row[:, 256:384] + row[:, 384:]
            )
        value_grad = value_grad.astype(BF)
        value_parts = [value_grad[:, q * 128 : q * 128 + 128] for q in range(4)]
        yield
        narrow = [jnp.concatenate([p[:16] for p in parts], 0) for parts in (key_parts, value_parts)]
        wide = [of_quadrants([p[16:] for p in parts], 4) for parts in (key_parts, value_parts)]
        pairs = [jnp.concatenate(sides, 1) for sides in (narrow, wide)]
        cell_grads = [mm(pairs[g], key_value_w[g], NT) for g in range(2)]
        yield
        normed_grad = mm(query_low, entry[0], NT)
        yield
        reduced_lows = []
        for g in range(2):
            unit, slope = cells_f[g][slot, 0], cells_f[g][slot, 1]
            cell_grad = cell_grads[g] * slope
            add_norm(1 + g, cell_grad, unit)
            reduced_lows.append(
                normalise_back(cell_grad * gain(1 + g), unit, cells_scale[g][slot]).astype(BF)
            )
        yield
        d_entry[0] += mm(normed_s[slot], query_low, TN)
        yield
        spreads = [mm(reduced_lows[g], reduce_low[rows_of[g], :], NT) for g in range(2)]
        yield
        for g in range(2):
            d_key_value[g] += mm(cells_f[g][slot, 2].astype(BF), pairs[g], TN)
        yield
        for g in range(2):
            if g == 0:
                order = [place_of(block) for block in range(16)]
                order = [a4 * 4 + b4 for a4, b4 in order]
            else:
                order = range(4)
            normed_grad = normed_grad + jnp.concatenate(
                [spreads[g][:, t * 128 : t * 128 + 128] for t in order], 0
            )
        yield
        for g in range(2):
            d_reduce_t[:, rows_of[g]] += mm(reduced_lows[g], patches_of(slot, g), TN)
        yield
        unit1 = unit1_s[slot]
        add_norm(0, normed_grad, unit1)
        raw = middle_grad + normalise_back(normed_grad * gain(0), unit1, scale1_s[slot])
        restore(raw.astype(BF), input_low, slot, input_grad)
        yield

    def together(*parts):
        parts = list(parts)
        while parts:
            parts = [part for part in parts if next(part, parts) is not parts]

    first = PAIR * step
    together(*[attend(k, first + k) for k in range(PAIR)])

    def feed_one(k, carry):
        feed(k, first + k)
        return carry

    lax.fori_loop(0, PAIR, feed_one, 0)
    together(*[back(k, first + k) for k in range(PAIR)])

    @pl.when(step == last)
    def finish():
        gains = [hidden_filter[tap : tap + 1, :] * ROOT for tap in range(9)]
        gains[4] = gains[4] + ROOT
        for c in range(0, ff, 128):
            cols = slice(c, c + 128)
            taps = [None] * 9
            for r in range(0, 128, 64):
                weight = expand[r : r + 64, cols]
                total = None
                for column in range(3):
                    rows = slice(column * 128 + r, column * 128 + r + 64)
                    one, two = m_sum[1, rows, cols], m_sum[2, rows, cols]
                    both = (one + two) * 0.5
                    for a in range(3):
                        if a == 1:
                            part = (one - two) * 0.5
                        else:
                            part = m_sum[a // 2 * 3, rows, cols] + both
                        tap = 3 * a + column
                        row = jnp.sum(part * weight, 0, keepdims=True)
                        taps[tap] = row if taps[tap] is None else taps[tap] + row
                        part = part * gains[tap][:, cols]
                        total = part if total is None else total + part
                wide_s[0, r : r + 64, cols] = total
            for tap in range(9):
                hidden_filter[tap : tap + 1, cols] = taps[tap] * ROOT
        wide_s[1] = d_shrink_t[...]
        d_entry[1] = jnp.where(
            first_lanes, d_key_value[0, :, :128], pltpu.roll(d_key_value[0, :, 128:], 32, 1)
        )
        d_entry[2] = jnp.where(
            first_lanes, pltpu.roll(d_key_value[1, :, :128], 96, 1), d_key_value[1, :, 128:]
        )
        is_second = head[0] == 1
        d_reduce = reduce_w
        for n in range(20):
            rows = slice(n * 128, n * 128 + 128)
            d_reduce[rows, :] = d_reduce_t[:, rows].T
        top, chunk = 12 * width, ff // 256
        planes = mine.shape[1]

        def put(d, rows, first, second):
            place = (d // planes, d % planes, rows)
            mine[place] = jnp.where(is_second, second, first)
            theirs[place] = jnp.where(is_second, first, second).astype(BF)

        for d in range(devices):
            rows = slice(width * d, width * d + width)
            upper = d_reduce[20 * width * d : 20 * width * d + top, :]
            lower = jnp.concatenate(
                [d_reduce[20 * width * d + top : 20 * width * (d + 1), :]]
                + [d_entry[e, rows, :] for e in range(3)]
                + [d_mixing_t[rows, :]],
                0,
            )
            firsts = [jnp.where(left(top), upper, pltpu.roll(lower, 64, 1))]
            seconds = [jnp.where(left(top), pltpu.roll(upper, 64, 1), lower)]
            for n in range(2):
                for h, parts in enumerate((firsts, seconds)):
                    for u in range(chunk):
                        cols = slice((h * chunk + u) * 128, (h * chunk + u + 1) * 128)
                        parts.append(wide_s[n, rows, cols])
            pad = mine.shape[2] - 20 * width
            if pad:
                firsts.append(jnp.zeros((pad, 128), F32))
                seconds.append(jnp.zeros((pad, 128), F32))
            put(d, slice(None), jnp.concatenate(firsts, 0), jnp.concatenate(seconds, 0))
        count = jnp.int32(0)
        for n in range(steps):
            side = resolution[head[0] * steps + n]
            count = count + side * side * live_images[head[0] * steps + n]
        halves = [
            jnp.concatenate(
                [
                    hidden_filter[:, (h * chunk + u) * 128 : (h * chunk + u + 1) * 128]
                    for u in range(chunk)
                ],
                0,
            )
            for h in range(2)
        ]
        for ref, flip in ((small_mine, False), (small_theirs, True)):
            ref[...] = jnp.zeros_like(ref)
            ref[:8, :] = d_norm[...]
            ref[8:17, :] = d_value[...]
            ref[17:18, :] = jnp.full((1, 128), count, jnp.int32).astype(F32)
            second = jnp.logical_not(is_second) if flip else is_second
            ref[18 : 18 + 9 * chunk, :] = jnp.where(second, halves[1], halves[0])


def run_block(resolution, live_images, head, tokens, cotangent, packed, filters, norms):
    steps = tokens.shape[0] // 2
    devices, rows = packed.shape[0] // 2, packed.shape[1] - 16
    ff = 2 * (filters.shape[2] - 128)
    lines = line_of(devices)
    consts = [
        jnp.asarray(order_matrix(), BF),
        jnp.asarray(order_matrix().T, BF),
        jnp.asarray(cell_shifts(), BF),
        jnp.asarray(score_bias(), F32),
        jnp.asarray(shift_masks(), F32),
    ]
    whole = [packed, filters, norms] + consts

    def all_of(a):
        return pl.BlockSpec(a.shape, lambda i, *_, n=a.ndim: (0,) * n)

    grid_in = pl.BlockSpec(
        (PAIR, 32, 32, 128), lambda i, res, live, head: (head[0] * (steps // PAIR) + i, 0, 0, 0)
    )
    grid_out = pl.BlockSpec((PAIR, 32, 32, 128), lambda i, *_: (i, 0, 0, 0))
    out_shape = [
        jax.ShapeDtypeStruct((2 * steps, 32, 32, 128), BF),
        jax.ShapeDtypeStruct((2 * steps, 32, 32, 128), F32),
        jax.ShapeDtypeStruct((steps, 32, 32, 128), BF),
        jax.ShapeDtypeStruct((lines, devices // lines, rows, 128), F32),
        jax.ShapeDtypeStruct((lines, devices // lines, rows, 128), BF),
        jax.ShapeDtypeStruct((SMALL, 128), F32),
        jax.ShapeDtypeStruct((SMALL, 128), F32),
    ]

    def kernel(*refs):
        block_kernel(*refs, steps=steps)

    return pl.pallas_call(
        kernel,
        out_shape=out_shape,
        grid_spec=pltpu.PrefetchScalarGridSpec(
            num_scalar_prefetch=3,
            grid=(steps // PAIR,),
            in_specs=[grid_in, grid_in] + [all_of(a) for a in whole],
            out_specs=[grid_in, grid_in, grid_out] + [all_of(a) for a in out_shape[3:]],
            scratch_shapes=[
                pltpu.VMEM((3, 128, 128), BF),
                pltpu.VMEM((128, 128), BF),
                pltpu.VMEM((128, ff), F32),
                pltpu.VMEM((128, ff), BF),
                pltpu.VMEM((2560, 128), F32),
                pltpu.VMEM((9, 128), F32),
                pltpu.VMEM((9, ff), F32),
                pltpu.VMEM((2, 128, ff), F32),
                pltpu.VMEM((4, 128, 128), F32),
                pltpu.VMEM((3, 128, 128), F32),
                pltpu.VMEM((128, 128), F32),
                pltpu.VMEM((128, ff), F32),
                pltpu.VMEM((128, 2560), F32),
                pltpu.VMEM((8, 128), F32),
                pltpu.VMEM((9, 128), F32),
                pltpu.VMEM((4, 384, ff), BF),
                pltpu.VMEM((2, 128, 256), BF),
                pltpu.VMEM((4, 512, ff), BF),
                pltpu.VMEM((4, 384, ff), F32),
                pltpu.VMEM((4, 512, 384), F32),
                pltpu.VMEM((2, 128, 256), F32),
                pltpu.VMEM((2560, 128), BF),
                pltpu.VMEM((2, 4, 512, 384), BF),
                pltpu.VMEM((4, 384, 512), BF),
                pltpu.VMEM((2, 1024, 128), F32),
                pltpu.VMEM((2, 1024, 128), BF),
                pltpu.VMEM((2, 1024, 128), F32),
                pltpu.VMEM((2, 1024, 1), F32),
                pltpu.VMEM((2, 1024, 128), F32),
                pltpu.VMEM((2, 1024, 1), F32),
                pltpu.VMEM((2, 1024, 128), BF),
                pltpu.VMEM((2, 1024, 128), BF),
                pltpu.VMEM((2, 1024, 128), BF),
                pltpu.VMEM((2, 4, 160, 256), F32),
                pltpu.VMEM((2, 4, 160, 128), BF),
                pltpu.VMEM((2, 4, 160, 128), BF),
                pltpu.VMEM((2, 80, 512), F32),
                pltpu.VMEM((2, 3, 64, 128), F32),
                pltpu.VMEM((2, 64, 1), F32),
                pltpu.VMEM((2, 3, 256, 128), F32),
                pltpu.VMEM((2, 256, 1), F32),
                pltpu.VMEM((2, 1024, 128), F32),
                pltpu.VMEM((1, 128), F32),
            ],
        ),
        compiler_params=pltpu.CompilerParams(
            dimension_semantics=("arbitrary",), vmem_limit_bytes=LIMIT
        ),
        name="block",
    )(resolution, live_images, head, tokens, cotangent, *whole)


def line_of(devices):
    return 4 if devices % 4 == 0 else 1


def rows_of_block(devices):
    return -(-20 * (128 // devices) // 16) * 16


def pack_kernel(resolution, live_images, head, entry, mixing_t, expand, shrink_t, reduce_t, values, hidden, block, filters, held):
    width, ff = expand.shape
    top, chunk = 12 * width, ff // 128
    held[...] = jnp.zeros_like(held)
    rows = reduce_t[...].T
    held[:top, :64] = rows[:top, :]
    held[: 8 * width, 64:] = rows[top:, :]
    for e in range(3):
        held[(8 + e) * width : (9 + e) * width, 64:] = entry[e]
    held[11 * width : top, 64:] = mixing_t[...]
    for u in range(chunk):
        cols = slice(u * 128, (u + 1) * 128)
        held[top + u * width : top + (u + 1) * width, :] = expand[:, cols]
        held[top + (chunk + u) * width : top + (chunk + u + 1) * width, :] = shrink_t[:, cols]
    half = live_images.shape[0] // 2
    count = jnp.int32(0)
    for n in range(half):
        side = resolution[head[0] * half + n]
        count = count + side * side * live_images[head[0] * half + n]
    count = count // 64
    last = held.shape[0] - 16
    held[last : last + 1, :] = jnp.full((1, 128), count % 256, jnp.int32).astype(F32)
    held[last + 1 : last + 2, :] = jnp.full((1, 128), count // 256, jnp.int32).astype(F32)
    block[...] = held[...].astype(BF)
    filters[...] = jnp.zeros_like(filters)
    filters[:9, :ff] = hidden[...]
    for g in range(2):
        filters[:9, ff + 32 * g : ff + 32 * g + 32] = values[:, g]


def run_pack(
    devices, resolution, live_images, head, entry, mixing_t, expand, shrink_t, reduce_t, values, hidden
):
    rows = rows_of_block(devices) + 16
    smem = pl.BlockSpec(memory_space=pltpu.SMEM)
    vmem = pl.BlockSpec(memory_space=pltpu.VMEM)
    return pl.pallas_call(
        pack_kernel,
        out_shape=[
            jax.ShapeDtypeStruct((rows, 128), BF),
            jax.ShapeDtypeStruct((16, hidden.shape[1] + 128), F32),
        ],
        in_specs=[smem] * 3 + [vmem] * 7,
        out_specs=[vmem] * 2,
        scratch_shapes=[pltpu.VMEM((rows, 128), F32)],
        compiler_params=pltpu.CompilerParams(vmem_limit_bytes=LIMIT),
        name="pack",
    )(resolution, live_images, head, entry, mixing_t, expand, shrink_t, reduce_t, values, hidden)


def greet(peers):
    barrier = pltpu.get_barrier_semaphore()
    for peer in peers:
        pl.semaphore_signal(barrier, inc=1, device_id=peer, device_id_type=MESH)
    pl.semaphore_wait(barrier, len(peers))


def places(devices):
    lines = line_of(devices)
    planes = devices // lines
    me, head = lax.axis_index("dp"), lax.axis_index("head")
    z, p = me // planes, me % planes
    line_peers = [((z + k) % lines) for k in range(1, lines)]
    plane_peers = [((p + k) % planes) for k in range(1, planes)]
    return lines, planes, z, p, head, line_peers, plane_peers


def gather_kernel(devices, block, filters, blocks, both, send_sem, recv_sem, filter_sem, local_sem):
    lines, planes, z, p, head, line_peers, plane_peers = places(devices)

    def slot(line, plane, core):
        return (line * planes + plane) * 2 + core

    def at(line, plane, core):
        return (line * planes + plane, core)

    sibling = at(z, p, 1 - head)
    greet(
        [at(k, p, head) for k in line_peers] + [at(z, k, head) for k in plane_peers] + [sibling]
    )
    sends = []

    def send(source, index, target):
        copy = pltpu.make_async_remote_copy(
            src_ref=source,
            dst_ref=blocks.at[index],
            send_sem=send_sem.at[len(sends)],
            recv_sem=recv_sem.at[index],
            device_id=target,
            device_id_type=MESH,
        )
        copy.start()
        sends.append(copy)

    def arrived(index):
        pltpu.make_async_remote_copy(
            src_ref=block,
            dst_ref=blocks.at[index],
            send_sem=send_sem.at[0],
            recv_sem=recv_sem.at[index],
            device_id=sibling,
            device_id_type=MESH,
        ).wait_recv()

    own = slot(z, p, head)
    for k in line_peers:
        send(block, own, at(k, p, head))
    for k in plane_peers:
        send(block, own, at(z, k, head))
    send(block, own, sibling)
    swap = pltpu.make_async_remote_copy(
        src_ref=filters,
        dst_ref=both.at[head],
        send_sem=filter_sem.at[0],
        recv_sem=filter_sem.at[1],
        device_id=sibling,
        device_id_type=MESH,
    )
    swap.start()
    keep = [
        pltpu.make_async_copy(block, blocks.at[own], local_sem.at[0]),
        pltpu.make_async_copy(filters, both.at[head], local_sem.at[1]),
    ]
    for copy in keep:
        copy.start()
    for k in line_peers:
        index = slot(k, p, head)
        arrived(index)
        for j in plane_peers:
            send(blocks.at[index], index, at(z, j, head))
        send(blocks.at[index], index, sibling)
    for line in [z] + line_peers:
        for j in plane_peers:
            index = slot(line, j, head)
            arrived(index)
            send(blocks.at[index], index, sibling)
    for line in [z] + line_peers:
        for j in [p] + plane_peers:
            arrived(slot(line, j, 1 - head))
    for copy in sends:
        copy.wait_send()
    swap.wait_send()
    pltpu.make_async_remote_copy(
        src_ref=filters,
        dst_ref=both.at[1 - head],
        send_sem=filter_sem.at[0],
        recv_sem=filter_sem.at[1],
        device_id=sibling,
        device_id_type=MESH,
    ).wait_recv()
    for copy in keep:
        copy.wait()


def run_gather(devices, block, filters):
    lines = line_of(devices)
    planes = devices // lines
    copies = (lines - 1) + lines * (planes - 1) + lines * planes
    anywhere = pl.BlockSpec(memory_space=pl.ANY)

    def kernel(*refs):
        gather_kernel(devices, *refs)

    return pl.pallas_call(
        kernel,
        out_shape=[
            jax.ShapeDtypeStruct((2 * devices,) + block.shape, BF),
            jax.ShapeDtypeStruct((2,) + filters.shape, F32),
        ],
        in_specs=[anywhere, anywhere],
        out_specs=[anywhere, anywhere],
        scratch_shapes=[
            pltpu.SemaphoreType.DMA((copies,)),
            pltpu.SemaphoreType.DMA((2 * devices,)),
            pltpu.SemaphoreType.DMA((2,)),
            pltpu.SemaphoreType.DMA((2,)),
        ],
        compiler_params=pltpu.CompilerParams(collective_id=0, has_side_effects=True),
        name="gather",
    )(block, filters)


def reduce_kernel(
    devices,
    mine,
    theirs,
    small_mine,
    small_theirs,
    out_half,
    input_half,
    grad,
    small,
    out_other,
    input_other,
    core_in,
    core_small,
    plane_out,
    plane_in,
    plane_small,
    line_out,
    line_in,
    line_small,
    core_send,
    core_recv,
    plane_send,
    plane_recv,
    line_send,
    line_recv,
):
    lines, planes, z, p, head, line_peers, plane_peers = places(devices)
    half = input_half.shape[0]

    def at(line, plane, core):
        return (line * planes + plane, core)

    sibling = at(z, p, 1 - head)
    greet(
        [at(k, p, head) for k in line_peers] + [at(z, k, head) for k in plane_peers] + [sibling]
    )

    def remote(source, target, send, recv, device):
        return pltpu.make_async_remote_copy(
            src_ref=source,
            dst_ref=target,
            send_sem=send,
            recv_sem=recv,
            device_id=device,
            device_id_type=MESH,
        )

    started = []

    def go(*args):
        copy = remote(*args)
        copy.start()
        started.append(copy)

    order = line_peers + [z]
    go(small_theirs, core_small, core_send.at[lines], core_recv.at[lines], sibling)
    for a in order:
        go(theirs.at[a], core_in.at[a], core_send.at[a], core_recv.at[a], sibling)
    remote(
        small_theirs, core_small, core_send.at[lines], core_recv.at[lines], sibling
    ).wait_recv()
    plane_small[pl.ds(p, 1)] = (small_mine[...] + core_small[...])[None]
    for n, k in enumerate(plane_peers):
        go(
            plane_small.at[p],
            plane_small.at[p],
            plane_send.at[lines * (planes - 1) + n],
            plane_recv.at[lines * planes + p],
            at(z, k, head),
        )
    for m, a in enumerate(order):
        remote(
            theirs.at[a], core_in.at[a], core_send.at[a], core_recv.at[a], sibling
        ).wait_recv()
        both = mine[pl.ds(a, 1)] + core_in[pl.ds(a, 1)].astype(F32)
        plane_out[pl.ds(a, 1)] = both.astype(BF)
        for n, k in enumerate(plane_peers):
            go(
                plane_out.at[a, k],
                plane_in.at[a, p],
                plane_send.at[m * (planes - 1) + n],
                plane_recv.at[a * planes + p],
                at(z, k, head),
            )
    own_out = out_half.at[pl.ds(head * half, half)]
    go(own_out, out_other, core_send.at[lines + 1], core_recv.at[lines + 1], sibling)
    go(input_half, input_other, core_send.at[lines + 2], core_recv.at[lines + 2], sibling)
    for k in plane_peers:
        remote(
            plane_small.at[p],
            plane_small.at[k],
            plane_send.at[0],
            plane_recv.at[lines * planes + k],
            sibling,
        ).wait_recv()
    part = plane_small[0]
    for k in range(1, planes):
        part = part + plane_small[k]
    line_small[pl.ds(z, 1)] = part[None]
    for n, k in enumerate(line_peers):
        go(
            line_small.at[z],
            line_small.at[z],
            line_send.at[lines + n],
            line_recv.at[lines + z],
            at(k, p, head),
        )
    own = None
    for m, a in enumerate(order):
        total = (
            mine[pl.ds(a, 1), pl.ds(p, 1)] + core_in[pl.ds(a, 1), pl.ds(p, 1)].astype(F32)
        )[0, 0]
        for k in plane_peers:
            remote(
                plane_out.at[a, k],
                plane_in.at[a, k],
                plane_send.at[0],
                plane_recv.at[a * planes + k],
                sibling,
            ).wait_recv()
            total = total + plane_in[pl.ds(a, 1), pl.ds(k, 1)][0, 0].astype(F32)
        if m < lines - 1:
            line_out[pl.ds(a, 1)] = total.astype(BF)[None]
            go(line_out.at[a], line_in.at[z], line_send.at[m], line_recv.at[z], at(a, p, head))
        else:
            own = total
    for k in line_peers:
        remote(
            line_out.at[k], line_in.at[k], line_send.at[0], line_recv.at[k], sibling
        ).wait_recv()
        own = own + line_in[pl.ds(k, 1)][0].astype(F32)
    grad[...] = own
    for k in line_peers:
        remote(
            line_small.at[z],
            line_small.at[k],
            line_send.at[0],
            line_recv.at[lines + k],
            sibling,
        ).wait_recv()
    part = line_small[0]
    for k in range(1, lines):
        part = part + line_small[k]
    small[...] = part
    remote(
        own_out, out_other, core_send.at[lines + 1], core_recv.at[lines + 1], sibling
    ).wait_recv()
    remote(
        input_half, input_other, core_send.at[lines + 2], core_recv.at[lines + 2], sibling
    ).wait_recv()
    for copy in started:
        copy.wait_send()


def run_reduce(devices, mine, theirs, small_mine, small_theirs, out_half, input_half):
    lines, planes, rows = mine.shape[:3]
    anywhere = pl.BlockSpec(memory_space=pl.ANY)
    vmem = pl.BlockSpec(memory_space=pltpu.VMEM)
    sem = pltpu.SemaphoreType.DMA

    def kernel(*refs):
        reduce_kernel(devices, *refs)

    return pl.pallas_call(
        kernel,
        out_shape=[
            jax.ShapeDtypeStruct((rows, 128), F32),
            jax.ShapeDtypeStruct((SMALL, 128), F32),
            jax.ShapeDtypeStruct(input_half.shape, BF),
            jax.ShapeDtypeStruct(input_half.shape, BF),
        ],
        in_specs=[vmem] * 4 + [anywhere] * 2,
        out_specs=[vmem] * 2 + [anywhere] * 2,
        scratch_shapes=[
            pltpu.VMEM((lines, planes, rows, 128), BF),
            pltpu.VMEM((SMALL, 128), F32),
            pltpu.VMEM((lines, planes, rows, 128), BF),
            pltpu.VMEM((lines, planes, rows, 128), BF),
            pltpu.VMEM((planes, SMALL, 128), F32),
            pltpu.VMEM((lines, rows, 128), BF),
            pltpu.VMEM((lines, rows, 128), BF),
            pltpu.VMEM((lines, SMALL, 128), F32),
            sem((lines + 3,)),
            sem((lines + 3,)),
            sem((lines * (planes - 1) + planes,)),
            sem((lines * planes + planes,)),
            sem((2 * lines,)),
            sem((2 * lines,)),
        ],
        compiler_params=pltpu.CompilerParams(
            collective_id=1, has_side_effects=True, vmem_limit_bytes=LIMIT
        ),
        name="reduce",
    )(mine, theirs, small_mine, small_theirs, out_half, input_half)


def advance(weight, moment, average, gradient, step_rate, weight_decay):
    gradient = gradient + weight_decay * weight
    moment = 0.9 * moment + gradient
    weight = weight - step_rate * (gradient + 0.9 * moment)
    return (moment, weight, 0.8 * average + 0.2 * weight)


RATES = (0.3, 0.12, 0.12, 0.03, 0.1, 0.2, 0.4, 0.5)


def update_kernel(head, *refs, tokens_all):
    out_other, in_other, grad, small = refs[:4]
    state = refs[6:30]
    output, input_grad = refs[30:32]
    results = refs[32:]
    step = pl.program_id(0)
    factor = tokens_all / small[17:18, :]
    output[...] = out_other[...]
    input_grad[...] = in_other[...].astype(F32) * factor

    @pl.when(step == 0)
    def update():
        width, ff = state[6].shape
        top, chunk = 12 * width, ff // 128
        rate_unit = tokens_all**-0.5

        def apply(n, place, raw, scale):
            new = advance(
                state[3 * n][place],
                state[3 * n + 1][place],
                state[3 * n + 2][place],
                scale * raw,
                RATES[n] * rate_unit,
                0.0 if n == 5 else 0.05,
            )
            for k in range(3):
                results[3 * n + k][place] = new[k]

        scale = factor[:, :64]
        for e in range(3):
            apply(0, e, grad[(8 + e) * width : (9 + e) * width, 64:], scale)
        apply(1, Ellipsis, grad[11 * width : top, 64:], scale)
        for u in range(chunk):
            cols = slice(u * 128, (u + 1) * 128)
            apply(2, (slice(None), cols), grad[top + u * width : top + (u + 1) * width, :], factor)
            apply(
                3,
                (slice(None), cols),
                grad[top + (chunk + u) * width : top + (chunk + u + 1) * width, :],
                factor,
            )
        turned = grad[:top, :].T
        apply(4, (slice(None), slice(0, top)), turned[:64, :], factor[:, :1])
        apply(4, (slice(None), slice(top, 20 * width)), turned[64:, : 8 * width], factor[:, :1])
        for n in range(2):
            apply(5, n, small[4 * n : 4 * n + 4, :], factor)
        values = small[8:17, :]
        values = jnp.where(head[0] == 1, pltpu.roll(values, 64, 1), values)
        for g in range(2):
            apply(6, (slice(None), g), values[:, 32 * g : 32 * g + 32], factor[:, :32])
        for u in range(chunk):
            apply(
                7,
                (slice(None), slice(u * 128, (u + 1) * 128)),
                small[18 + 9 * u : 27 + 9 * u, :],
                factor,
            )


def run_update(tokens_all, head, output, input_grad, out_other, in_other, grad, small, state):
    half = out_other.shape[0]
    steps = half // PAIR

    def all_of(a):
        return pl.BlockSpec(a.shape, lambda i, *_, n=a.ndim: (0,) * n)

    block = (PAIR,) + out_other.shape[1:]
    other = pl.BlockSpec(block, lambda i, *_: (i, 0, 0, 0))
    final = pl.BlockSpec(block, lambda i, head: ((1 - head[0]) * steps + i, 0, 0, 0))
    anywhere = pl.BlockSpec(memory_space=pl.ANY)

    def kernel(*refs):
        update_kernel(*refs, tokens_all=tokens_all)

    return pl.pallas_call(
        kernel,
        out_shape=[jax.ShapeDtypeStruct(a.shape, a.dtype) for a in (output, input_grad, *state)],
        grid_spec=pltpu.PrefetchScalarGridSpec(
            num_scalar_prefetch=1,
            grid=(steps,),
            in_specs=[other, other, all_of(grad), all_of(small), anywhere, anywhere]
            + [all_of(a) for a in state],
            out_specs=[final, final] + [all_of(a) for a in state],
        ),
        input_output_aliases={5: 0, 6: 1},
        compiler_params=pltpu.CompilerParams(
            dimension_semantics=("arbitrary",), vmem_limit_bytes=LIMIT
        ),
        name="update",
    )(head, out_other, in_other, grad, small, output, input_grad, *state)


def per_device(
    tokens,
    cotangent,
    resolution,
    live_images,
    entry_weight,
    entry_momentum,
    entry_average,
    mixing_weight,
    mixing_momentum,
    mixing_average,
    expand_weight,
    expand_momentum,
    expand_average,
    shrink_weight,
    shrink_momentum,
    shrink_average,
    reduce_weight,
    reduce_momentum,
    reduce_average,
    norm_params,
    norm_momentum,
    norm_average,
    value_filter,
    value_momentum,
    value_average,
    hidden_filter,
    hidden_momentum,
    hidden_average,
):
    devices = lax.axis_size("dp")
    head = lax.axis_index("head").reshape(1).astype(jnp.int32)
    turns = ((1, 0), (1, 0), (1, 0), (1, 0, 2))
    mixing, shrink, reduced, values = [
        tuple(a.transpose(turn) for a in arrays)
        for turn, arrays in zip(
            turns,
            (
                (mixing_weight, mixing_momentum, mixing_average),
                (shrink_weight, shrink_momentum, shrink_average),
                (reduce_weight, reduce_momentum, reduce_average),
                (value_filter, value_momentum, value_average),
            ),
        )
    ]
    block, filters = run_pack(
        devices,
        resolution,
        live_images,
        head,
        entry_weight,
        mixing[0],
        expand_weight,
        shrink[0],
        reduced[0],
        values[0],
        hidden_filter,
    )
    blocks, filters = run_gather(devices, block, filters)
    output, input_grad, input_low, mine, theirs, small_mine, small_theirs = run_block(
        resolution, live_images, head, tokens, cotangent, blocks, filters, norm_params
    )
    grad, small, out_other, input_other = run_reduce(
        devices, mine, theirs, small_mine, small_theirs, output, input_low
    )
    state = (
        entry_weight,
        entry_momentum,
        entry_average,
        *mixing,
        expand_weight,
        expand_momentum,
        expand_average,
        *shrink,
        *reduced,
        norm_params,
        norm_momentum,
        norm_average,
        *values,
        hidden_filter,
        hidden_momentum,
        hidden_average,
    )
    tokens_all = devices * tokens.shape[0] * tokens.shape[1] * tokens.shape[2]
    results = list(
        run_update(
            tokens_all, head, output, input_grad, out_other, input_other, grad, small, state
        )
    )
    for n, turn in zip((1, 3, 4, 6), turns):
        for k in range(2 + 3 * n, 5 + 3 * n):
            results[k] = results[k].transpose(turn)
    return tuple(results)


def solution(mesh):
    in_specs = (
        P("dp", None, None, None),
        P("dp", None, None, None),
        P("dp"),
        P("dp"),
        P(None, "dp", "head"),
        P(None, "dp", "head"),
        P(None, "dp", "head"),
        P("head", "dp"),
        P("head", "dp"),
        P("head", "dp"),
        P("dp", "head"),
        P("dp", "head"),
        P("dp", "head"),
        P("head", "dp"),
        P("head", "dp"),
        P("head", "dp"),
        P("dp", "head"),
        P("dp", "head"),
        P("dp", "head"),
        P(),
        P(),
        P(),
        P(None, None, "head"),
        P(None, None, "head"),
        P(None, None, "head"),
        P(None, "head"),
        P(None, "head"),
        P(None, "head"),
    )
    out_specs = (
        P("dp", None, None, None),
        P("dp", None, None, None),
        P(None, "dp", "head"),
        P(None, "dp", "head"),
        P(None, "dp", "head"),
        P("head", "dp"),
        P("head", "dp"),
        P("head", "dp"),
        P("dp", "head"),
        P("dp", "head"),
        P("dp", "head"),
        P("head", "dp"),
        P("head", "dp"),
        P("head", "dp"),
        P("dp", "head"),
        P("dp", "head"),
        P("dp", "head"),
        P(),
        P(),
        P(),
        P(None, None, "head"),
        P(None, None, "head"),
        P(None, None, "head"),
        P(None, "head"),
        P(None, "head"),
        P(None, "head"),
    )
    return jax.shard_map(
        per_device, mesh=mesh, in_specs=in_specs, out_specs=out_specs, check_vma=False
    )
```

```python
import math

import jax
import jax.numpy as jnp
import numpy as np
from jax import lax
from jax.experimental import pallas as pl
from jax.experimental.pallas import tpu as pltpu
from jax.sharding import PartitionSpec as P

BF = jnp.bfloat16
F32 = jnp.float32
EPSILON = 1e-06
HALF = 16
MASKED = -1e9
NN = (((1,), (0,)), ((), ()))
NT = (((1,), (1,)), ((), ()))
TN = (((0,), (0,)), ((), ()))
MESH = pl.DeviceIdType.MESH
SMALL = 64
PAIR = 2
LIMIT = 60 * 1024 * 1024
ROOT = math.sqrt(0.5)


def mm(a, b, dims=NN):
    return lax.dot_general(a, b, dims, preferred_element_type=F32)


def block_of(a4, b4):
    return (a4 % 2) * 8 + (b4 % 2) * 4 + (a4 // 2) * 2 + b4 // 2


def place_of(block):
    return ((block >> 1) & 1) * 2 + (block >> 3), (block & 1) * 2 + ((block >> 2) & 1)


def order_matrix():
    perm = np.zeros((256, 256), np.float32)
    for block in range(16):
        a4, b4 = place_of(block)
        for ci in range(4):
            for ck in range(4):
                perm[block * 16 + ci * 4 + ck, (4 * ci + a4) * HALF + 4 * ck + b4] = 1
    return perm


def cell_shifts():
    places = []
    for ci in range(4):
        for ck in range(4):
            places.append((0, ci, ck, ci // 2, ck // 2))
    for ah in range(2):
        for bh in range(2):
            for ci in range(4):
                for ck in range(4):
                    places.append((1, 2 * ci + ah, 2 * ck + bh, ci // 2, ck // 2))
    index = {p[:3]: n for n, p in enumerate(places)}
    shifts = np.zeros((2, 9, 80, 80), np.float32)
    for n, (g, i, k, si, sk) in enumerate(places):
        for tap in range(9):
            other = index.get((g, i + tap // 3 - 1, k + tap % 3 - 1))
            if other is not None:
                shifts[0, tap, n, other] = 1
                if places[other][3:] == (si, sk):
                    shifts[1, tap, n, other] = 1
    shifts = shifts.reshape(2, 720, 80)
    return np.concatenate([shifts, shifts], 2)


def score_bias():
    rows = np.array([(n % 16) for _ in range(2) for n in list(range(16)) + list(range(64))])
    cols = np.arange(256) % 16

    def image(n):
        return (n // 8) * 2 + (n % 4) // 2

    return np.where(image(rows)[:, None] == image(cols)[None, :], 0.0, MASKED).astype(np.float32)


def shift_masks():
    masks = np.zeros((2, 4, 16, 128), np.float32)
    for fine in range(2):
        for ci in range(4):
            for ck in range(4):
                row = ci * 4 + ck
                for n, (d, e) in enumerate(((1, 0), (-1, 0), (0, 1), (0, -1))):
                    ni, nk = ci + d, ck + e
                    ok = 0 <= ni < 4 and 0 <= nk < 4
                    if fine:
                        ok = ok and ni // 2 == ci // 2 and nk // 2 == ck // 2
                    masks[fine, n, row] = ok
    return masks


def normalise(x):
    centred = x - jnp.mean(x, -1, keepdims=True)
    scale = lax.rsqrt(jnp.mean(centred * centred, -1, keepdims=True) + EPSILON)
    return centred * scale, scale


def normalise_back(grad, unit, scale):
    return scale * (
        grad
        - jnp.mean(grad, -1, keepdims=True)
        - unit * jnp.mean(grad * unit, -1, keepdims=True)
    )


def gelu_pair(h):
    below = 0.5 + 0.5 * lax.erf(h * math.sqrt(0.5))
    density = jnp.exp2(h * h * (-0.5 * math.log2(math.e)))
    return h * below, below + h * density * (1.0 / math.sqrt(2 * math.pi))


def scaled_gelu_pair(u):
    below = math.sqrt(0.5) + math.sqrt(0.5) * lax.erf(u)
    density = jnp.exp2(u * u * (-math.log2(math.e)))
    return u * below, below + u * density * (2.0 / math.sqrt(2 * math.pi))


def block_kernel(
    resolution,
    live_images,
    head,
    tokens,
    cotangent,
    packed,
    filters,
    norms,
    perm,
    perm_t,
    shifts,
    bias,
    edge,
    out,
    input_grad,
    input_low,
    mine,
    theirs,
    small_mine,
    small_theirs,
    entry,
    mixing_t,
    expand,
    shrink_t,
    reduce_w,
    value_filter,
    hidden_filter,
    wide_s,
    square_s,
    d_entry,
    d_mixing_t,
    d_shrink_t,
    d_reduce_t,
    d_norm,
    d_value,
    conv_w,
    key_value_w,
    g_low,
    m_sum,
    folds,
    d_key_value,
    reduce_low,
    rows_in,
    rows_in_t,
    middle_s,
    up_s,
    unit1_s,
    scale1_s,
    unit2_s,
    scale2_s,
    normed_s,
    queries_s,
    mixed_s,
    probs,
    keys_s,
    enhanced_s,
    values_s,
    wide_cells,
    wide_scale,
    narrow_cells,
    narrow_scale,
    second_grad_s,
    factor_s,
    *,
    steps,
):
    step = pl.program_id(0)
    last = pl.num_programs(0) - 1
    first_grid = head[0] * steps
    devices = packed.shape[0] // 2
    width = 128 // devices
    ff = expand.shape[1]
    lane = lax.broadcasted_iota(jnp.int32, (128, 128), 1)
    first_lanes = lane % 64 < 32

    def left(rows):
        return lax.broadcasted_iota(jnp.int32, (rows, 128), 1) < 64

    @pl.when(step == 0)
    def prepare():
        top, chunk = 12 * width, ff // 256
        counts = jnp.zeros((1, 128), F32)
        last_rows = packed.shape[1] - 16
        for n in range(2 * devices):
            pair = packed[n, last_rows : last_rows + 16, :].astype(F32)
            counts = counts + (pair[:1] + 256.0 * pair[1:2])
        factor_s[...] = (devices * 2 * steps * 1024 / 64) / counts
        for d in range(devices):
            one, two = [packed[2 * d + h].astype(F32) for h in range(2)]
            mask = left(top)
            reduce_w[20 * width * d : 20 * width * d + top, :] = jnp.where(
                mask, one[:top], pltpu.roll(two[:top], 64, 1)
            )
            rest = jnp.where(mask, pltpu.roll(one[:top], 64, 1), two[:top])
            reduce_w[20 * width * d + top : 20 * width * (d + 1), :] = rest[: 8 * width]
            rows = slice(width * d, width * d + width)
            for e in range(4):
                square_s[e, rows, :] = rest[(8 + e) * width : (9 + e) * width]
            for h, part in enumerate((one, two)):
                for u in range(chunk):
                    cols = slice((h * chunk + u) * 128, (h * chunk + u + 1) * 128)
                    wide_s[0, rows, cols] = part[top + u * width : top + (u + 1) * width]
                    wide_s[1, rows, cols] = part[
                        top + (chunk + u) * width : top + (chunk + u + 1) * width
                    ]
        reduce_low[...] = reduce_w[...].astype(BF)
        entry[...] = square_s[:3].astype(BF)
        mixing_t[...] = square_s[3].astype(BF)
        expand[...] = wide_s[0]
        shrink_t[...] = wide_s[1].astype(BF)
        for h in range(2):
            hidden_filter[:, h * (ff // 2) : (h + 1) * (ff // 2)] = filters[h, :9, : ff // 2]
        value_filter[...] = jnp.where(
            left(9),
            filters[0, :9, ff // 2 :],
            pltpu.roll(filters[1, :9, ff // 2 :], 64, 1),
        )
        for column in range(3):
            top, mid, low = [
                hidden_filter[3 * a + column : 3 * a + column + 1, :] * ROOT for a in range(3)
            ]
            if column == 1:
                mid = mid + ROOT
            rows = slice(column * 128, column * 128 + 128)
            for n, gain in enumerate(
                (top, 0.5 * (top + mid + low), 0.5 * (top - mid + low), low)
            ):
                conv_w[n, rows, :] = (expand[...] * gain).astype(BF)
        for g in range(2):
            w = entry[1 + g].astype(F32)
            if g == 0:
                keys, vals = w, pltpu.roll(w, 96, 1)
                keep = first_lanes
            else:
                keys, vals = pltpu.roll(w, 32, 1), w
                keep = jnp.logical_not(first_lanes)
            key_value_w[g, :, :128] = jnp.where(keep, keys, 0.0).astype(BF)
            key_value_w[g, :, 128:] = jnp.where(keep, vals, 0.0).astype(BF)
        for ref in (d_entry, d_mixing_t, d_shrink_t, d_reduce_t, d_norm, d_value, m_sum, d_key_value):
            ref[...] = jnp.zeros_like(ref)

    def ordered(ref, place):
        parts = [
            ref[place, a * 16 : a * 16 + 16, b * 16 : b * 16 + 16, :].reshape(256, 128)
            for a in range(2)
            for b in range(2)
        ]
        rows = mm(perm[...], jnp.concatenate(parts, 1))
        return jnp.stack(
            [rows[:, q * 128 : q * 128 + 128].reshape(16, 16, 128) for q in range(4)], 1
        ).reshape(1024, 128)

    def restore(value, ref, place, wide=None):
        blocks = value.reshape(16, 4, 16, 128)
        rows = mm(
            perm_t[...],
            jnp.concatenate([blocks[:, q].reshape(256, 128) for q in range(4)], 1),
        )
        for q in range(4):
            a, b = q // 2, q % 2
            index = (pl.ds(place, 1), slice(a * 16, a * 16 + 16), slice(b * 16, b * 16 + 16))
            part = rows[:, q * 128 : q * 128 + 128]
            ref[index] = part.astype(BF).reshape(1, 16, 16, 128)
            if wide is not None:
                wide[index] = (part * factor_s[...]).reshape(1, 16, 16, 128)

    def of_quadrant(value, q, blocks):
        return value.reshape(blocks, 4, 16, 128)[:, q].reshape(blocks * 16, 128)

    def of_quadrants(parts, blocks):
        return jnp.stack([p.reshape(blocks, 16, 128) for p in parts], 1).reshape(
            blocks * 64, 128
        )

    def gain(n):
        return norms[0, n : n + 1, :]

    def shift_by(n):
        return norms[1, n : n + 1, :]

    def add_norm(n, grad, unit):
        d_norm[n : n + 1, :] += jnp.sum(grad * unit, 0, keepdims=True)
        d_norm[4 + n : 5 + n, :] += jnp.sum(grad, 0, keepdims=True)

    lane80 = lax.broadcasted_iota(jnp.int32, (80, 128), 1)
    zero80 = jnp.zeros((80, 128), BF)
    segments = ((0, 16), (16, 80), (80, 96), (96, 160))
    scaling = 32**-0.5
    rows_of = (slice(0, 2048), slice(2048, 2560))
    cells_f = (wide_cells, narrow_cells)
    cells_scale = (wide_scale, narrow_scale)

    def fine_of(grid):
        return (resolution[first_grid + grid] == 8).astype(jnp.int32)

    def patches_of(slot, g):
        if g == 0:
            blocks = [block_of(t // 4, t % 4) for t in range(16)]
            parts = [normed_s[slot, b * 64 : b * 64 + 64, :] for b in blocks]
        else:
            parts = [normed_s[slot, t * 256 : t * 256 + 256, :] for t in range(4)]
        return jnp.concatenate(parts, 1)

    def move(value, fine, rows, columns):
        size = value.shape[0]
        if rows:
            n = 0 if rows > 0 else 1
            value = pltpu.roll(value, (-4 * rows) % size, 0)
            value = (
                value.reshape(size // 16, 16, 128) * edge[pl.ds(fine, 1), n : n + 1][0]
            ).reshape(size, 128)
        if columns:
            n = 2 if columns > 0 else 3
            value = pltpu.roll(value, (-columns) % size, 0)
            value = (
                value.reshape(size // 16, 16, 128) * edge[pl.ds(fine, 1), n : n + 1][0]
            ).reshape(size, 128)
        return value

    def wrap(a4, d):
        return (a4 + d) % 4, (a4 + d) // 4

    def attend(slot, grid):
        fine = fine_of(grid)
        alive = live_images[first_grid + grid]
        x = ordered(tokens, slot)
        yield
        raised = ordered(cotangent, slot)
        yield
        unit1, scale1 = normalise(x)
        unit1_s[slot] = unit1
        scale1_s[slot] = scale1
        yield
        normed = (unit1 * gain(0) + shift_by(0)).astype(BF)
        normed_s[slot] = normed
        yield
        reduced = [mm(patches_of(slot, g), reduce_low[rows_of[g], :]) for g in range(2)]
        yield
        queries_s[slot] = mm(normed, entry[0]).astype(BF)
        yield
        cells = [normalise(reduced[g]) for g in range(2)]
        yield
        row16 = lax.broadcasted_iota(jnp.int32, (16, 128), 0)
        within = (row16 // 8) * 4 + (row16 % 4) // 2
        live = jnp.stack(
            [
                jnp.where(
                    jnp.where(fine == 1, within + (q // 2) * 8 + (q % 2) * 2, q) < alive, 1.0, 0.0
                )
                for q in range(4)
            ],
            0,
        )
        up_s[slot] = (raised.reshape(16, 4, 16, 128) * live[None]).reshape(1024, 128).astype(BF)
        yield
        acts = []
        for g in range(2):
            unit, scale = cells[g]
            act, slope = gelu_pair(unit * gain(1 + g) + shift_by(1 + g))
            cells_f[g][slot, 0] = unit
            cells_f[g][slot, 1] = slope
            cells_f[g][slot, 2] = act
            cells_scale[g][slot] = scale
            acts.append(act.astype(BF))
        yield
        pairs = [mm(acts[g], key_value_w[g]) for g in range(2)]
        yield
        keys = [pair[:, :128].astype(BF) for pair in pairs]
        values = [pair[:, 128:] for pair in pairs]
        keys_all = [
            jnp.concatenate([keys[0][q * 16 : q * 16 + 16], of_quadrant(keys[1], q, 4)], 0)
            for q in range(4)
        ]
        values_all = jnp.concatenate(
            [
                jnp.concatenate(
                    [values[0][q * 16 : q * 16 + 16], of_quadrant(values[1], q, 4)], 0
                )
                for q in range(4)
            ],
            1,
        )
        values_s[slot] = values_all
        moves = shifts[pl.ds(fine, 1)][0]
        high = values_all.astype(BF)
        rest = (values_all - high.astype(F32)).astype(BF)
        moved = mm(moves, jnp.concatenate([high, rest], 0))
        taps4 = jnp.concatenate([value_filter[...]] * 4, 1)
        enhanced = values_all
        for tap in range(9):
            enhanced = enhanced + moved[tap * 80 : tap * 80 + 80] * taps4[tap : tap + 1]
        enhanced = enhanced.astype(BF)
        yield

        def both_heads(rows):
            return jnp.concatenate(
                [jnp.where(lane80 < 64, rows, zero80), jnp.where(lane80 < 64, zero80, rows)], 0
            )

        queries = queries_s[slot]
        scores = []
        for q in range(4):
            keys_s[slot, q] = both_heads(keys_all[q])
            enhanced_s[slot, q] = both_heads(enhanced[:, q * 128 : q * 128 + 128])
            scores.append(mm(keys_s[slot, q], of_quadrant(queries, q, 16), NT))
        yield
        for q in range(4):
            biased = scores[q] * scaling + fine.astype(F32) * bias[...]
            for lo, hi in segments:
                part = biased[lo:hi]
                part = jnp.exp(part - jnp.max(part, 0, keepdims=True))
                probs[slot, q, lo:hi, :] = part * (1.0 / jnp.sum(part, 0, keepdims=True))
        yield
        mixed_parts = [
            mm(probs[slot, q].astype(BF), enhanced_s[slot, q], TN) for q in range(4)
        ]
        yield
        mixed = of_quadrants(mixed_parts, 16).astype(BF)
        mixed_s[slot] = mixed
        middle = x + mm(mixed, mixing_t[...], NT)
        middle_s[slot] = middle
        yield
        unit2, scale2 = normalise(middle)
        unit2_s[slot] = unit2
        scale2_s[slot] = scale2
        second_low = (unit2 * gain(3) + shift_by(3)).astype(BF)
        second_f = second_low.astype(F32)
        yield
        moved_blocks = {}

        def neighbour(block, down, across):
            a4, b4 = place_of(block)
            na, wa = wrap(a4, down)
            nb, wb = wrap(b4, across)
            key = (block_of(na, nb), wa, wb)
            if key not in moved_blocks:
                rows = second_f[key[0] * 64 : key[0] * 64 + 64]
                moved_blocks[key] = move(rows, fine, wa, wb) if wa or wb else rows
            return moved_blocks[key]

        for block in range(8):
            for column in range(3):
                above, first, second = [neighbour(block, d, column - 1) for d in (-1, 0, 1)]
                below = neighbour(block + 8, 1, column - 1)
                for n, part in enumerate(
                    (above - second, first + second, second - first, below - first)
                ):
                    rows_in[
                        n,
                        slot * 512 + block * 64 : slot * 512 + block * 64 + 64,
                        column * 128 : column * 128 + 128,
                    ] = part.astype(BF)
            yield
    def feed():
        def halves(ref):
            return [
                jnp.concatenate([ref[k, h * 512 : h * 512 + 512, :] for k in range(PAIR)], 0)
                for h in range(2)
            ]

        totals, ups = halves(middle_s), halves(up_s)
        wide = 256
        held = None
        for c in range(0, ff + wide, wide):
            if c < ff:
                cols = slice(c, c + wide)
                m = [mm(rows_in[n], conv_w[n, :, cols]) for n in range(4)]
                hidden = (m[1] + m[0] + m[2], m[1] - m[2] + m[3])
                grads = [mm(ups[h], shrink_t[:, cols]) for h in range(2)]
            if c == 0:
                for n in range(4):
                    for column in range(3):
                        rows = slice(column * 128, column * 128 + 128)
                        rows_in_t[n, rows, :] = rows_in[n, :, rows].T
                ups_t = [ups[h].T for h in range(2)]
            if held:
                before, acts, backs = held
                for h in range(2):
                    totals[h] = totals[h] + mm(acts[h], shrink_t[:, before], NT)
                d_shrink_t[:, before] += mm(ups_t[0], acts[0]) + mm(ups_t[1], acts[1])
                for n in range(4):
                    m_sum[n, :, before] += mm(rows_in_t[n], backs[n])
            if c < ff:
                acts, gs = [], []
                for h in range(2):
                    act, slope = scaled_gelu_pair(hidden[h])
                    acts.append(act.astype(BF))
                    gs.append(grads[h] * slope)
                backs = [
                    v.astype(BF) for v in (gs[0], gs[0] + gs[1], gs[0] - gs[1], gs[1])
                ]
                for n in range(4):
                    g_low[n, :, cols] = backs[n]
                held = (cols, acts, backs)
        for k in range(PAIR):
            total = jnp.concatenate([totals[h][k * 512 : k * 512 + 512] for h in range(2)], 0)
            restore(total.astype(BF), out, k)
        for n in range(4):
            folds[n] = mm(g_low[n], conv_w[n], NT)

    def gather_folds(slot, grid):
        fine = fine_of(grid)
        sums = {}
        for block in range(8):
            for column in range(3):
                for down, other, terms in (
                    (-1, block, ((0, 1),)),
                    (0, block, ((1, 1), (2, -1), (3, -1))),
                    (1, block, ((1, 1), (2, 1), (0, -1))),
                    (1, block + 8, ((3, 1),)),
                ):
                    a4, b4 = place_of(other)
                    na, wa = wrap(a4, down)
                    nb, wb = wrap(b4, column - 1)
                    key = (block_of(na, nb), wa, wb)
                    sums.setdefault(key, []).extend((block, column, n, sign) for n, sign in terms)
        for block in range(16):
            total = None
            for (source, wa, wb), terms in sums.items():
                if source != block:
                    continue
                part = None
                for other, column, n, sign in terms:
                    term = folds[
                        n,
                        slot * 512 + other * 64 : slot * 512 + other * 64 + 64,
                        column * 128 : column * 128 + 128,
                    ]
                    if part is None:
                        part = term if sign > 0 else -term
                    else:
                        part = part + term if sign > 0 else part - term
                if wa or wb:
                    part = move(part, fine, -wa, -wb)
                total = part if total is None else total + part
            second_grad_s[slot, block * 64 : block * 64 + 64, :] = total

    def back(slot, grid):
        fine = fine_of(grid)
        second_grad = second_grad_s[slot]
        unit2 = unit2_s[slot]
        add_norm(3, second_grad, unit2)
        middle_grad = up_s[slot].astype(F32) + normalise_back(
            second_grad * gain(3), unit2, scale2_s[slot]
        )
        middle_low = middle_grad.astype(BF)
        yield
        mixed_grad = mm(middle_low, mixing_t[...]).astype(BF)
        queries = queries_s[slot]
        yield
        d_mixing_t[...] += mm(middle_low, mixed_s[slot], TN)
        yield
        out_grads = [of_quadrant(mixed_grad, q, 16) for q in range(4)]
        prob_grads = [mm(enhanced_s[slot, q], out_grads[q], NT) for q in range(4)]
        yield
        enhanced_parts = []
        for q in range(4):
            full = mm(probs[slot, q].astype(BF), out_grads[q])
            enhanced_parts.append(jnp.where(lane80 < 64, full[:80], full[80:]).astype(BF))
        yield
        score_lows = []
        for q in range(4):
            weights = probs[slot, q]
            product = weights * prob_grads[q]
            score_grad = []
            for lo, hi in segments:
                score_grad.append(
                    product[lo:hi] - weights[lo:hi] * jnp.sum(product[lo:hi], 0, keepdims=True)
                )
            score_lows.append((scaling * jnp.concatenate(score_grad, 0)).astype(BF))
        yield
        query_parts = [mm(score_lows[q], keys_s[slot, q], TN) for q in range(4)]
        yield
        key_parts = []
        for q in range(4):
            full = mm(score_lows[q], of_quadrant(queries, q, 16))
            key_parts.append(jnp.where(lane80 < 64, full[:80], full[80:]).astype(BF))
        yield
        query_low = of_quadrants(query_parts, 16).astype(BF)
        enhanced_grad = jnp.concatenate(enhanced_parts, 1)
        moved = mm(shifts[pl.ds(fine, 1)][0][:, :80], enhanced_grad)
        taps4 = jnp.concatenate([value_filter[...]] * 4, 1)
        value_grad = enhanced_grad.astype(F32)
        values_all = values_s[slot]
        for tap in range(9):
            part = moved[(8 - tap) * 80 : (8 - tap) * 80 + 80]
            value_grad = value_grad + part * taps4[tap : tap + 1]
            row = jnp.sum(part * values_all, 0, keepdims=True)
            d_value[tap : tap + 1, :] += (
                row[:, :128] + row[:, 128:256] + row[:, 256:384] + row[:, 384:]
            )
        value_grad = value_grad.astype(BF)
        value_parts = [value_grad[:, q * 128 : q * 128 + 128] for q in range(4)]
        yield
        narrow = [jnp.concatenate([p[:16] for p in parts], 0) for parts in (key_parts, value_parts)]
        wide = [of_quadrants([p[16:] for p in parts], 4) for parts in (key_parts, value_parts)]
        pairs = [jnp.concatenate(sides, 1) for sides in (narrow, wide)]
        cell_grads = [mm(pairs[g], key_value_w[g], NT) for g in range(2)]
        yield
        normed_grad = mm(query_low, entry[0], NT)
        yield
        reduced_lows = []
        for g in range(2):
            unit, slope = cells_f[g][slot, 0], cells_f[g][slot, 1]
            cell_grad = cell_grads[g] * slope
            add_norm(1 + g, cell_grad, unit)
            reduced_lows.append(
                normalise_back(cell_grad * gain(1 + g), unit, cells_scale[g][slot]).astype(BF)
            )
        yield
        d_entry[0] += mm(normed_s[slot], query_low, TN)
        yield
        spreads = [mm(reduced_lows[g], reduce_low[rows_of[g], :], NT) for g in range(2)]
        yield
        for g in range(2):
            d_key_value[g] += mm(cells_f[g][slot, 2].astype(BF), pairs[g], TN)
        yield
        for g in range(2):
            if g == 0:
                order = [place_of(block) for block in range(16)]
                order = [a4 * 4 + b4 for a4, b4 in order]
            else:
                order = range(4)
            normed_grad = normed_grad + jnp.concatenate(
                [spreads[g][:, t * 128 : t * 128 + 128] for t in order], 0
            )
        yield
        for g in range(2):
            d_reduce_t[:, rows_of[g]] += mm(reduced_lows[g], patches_of(slot, g), TN)
        yield
        unit1 = unit1_s[slot]
        add_norm(0, normed_grad, unit1)
        raw = middle_grad + normalise_back(normed_grad * gain(0), unit1, scale1_s[slot])
        restore(raw.astype(BF), input_low, slot, input_grad)
        yield

    def together(*parts):
        parts = list(parts)
        while parts:
            parts = [part for part in parts if next(part, parts) is not parts]

    first = PAIR * step
    together(*[attend(k, first + k) for k in range(PAIR)])

    feed()
    for k in range(PAIR):
        gather_folds(k, first + k)
    together(*[back(k, first + k) for k in range(PAIR)])

    @pl.when(step == last)
    def finish():
        gains = [hidden_filter[tap : tap + 1, :] * ROOT for tap in range(9)]
        gains[4] = gains[4] + ROOT
        for c in range(0, ff, 128):
            cols = slice(c, c + 128)
            taps = [None] * 9
            for r in range(0, 128, 64):
                weight = expand[r : r + 64, cols]
                total = None
                for column in range(3):
                    rows = slice(column * 128 + r, column * 128 + r + 64)
                    one, two = m_sum[1, rows, cols], m_sum[2, rows, cols]
                    both = (one + two) * 0.5
                    for a in range(3):
                        if a == 1:
                            part = (one - two) * 0.5
                        else:
                            part = m_sum[a // 2 * 3, rows, cols] + both
                        tap = 3 * a + column
                        row = jnp.sum(part * weight, 0, keepdims=True)
                        taps[tap] = row if taps[tap] is None else taps[tap] + row
                        part = part * gains[tap][:, cols]
                        total = part if total is None else total + part
                wide_s[0, r : r + 64, cols] = total
            for tap in range(9):
                hidden_filter[tap : tap + 1, cols] = taps[tap] * ROOT
        wide_s[1] = d_shrink_t[...]
        d_entry[1] = jnp.where(
            first_lanes, d_key_value[0, :, :128], pltpu.roll(d_key_value[0, :, 128:], 32, 1)
        )
        d_entry[2] = jnp.where(
            first_lanes, pltpu.roll(d_key_value[1, :, :128], 96, 1), d_key_value[1, :, 128:]
        )
        is_second = head[0] == 1
        d_reduce = reduce_w
        for n in range(20):
            rows = slice(n * 128, n * 128 + 128)
            d_reduce[rows, :] = d_reduce_t[:, rows].T
        top, chunk = 12 * width, ff // 256
        planes = mine.shape[1]

        def put(d, rows, first, second):
            place = (d // planes, d % planes, rows)
            mine[place] = jnp.where(is_second, second, first)
            theirs[place] = jnp.where(is_second, first, second).astype(BF)

        for d in range(devices):
            rows = slice(width * d, width * d + width)
            upper = d_reduce[20 * width * d : 20 * width * d + top, :]
            lower = jnp.concatenate(
                [d_reduce[20 * width * d + top : 20 * width * (d + 1), :]]
                + [d_entry[e, rows, :] for e in range(3)]
                + [d_mixing_t[rows, :]],
                0,
            )
            firsts = [jnp.where(left(top), upper, pltpu.roll(lower, 64, 1))]
            seconds = [jnp.where(left(top), pltpu.roll(upper, 64, 1), lower)]
            for n in range(2):
                for h, parts in enumerate((firsts, seconds)):
                    for u in range(chunk):
                        cols = slice((h * chunk + u) * 128, (h * chunk + u + 1) * 128)
                        parts.append(wide_s[n, rows, cols])
            pad = mine.shape[2] - 20 * width
            if pad:
                firsts.append(jnp.zeros((pad, 128), F32))
                seconds.append(jnp.zeros((pad, 128), F32))
            put(d, slice(None), jnp.concatenate(firsts, 0), jnp.concatenate(seconds, 0))
        count = jnp.int32(0)
        for n in range(steps):
            side = resolution[head[0] * steps + n]
            count = count + side * side * live_images[head[0] * steps + n]
        halves = [
            jnp.concatenate(
                [
                    hidden_filter[:, (h * chunk + u) * 128 : (h * chunk + u + 1) * 128]
                    for u in range(chunk)
                ],
                0,
            )
            for h in range(2)
        ]
        for ref, flip in ((small_mine, False), (small_theirs, True)):
            ref[...] = jnp.zeros_like(ref)
            ref[:8, :] = d_norm[...]
            ref[8:17, :] = d_value[...]
            ref[17:18, :] = jnp.full((1, 128), count, jnp.int32).astype(F32)
            second = jnp.logical_not(is_second) if flip else is_second
            ref[18 : 18 + 9 * chunk, :] = jnp.where(second, halves[1], halves[0])


def run_block(resolution, live_images, head, tokens, cotangent, packed, filters, norms):
    steps = tokens.shape[0] // 2
    devices, rows = packed.shape[0] // 2, packed.shape[1] - 16
    ff = 2 * (filters.shape[2] - 128)
    lines = line_of(devices)
    consts = [
        jnp.asarray(order_matrix(), BF),
        jnp.asarray(order_matrix().T, BF),
        jnp.asarray(cell_shifts(), BF),
        jnp.asarray(score_bias(), F32),
        jnp.asarray(shift_masks(), F32),
    ]
    whole = [packed, filters, norms] + consts

    def all_of(a):
        return pl.BlockSpec(a.shape, lambda i, *_, n=a.ndim: (0,) * n)

    grid_in = pl.BlockSpec(
        (PAIR, 32, 32, 128), lambda i, res, live, head: (head[0] * (steps // PAIR) + i, 0, 0, 0)
    )
    grid_out = pl.BlockSpec((PAIR, 32, 32, 128), lambda i, *_: (i, 0, 0, 0))
    out_shape = [
        jax.ShapeDtypeStruct((2 * steps, 32, 32, 128), BF),
        jax.ShapeDtypeStruct((2 * steps, 32, 32, 128), F32),
        jax.ShapeDtypeStruct((steps, 32, 32, 128), BF),
        jax.ShapeDtypeStruct((lines, devices // lines, rows, 128), F32),
        jax.ShapeDtypeStruct((lines, devices // lines, rows, 128), BF),
        jax.ShapeDtypeStruct((SMALL, 128), F32),
        jax.ShapeDtypeStruct((SMALL, 128), F32),
    ]

    def kernel(*refs):
        block_kernel(*refs, steps=steps)

    return pl.pallas_call(
        kernel,
        out_shape=out_shape,
        grid_spec=pltpu.PrefetchScalarGridSpec(
            num_scalar_prefetch=3,
            grid=(steps // PAIR,),
            in_specs=[grid_in, grid_in] + [all_of(a) for a in whole],
            out_specs=[grid_in, grid_in, grid_out] + [all_of(a) for a in out_shape[3:]],
            scratch_shapes=[
                pltpu.VMEM((3, 128, 128), BF),
                pltpu.VMEM((128, 128), BF),
                pltpu.VMEM((128, ff), F32),
                pltpu.VMEM((128, ff), BF),
                pltpu.VMEM((2560, 128), F32),
                pltpu.VMEM((9, 128), F32),
                pltpu.VMEM((9, ff), F32),
                pltpu.VMEM((2, 128, ff), F32),
                pltpu.VMEM((4, 128, 128), F32),
                pltpu.VMEM((3, 128, 128), F32),
                pltpu.VMEM((128, 128), F32),
                pltpu.VMEM((128, ff), F32),
                pltpu.VMEM((128, 2560), F32),
                pltpu.VMEM((8, 128), F32),
                pltpu.VMEM((9, 128), F32),
                pltpu.VMEM((4, 384, ff), BF),
                pltpu.VMEM((2, 128, 256), BF),
                pltpu.VMEM((4, PAIR * 512, ff), BF),
                pltpu.VMEM((4, 384, ff), F32),
                pltpu.VMEM((4, PAIR * 512, 384), F32),
                pltpu.VMEM((2, 128, 256), F32),
                pltpu.VMEM((2560, 128), BF),
                pltpu.VMEM((4, PAIR * 512, 384), BF),
                pltpu.VMEM((4, 384, PAIR * 512), BF),
                pltpu.VMEM((2, 1024, 128), F32),
                pltpu.VMEM((2, 1024, 128), BF),
                pltpu.VMEM((2, 1024, 128), F32),
                pltpu.VMEM((2, 1024, 1), F32),
                pltpu.VMEM((2, 1024, 128), F32),
                pltpu.VMEM((2, 1024, 1), F32),
                pltpu.VMEM((2, 1024, 128), BF),
                pltpu.VMEM((2, 1024, 128), BF),
                pltpu.VMEM((2, 1024, 128), BF),
                pltpu.VMEM((2, 4, 160, 256), F32),
                pltpu.VMEM((2, 4, 160, 128), BF),
                pltpu.VMEM((2, 4, 160, 128), BF),
                pltpu.VMEM((2, 80, 512), F32),
                pltpu.VMEM((2, 3, 64, 128), F32),
                pltpu.VMEM((2, 64, 1), F32),
                pltpu.VMEM((2, 3, 256, 128), F32),
                pltpu.VMEM((2, 256, 1), F32),
                pltpu.VMEM((2, 1024, 128), F32),
                pltpu.VMEM((1, 128), F32),
            ],
        ),
        compiler_params=pltpu.CompilerParams(
            dimension_semantics=("arbitrary",), vmem_limit_bytes=LIMIT
        ),
        name="block",
    )(resolution, live_images, head, tokens, cotangent, *whole)


def line_of(devices):
    return 4 if devices % 4 == 0 else 1


def rows_of_block(devices):
    return -(-20 * (128 // devices) // 16) * 16


def pack(
    head,
    resolution,
    live_images,
    entry,
    mixing_t,
    expand,
    shrink_t,
    reduce_t,
    values,
    hidden,
    block,
    filters,
    held,
):
    width, ff = expand.shape
    top, chunk = 12 * width, ff // 128
    held[...] = jnp.zeros_like(held)
    rows = reduce_t[...].T
    held[:top, :64] = rows[:top, :]
    held[: 8 * width, 64:] = rows[top:, :]
    for e in range(3):
        held[(8 + e) * width : (9 + e) * width, 64:] = entry[e]
    held[11 * width : top, 64:] = mixing_t[...]
    for u in range(chunk):
        cols = slice(u * 128, (u + 1) * 128)
        held[top + u * width : top + (u + 1) * width, :] = expand[:, cols]
        held[top + (chunk + u) * width : top + (chunk + u + 1) * width, :] = shrink_t[:, cols]
    half = live_images.shape[0] // 2
    count = jnp.int32(0)
    for n in range(half):
        side = resolution[head * half + n]
        count = count + side * side * live_images[head * half + n]
    count = count // 64
    last = held.shape[0] - 16
    held[last : last + 1, :] = jnp.full((1, 128), count % 256, jnp.int32).astype(F32)
    held[last + 1 : last + 2, :] = jnp.full((1, 128), count // 256, jnp.int32).astype(F32)
    block[...] = held[...].astype(BF)
    filters[...] = jnp.zeros_like(filters)
    filters[:9, :ff] = hidden[...]
    for g in range(2):
        filters[:9, ff + 32 * g : ff + 32 * g + 32] = values[:, g]


def greet(peers, meanwhile=None):
    barrier = pltpu.get_barrier_semaphore()
    for peer in peers:
        pl.semaphore_signal(barrier, inc=1, device_id=peer, device_id_type=MESH)
    if meanwhile is not None:
        meanwhile()
    pl.semaphore_wait(barrier, len(peers))


def places(devices):
    lines = line_of(devices)
    planes = devices // lines
    me, head = lax.axis_index("dp"), lax.axis_index("head")
    z, p = me // planes, me % planes
    line_peers = [((z + k) % lines) for k in range(1, lines)]
    plane_peers = [((p + k) % planes) for k in range(1, planes)]
    return lines, planes, z, p, head, line_peers, plane_peers


def gather_kernel(
    devices,
    resolution,
    live_images,
    entry,
    mixing_t,
    expand,
    shrink_t,
    reduce_t,
    values,
    hidden,
    blocks,
    both,
    block,
    filters,
    held,
    send_sem,
    recv_sem,
    filter_sem,
    local_sem,
):
    lines, planes, z, p, head, line_peers, plane_peers = places(devices)

    def slot(line, plane, core):
        return (line * planes + plane) * 2 + core

    def at(line, plane, core):
        return (line * planes + plane, core)

    sibling = at(z, p, 1 - head)
    greet(
        [at(k, p, head) for k in line_peers] + [at(z, k, head) for k in plane_peers] + [sibling],
        lambda: pack(
            head,
            resolution,
            live_images,
            entry,
            mixing_t,
            expand,
            shrink_t,
            reduce_t,
            values,
            hidden,
            block,
            filters,
            held,
        ),
    )
    sends = []

    def send(source, index, target):
        copy = pltpu.make_async_remote_copy(
            src_ref=source,
            dst_ref=blocks.at[index],
            send_sem=send_sem.at[len(sends)],
            recv_sem=recv_sem.at[index],
            device_id=target,
            device_id_type=MESH,
        )
        copy.start()
        sends.append(copy)

    def arrived(index):
        pltpu.make_async_remote_copy(
            src_ref=block,
            dst_ref=blocks.at[index],
            send_sem=send_sem.at[0],
            recv_sem=recv_sem.at[index],
            device_id=sibling,
            device_id_type=MESH,
        ).wait_recv()

    own = slot(z, p, head)
    for k in line_peers:
        send(block, own, at(k, p, head))
    for k in plane_peers:
        send(block, own, at(z, k, head))
    send(block, own, sibling)
    swap = pltpu.make_async_remote_copy(
        src_ref=filters,
        dst_ref=both.at[head],
        send_sem=filter_sem.at[0],
        recv_sem=filter_sem.at[1],
        device_id=sibling,
        device_id_type=MESH,
    )
    swap.start()
    keep = [
        pltpu.make_async_copy(block, blocks.at[own], local_sem.at[0]),
        pltpu.make_async_copy(filters, both.at[head], local_sem.at[1]),
    ]
    for copy in keep:
        copy.start()
    for k in line_peers:
        index = slot(k, p, head)
        arrived(index)
        for j in plane_peers:
            send(blocks.at[index], index, at(z, j, head))
        send(blocks.at[index], index, sibling)
    for line in [z] + line_peers:
        for j in plane_peers:
            index = slot(line, j, head)
            arrived(index)
            send(blocks.at[index], index, sibling)
    for line in [z] + line_peers:
        for j in [p] + plane_peers:
            arrived(slot(line, j, 1 - head))
    for copy in sends:
        copy.wait_send()
    swap.wait_send()
    pltpu.make_async_remote_copy(
        src_ref=filters,
        dst_ref=both.at[1 - head],
        send_sem=filter_sem.at[0],
        recv_sem=filter_sem.at[1],
        device_id=sibling,
        device_id_type=MESH,
    ).wait_recv()
    for copy in keep:
        copy.wait()


def run_gather(devices, resolution, live_images, *weights):
    lines = line_of(devices)
    planes = devices // lines
    copies = (lines - 1) + lines * (planes - 1) + lines * planes
    rows = rows_of_block(devices) + 16
    filters = (16, weights[-1].shape[1] + 128)
    smem = pl.BlockSpec(memory_space=pltpu.SMEM)
    vmem = pl.BlockSpec(memory_space=pltpu.VMEM)

    def kernel(*refs):
        gather_kernel(devices, *refs)

    return pl.pallas_call(
        kernel,
        out_shape=[
            jax.ShapeDtypeStruct((2 * devices, rows, 128), BF),
            jax.ShapeDtypeStruct((2,) + filters, F32),
        ],
        in_specs=[smem] * 2 + [vmem] * len(weights),
        out_specs=[pl.BlockSpec(memory_space=pl.ANY)] * 2,
        scratch_shapes=[
            pltpu.VMEM((rows, 128), BF),
            pltpu.VMEM(filters, F32),
            pltpu.VMEM((rows, 128), F32),
            pltpu.SemaphoreType.DMA((copies,)),
            pltpu.SemaphoreType.DMA((2 * devices,)),
            pltpu.SemaphoreType.DMA((2,)),
            pltpu.SemaphoreType.DMA((2,)),
        ],
        compiler_params=pltpu.CompilerParams(
            collective_id=0, has_side_effects=True, vmem_limit_bytes=LIMIT
        ),
        name="gather",
    )(resolution, live_images, *weights)


def reduce_kernel(
    devices,
    mine,
    theirs,
    small_mine,
    small_theirs,
    out_half,
    input_half,
    grad,
    small,
    out_other,
    input_other,
    core_in,
    core_small,
    plane_out,
    plane_in,
    plane_small,
    line_out,
    line_in,
    line_small,
    core_send,
    core_recv,
    plane_send,
    plane_recv,
    line_send,
    line_recv,
):
    lines, planes, z, p, head, line_peers, plane_peers = places(devices)
    half = input_half.shape[0]

    def at(line, plane, core):
        return (line * planes + plane, core)

    sibling = at(z, p, 1 - head)
    greet(
        [at(k, p, head) for k in line_peers] + [at(z, k, head) for k in plane_peers] + [sibling]
    )

    def remote(source, target, send, recv, device):
        return pltpu.make_async_remote_copy(
            src_ref=source,
            dst_ref=target,
            send_sem=send,
            recv_sem=recv,
            device_id=device,
            device_id_type=MESH,
        )

    started = []

    def go(*args):
        copy = remote(*args)
        copy.start()
        started.append(copy)

    order = line_peers + [z]
    go(small_theirs, core_small, core_send.at[lines], core_recv.at[lines], sibling)
    for a in order:
        go(theirs.at[a], core_in.at[a], core_send.at[a], core_recv.at[a], sibling)
    remote(
        small_theirs, core_small, core_send.at[lines], core_recv.at[lines], sibling
    ).wait_recv()
    plane_small[pl.ds(p, 1)] = (small_mine[...] + core_small[...])[None]
    for n, k in enumerate(plane_peers):
        go(
            plane_small.at[p],
            plane_small.at[p],
            plane_send.at[lines * (planes - 1) + n],
            plane_recv.at[lines * planes + p],
            at(z, k, head),
        )
    for m, a in enumerate(order):
        remote(
            theirs.at[a], core_in.at[a], core_send.at[a], core_recv.at[a], sibling
        ).wait_recv()
        both = mine[pl.ds(a, 1)] + core_in[pl.ds(a, 1)].astype(F32)
        plane_out[pl.ds(a, 1)] = both.astype(BF)
        for n, k in enumerate(plane_peers):
            go(
                plane_out.at[a, k],
                plane_in.at[a, p],
                plane_send.at[m * (planes - 1) + n],
                plane_recv.at[a * planes + p],
                at(z, k, head),
            )
    own_out = out_half.at[pl.ds(head * half, half)]
    go(own_out, out_other, core_send.at[lines + 1], core_recv.at[lines + 1], sibling)
    go(input_half, input_other, core_send.at[lines + 2], core_recv.at[lines + 2], sibling)
    for k in plane_peers:
        remote(
            plane_small.at[p],
            plane_small.at[k],
            plane_send.at[0],
            plane_recv.at[lines * planes + k],
            sibling,
        ).wait_recv()
    part = plane_small[0]
    for k in range(1, planes):
        part = part + plane_small[k]
    line_small[pl.ds(z, 1)] = part[None]
    for n, k in enumerate(line_peers):
        go(
            line_small.at[z],
            line_small.at[z],
            line_send.at[lines + n],
            line_recv.at[lines + z],
            at(k, p, head),
        )
    own = None
    for m, a in enumerate(order):
        total = (
            mine[pl.ds(a, 1), pl.ds(p, 1)] + core_in[pl.ds(a, 1), pl.ds(p, 1)].astype(F32)
        )[0, 0]
        for k in plane_peers:
            remote(
                plane_out.at[a, k],
                plane_in.at[a, k],
                plane_send.at[0],
                plane_recv.at[a * planes + k],
                sibling,
            ).wait_recv()
            total = total + plane_in[pl.ds(a, 1), pl.ds(k, 1)][0, 0].astype(F32)
        if m < lines - 1:
            line_out[pl.ds(a, 1)] = total.astype(BF)[None]
            go(line_out.at[a], line_in.at[z], line_send.at[m], line_recv.at[z], at(a, p, head))
        else:
            own = total
    for k in line_peers:
        remote(
            line_out.at[k], line_in.at[k], line_send.at[0], line_recv.at[k], sibling
        ).wait_recv()
        own = own + line_in[pl.ds(k, 1)][0].astype(F32)
    grad[...] = own
    for k in line_peers:
        remote(
            line_small.at[z],
            line_small.at[k],
            line_send.at[0],
            line_recv.at[lines + k],
            sibling,
        ).wait_recv()
    part = line_small[0]
    for k in range(1, lines):
        part = part + line_small[k]
    small[...] = part
    remote(
        own_out, out_other, core_send.at[lines + 1], core_recv.at[lines + 1], sibling
    ).wait_recv()
    remote(
        input_half, input_other, core_send.at[lines + 2], core_recv.at[lines + 2], sibling
    ).wait_recv()
    for copy in started:
        copy.wait_send()


def run_reduce(devices, mine, theirs, small_mine, small_theirs, out_half, input_half):
    lines, planes, rows = mine.shape[:3]
    anywhere = pl.BlockSpec(memory_space=pl.ANY)
    vmem = pl.BlockSpec(memory_space=pltpu.VMEM)
    sem = pltpu.SemaphoreType.DMA

    def kernel(*refs):
        reduce_kernel(devices, *refs)

    return pl.pallas_call(
        kernel,
        out_shape=[
            jax.ShapeDtypeStruct((rows, 128), F32),
            jax.ShapeDtypeStruct((SMALL, 128), F32),
            jax.ShapeDtypeStruct(input_half.shape, BF),
            jax.ShapeDtypeStruct(input_half.shape, BF),
        ],
        in_specs=[vmem] * 4 + [anywhere] * 2,
        out_specs=[vmem] * 2 + [anywhere] * 2,
        scratch_shapes=[
            pltpu.VMEM((lines, planes, rows, 128), BF),
            pltpu.VMEM((SMALL, 128), F32),
            pltpu.VMEM((lines, planes, rows, 128), BF),
            pltpu.VMEM((lines, planes, rows, 128), BF),
            pltpu.VMEM((planes, SMALL, 128), F32),
            pltpu.VMEM((lines, rows, 128), BF),
            pltpu.VMEM((lines, rows, 128), BF),
            pltpu.VMEM((lines, SMALL, 128), F32),
            sem((lines + 3,)),
            sem((lines + 3,)),
            sem((lines * (planes - 1) + planes,)),
            sem((lines * planes + planes,)),
            sem((2 * lines,)),
            sem((2 * lines,)),
        ],
        compiler_params=pltpu.CompilerParams(
            collective_id=1, has_side_effects=True, vmem_limit_bytes=LIMIT
        ),
        name="reduce",
    )(mine, theirs, small_mine, small_theirs, out_half, input_half)


def advance(weight, moment, average, gradient, step_rate, weight_decay):
    gradient = gradient + weight_decay * weight
    moment = 0.9 * moment + gradient
    weight = weight - step_rate * (gradient + 0.9 * moment)
    return (moment, weight, 0.8 * average + 0.2 * weight)


RATES = (0.3, 0.12, 0.12, 0.03, 0.1, 0.2, 0.4, 0.5)


def update_kernel(head, *refs, tokens_all):
    out_other, in_other, grad, small = refs[:4]
    state = refs[6:30]
    output, input_grad = refs[30:32]
    results = refs[32:]
    step = pl.program_id(0)
    factor = tokens_all / small[17:18, :]
    output[...] = out_other[...]
    input_grad[...] = in_other[...].astype(F32) * factor

    @pl.when(step == 0)
    def update():
        width, ff = state[6].shape
        top, chunk = 12 * width, ff // 128
        rate_unit = tokens_all**-0.5

        def apply(n, place, raw, scale):
            new = advance(
                state[3 * n][place],
                state[3 * n + 1][place],
                state[3 * n + 2][place],
                scale * raw,
                RATES[n] * rate_unit,
                0.0 if n == 5 else 0.05,
            )
            for k in range(3):
                results[3 * n + k][place] = new[k]

        scale = factor[:, :64]
        for e in range(3):
            apply(0, e, grad[(8 + e) * width : (9 + e) * width, 64:], scale)
        apply(1, Ellipsis, grad[11 * width : top, 64:], scale)
        for u in range(chunk):
            cols = slice(u * 128, (u + 1) * 128)
            apply(2, (slice(None), cols), grad[top + u * width : top + (u + 1) * width, :], factor)
            apply(
                3,
                (slice(None), cols),
                grad[top + (chunk + u) * width : top + (chunk + u + 1) * width, :],
                factor,
            )
        turned = grad[:top, :].T
        apply(4, (slice(None), slice(0, top)), turned[:64, :], factor[:, :1])
        apply(4, (slice(None), slice(top, 20 * width)), turned[64:, : 8 * width], factor[:, :1])
        for n in range(2):
            apply(5, n, small[4 * n : 4 * n + 4, :], factor)
        values = small[8:17, :]
        values = jnp.where(head[0] == 1, pltpu.roll(values, 64, 1), values)
        for g in range(2):
            apply(6, (slice(None), g), values[:, 32 * g : 32 * g + 32], factor[:, :32])
        for u in range(chunk):
            apply(
                7,
                (slice(None), slice(u * 128, (u + 1) * 128)),
                small[18 + 9 * u : 27 + 9 * u, :],
                factor,
            )


def run_update(tokens_all, head, output, input_grad, out_other, in_other, grad, small, state):
    half = out_other.shape[0]
    steps = half // PAIR

    def all_of(a):
        return pl.BlockSpec(a.shape, lambda i, *_, n=a.ndim: (0,) * n)

    block = (PAIR,) + out_other.shape[1:]
    other = pl.BlockSpec(block, lambda i, *_: (i, 0, 0, 0))
    final = pl.BlockSpec(block, lambda i, head: ((1 - head[0]) * steps + i, 0, 0, 0))
    anywhere = pl.BlockSpec(memory_space=pl.ANY)

    def kernel(*refs):
        update_kernel(*refs, tokens_all=tokens_all)

    return pl.pallas_call(
        kernel,
        out_shape=[jax.ShapeDtypeStruct(a.shape, a.dtype) for a in (output, input_grad, *state)],
        grid_spec=pltpu.PrefetchScalarGridSpec(
            num_scalar_prefetch=1,
            grid=(steps,),
            in_specs=[other, other, all_of(grad), all_of(small), anywhere, anywhere]
            + [all_of(a) for a in state],
            out_specs=[final, final] + [all_of(a) for a in state],
        ),
        input_output_aliases={5: 0, 6: 1},
        compiler_params=pltpu.CompilerParams(
            dimension_semantics=("arbitrary",), vmem_limit_bytes=LIMIT
        ),
        name="update",
    )(head, out_other, in_other, grad, small, output, input_grad, *state)


def per_device(
    tokens,
    cotangent,
    resolution,
    live_images,
    entry_weight,
    entry_momentum,
    entry_average,
    mixing_weight,
    mixing_momentum,
    mixing_average,
    expand_weight,
    expand_momentum,
    expand_average,
    shrink_weight,
    shrink_momentum,
    shrink_average,
    reduce_weight,
    reduce_momentum,
    reduce_average,
    norm_params,
    norm_momentum,
    norm_average,
    value_filter,
    value_momentum,
    value_average,
    hidden_filter,
    hidden_momentum,
    hidden_average,
):
    devices = lax.axis_size("dp")
    head = lax.axis_index("head").reshape(1).astype(jnp.int32)
    turns = ((1, 0), (1, 0), (1, 0), (1, 0, 2))
    mixing, shrink, reduced, values = [
        tuple(a.transpose(turn) for a in arrays)
        for turn, arrays in zip(
            turns,
            (
                (mixing_weight, mixing_momentum, mixing_average),
                (shrink_weight, shrink_momentum, shrink_average),
                (reduce_weight, reduce_momentum, reduce_average),
                (value_filter, value_momentum, value_average),
            ),
        )
    ]
    blocks, filters = run_gather(
        devices,
        resolution,
        live_images,
        entry_weight,
        mixing[0],
        expand_weight,
        shrink[0],
        reduced[0],
        values[0],
        hidden_filter,
    )
    output, input_grad, input_low, mine, theirs, small_mine, small_theirs = run_block(
        resolution, live_images, head, tokens, cotangent, blocks, filters, norm_params
    )
    grad, small, out_other, input_other = run_reduce(
        devices, mine, theirs, small_mine, small_theirs, output, input_low
    )
    state = (
        entry_weight,
        entry_momentum,
        entry_average,
        *mixing,
        expand_weight,
        expand_momentum,
        expand_average,
        *shrink,
        *reduced,
        norm_params,
        norm_momentum,
        norm_average,
        *values,
        hidden_filter,
        hidden_momentum,
        hidden_average,
    )
    tokens_all = devices * tokens.shape[0] * tokens.shape[1] * tokens.shape[2]
    results = list(
        run_update(
            tokens_all, head, output, input_grad, out_other, input_other, grad, small, state
        )
    )
    for n, turn in zip((1, 3, 4, 6), turns):
        for k in range(2 + 3 * n, 5 + 3 * n):
            results[k] = results[k].transpose(turn)
    return tuple(results)


def solution(mesh):
    in_specs = (
        P("dp", None, None, None),
        P("dp", None, None, None),
        P("dp"),
        P("dp"),
        P(None, "dp", "head"),
        P(None, "dp", "head"),
        P(None, "dp", "head"),
        P("head", "dp"),
        P("head", "dp"),
        P("head", "dp"),
        P("dp", "head"),
        P("dp", "head"),
        P("dp", "head"),
        P("head", "dp"),
        P("head", "dp"),
        P("head", "dp"),
        P("dp", "head"),
        P("dp", "head"),
        P("dp", "head"),
        P(),
        P(),
        P(),
        P(None, None, "head"),
        P(None, None, "head"),
        P(None, None, "head"),
        P(None, "head"),
        P(None, "head"),
        P(None, "head"),
    )
    out_specs = (
        P("dp", None, None, None),
        P("dp", None, None, None),
        P(None, "dp", "head"),
        P(None, "dp", "head"),
        P(None, "dp", "head"),
        P("head", "dp"),
        P("head", "dp"),
        P("head", "dp"),
        P("dp", "head"),
        P("dp", "head"),
        P("dp", "head"),
        P("head", "dp"),
        P("head", "dp"),
        P("head", "dp"),
        P("dp", "head"),
        P("dp", "head"),
        P("dp", "head"),
        P(),
        P(),
        P(),
        P(None, None, "head"),
        P(None, None, "head"),
        P(None, None, "head"),
        P(None, "head"),
        P(None, "head"),
        P(None, "head"),
    )
    return jax.shard_map(
        per_device, mesh=mesh, in_specs=in_specs, out_specs=out_specs, check_vma=False
    )
```

```python
import math

import jax
import jax.numpy as jnp
import numpy as np
from jax import lax
from jax.experimental import pallas as pl
from jax.experimental.pallas import tpu as pltpu
from jax.sharding import PartitionSpec as P

BF = jnp.bfloat16
F32 = jnp.float32
EPSILON = 1e-06
HALF = 16
MASKED = -1e9
NN = (((1,), (0,)), ((), ()))
NT = (((1,), (1,)), ((), ()))
TN = (((0,), (0,)), ((), ()))
MESH = pl.DeviceIdType.MESH
SMALL = 64
PAIR = 2
LIMIT = 60 * 1024 * 1024
ROOT = math.sqrt(0.5)


def mm(a, b, dims=NN):
    return lax.dot_general(a, b, dims, preferred_element_type=F32)


def block_of(a4, b4):
    return (a4 % 2) * 8 + (b4 % 2) * 4 + (a4 // 2) * 2 + b4 // 2


def place_of(block):
    return ((block >> 1) & 1) * 2 + (block >> 3), (block & 1) * 2 + ((block >> 2) & 1)


def order_matrix():
    perm = np.zeros((256, 256), np.float32)
    for block in range(16):
        a4, b4 = place_of(block)
        for ci in range(4):
            for ck in range(4):
                perm[block * 16 + ci * 4 + ck, (4 * ci + a4) * HALF + 4 * ck + b4] = 1
    return perm


def score_bias():
    rows = np.array([(n % 16) for _ in range(2) for n in list(range(16)) + list(range(64))])
    cols = np.arange(256) % 16

    def image(n):
        return (n // 8) * 2 + (n % 4) // 2

    return np.where(image(rows)[:, None] == image(cols)[None, :], 0.0, MASKED).astype(np.float32)


def shift_masks():
    masks = np.zeros((2, 4, 16, 128), np.float32)
    for fine in range(2):
        for ci in range(4):
            for ck in range(4):
                row = ci * 4 + ck
                for n, (d, e) in enumerate(((1, 0), (-1, 0), (0, 1), (0, -1))):
                    ni, nk = ci + d, ck + e
                    ok = 0 <= ni < 4 and 0 <= nk < 4
                    if fine:
                        ok = ok and ni // 2 == ci // 2 and nk // 2 == ck // 2
                    masks[fine, n, row] = ok
    return masks


def normalise(x):
    centred = x - jnp.mean(x, -1, keepdims=True)
    scale = lax.rsqrt(jnp.mean(centred * centred, -1, keepdims=True) + EPSILON)
    return centred * scale, scale


def normalise_back(grad, unit, scale):
    return scale * (
        grad
        - jnp.mean(grad, -1, keepdims=True)
        - unit * jnp.mean(grad * unit, -1, keepdims=True)
    )


def gelu_pair(h):
    below = 0.5 + 0.5 * lax.erf(h * math.sqrt(0.5))
    density = jnp.exp2(h * h * (-0.5 * math.log2(math.e)))
    return h * below, below + h * density * (1.0 / math.sqrt(2 * math.pi))


def scaled_gelu_pair(u):
    below = math.sqrt(0.5) + math.sqrt(0.5) * lax.erf(u)
    density = jnp.exp2(u * u * (-math.log2(math.e)))
    return u * below, below + u * density * (2.0 / math.sqrt(2 * math.pi))


def block_kernel(
    resolution,
    live_images,
    head,
    tokens,
    cotangent,
    packed,
    filters,
    norms,
    perm,
    perm_t,
    bias,
    edge,
    out,
    input_grad,
    input_low,
    mine,
    theirs,
    small_mine,
    small_theirs,
    entry,
    mixing_t,
    expand,
    shrink_t,
    reduce_w,
    value_filter,
    hidden_filter,
    wide_s,
    square_s,
    d_entry,
    d_mixing_t,
    d_shrink_t,
    d_reduce_t,
    d_norm,
    d_value,
    conv_w,
    key_value_w,
    g_low,
    m_sum,
    folds,
    d_key_value,
    reduce_low,
    rows_in,
    rows_in_t,
    middle_s,
    up_s,
    unit1_s,
    scale1_s,
    unit2_s,
    scale2_s,
    normed_s,
    queries_s,
    mixed_s,
    probs,
    keys_s,
    enhanced_s,
    values_s,
    wide_cells,
    wide_scale,
    narrow_cells,
    narrow_scale,
    second_grad_s,
    factor_s,
    *,
    steps,
):
    step = pl.program_id(0)
    last = pl.num_programs(0) - 1
    first_grid = head[0] * steps
    devices = packed.shape[0] // 2
    width = 128 // devices
    ff = expand.shape[1]
    lane = lax.broadcasted_iota(jnp.int32, (128, 128), 1)
    first_lanes = lane % 64 < 32

    def left(rows):
        return lax.broadcasted_iota(jnp.int32, (rows, 128), 1) < 64

    @pl.when(step == 0)
    def prepare():
        top, chunk = 12 * width, ff // 256
        counts = jnp.zeros((1, 128), F32)
        last_rows = packed.shape[1] - 16
        for n in range(2 * devices):
            pair = packed[n, last_rows : last_rows + 16, :].astype(F32)
            counts = counts + (pair[:1] + 256.0 * pair[1:2])
        factor_s[...] = (devices * 2 * steps * 1024 / 64) / counts
        for d in range(devices):
            one, two = [packed[2 * d + h].astype(F32) for h in range(2)]
            mask = left(top)
            reduce_w[20 * width * d : 20 * width * d + top, :] = jnp.where(
                mask, one[:top], pltpu.roll(two[:top], 64, 1)
            )
            rest = jnp.where(mask, pltpu.roll(one[:top], 64, 1), two[:top])
            reduce_w[20 * width * d + top : 20 * width * (d + 1), :] = rest[: 8 * width]
            rows = slice(width * d, width * d + width)
            for e in range(4):
                square_s[e, rows, :] = rest[(8 + e) * width : (9 + e) * width]
            for h, part in enumerate((one, two)):
                for u in range(chunk):
                    cols = slice((h * chunk + u) * 128, (h * chunk + u + 1) * 128)
                    wide_s[0, rows, cols] = part[top + u * width : top + (u + 1) * width]
                    wide_s[1, rows, cols] = part[
                        top + (chunk + u) * width : top + (chunk + u + 1) * width
                    ]
        reduce_low[...] = reduce_w[...].astype(BF)
        entry[...] = square_s[:3].astype(BF)
        mixing_t[...] = square_s[3].astype(BF)
        expand[...] = wide_s[0]
        shrink_t[...] = wide_s[1].astype(BF)
        for h in range(2):
            hidden_filter[:, h * (ff // 2) : (h + 1) * (ff // 2)] = filters[h, :9, : ff // 2]
        value_filter[...] = jnp.where(
            left(9),
            filters[0, :9, ff // 2 :],
            pltpu.roll(filters[1, :9, ff // 2 :], 64, 1),
        )
        for column in range(3):
            top, mid, low = [
                hidden_filter[3 * a + column : 3 * a + column + 1, :] * ROOT for a in range(3)
            ]
            if column == 1:
                mid = mid + ROOT
            rows = slice(column * 128, column * 128 + 128)
            for n, gain in enumerate(
                (top, 0.5 * (top + mid + low), 0.5 * (top - mid + low), low)
            ):
                conv_w[n, rows, :] = (expand[...] * gain).astype(BF)
        for g in range(2):
            w = entry[1 + g].astype(F32)
            if g == 0:
                keys, vals = w, pltpu.roll(w, 96, 1)
                keep = first_lanes
            else:
                keys, vals = pltpu.roll(w, 32, 1), w
                keep = jnp.logical_not(first_lanes)
            key_value_w[g, :, :128] = jnp.where(keep, keys, 0.0).astype(BF)
            key_value_w[g, :, 128:] = jnp.where(keep, vals, 0.0).astype(BF)
        for ref in (d_entry, d_mixing_t, d_shrink_t, d_reduce_t, d_norm, d_value, m_sum, d_key_value):
            ref[...] = jnp.zeros_like(ref)

    def ordered(ref, place):
        parts = [
            ref[place, a * 16 : a * 16 + 16, b * 16 : b * 16 + 16, :].reshape(256, 128)
            for a in range(2)
            for b in range(2)
        ]
        rows = mm(perm[...], jnp.concatenate(parts, 1))
        return jnp.stack(
            [rows[:, q * 128 : q * 128 + 128].reshape(16, 16, 128) for q in range(4)], 1
        ).reshape(1024, 128)

    def restore(value, ref, place, wide=None):
        blocks = value.reshape(16, 4, 16, 128)
        rows = mm(
            perm_t[...],
            jnp.concatenate([blocks[:, q].reshape(256, 128) for q in range(4)], 1),
        )
        for q in range(4):
            a, b = q // 2, q % 2
            index = (pl.ds(place, 1), slice(a * 16, a * 16 + 16), slice(b * 16, b * 16 + 16))
            part = rows[:, q * 128 : q * 128 + 128]
            ref[index] = part.astype(BF).reshape(1, 16, 16, 128)
            if wide is not None:
                wide[index] = (part * factor_s[...]).reshape(1, 16, 16, 128)

    def of_quadrant(value, q, blocks):
        return value.reshape(blocks, 4, 16, 128)[:, q].reshape(blocks * 16, 128)

    def of_quadrants(parts, blocks):
        return jnp.stack([p.reshape(blocks, 16, 128) for p in parts], 1).reshape(
            blocks * 64, 128
        )

    def gain(n):
        return norms[0, n : n + 1, :]

    def shift_by(n):
        return norms[1, n : n + 1, :]

    def add_norm(n, grad, unit):
        d_norm[n : n + 1, :] += jnp.sum(grad * unit, 0, keepdims=True)
        d_norm[4 + n : 5 + n, :] += jnp.sum(grad, 0, keepdims=True)

    lane80 = lax.broadcasted_iota(jnp.int32, (80, 128), 1)
    zero80 = jnp.zeros((80, 128), BF)
    segments = ((0, 16), (16, 80), (80, 96), (96, 160))
    scaling = 32**-0.5
    rows_of = (slice(0, 2048), slice(2048, 2560))
    cells_f = (wide_cells, narrow_cells)
    cells_scale = (wide_scale, narrow_scale)

    def fine_of(grid):
        return (resolution[first_grid + grid] == 8).astype(jnp.int32)

    def patches_of(slot, g):
        if g == 0:
            blocks = [block_of(t // 4, t % 4) for t in range(16)]
            parts = [normed_s[slot, b * 64 : b * 64 + 64, :] for b in blocks]
        else:
            parts = [normed_s[slot, t * 256 : t * 256 + 256, :] for t in range(4)]
        return jnp.concatenate(parts, 1)

    def move(value, fine, rows, columns):
        size = value.shape[0]
        if rows:
            n = 0 if rows > 0 else 1
            value = pltpu.roll(value, (-4 * rows) % size, 0)
            value = (
                value.reshape(size // 16, 16, 128) * edge[pl.ds(fine, 1), n : n + 1][0]
            ).reshape(size, 128)
        if columns:
            n = 2 if columns > 0 else 3
            value = pltpu.roll(value, (-columns) % size, 0)
            value = (
                value.reshape(size // 16, 16, 128) * edge[pl.ds(fine, 1), n : n + 1][0]
            ).reshape(size, 128)
        return value

    def cell_moves(value, fine):
        masks = [
            jnp.concatenate([edge[pl.ds(fine, 1), n : n + 1][0, 0]] * 4, 1) for n in range(4)
        ]
        made = {}

        def of(source, rows, columns):
            if (source, rows, columns) not in made:
                part = value[source * 16 : source * 16 + 16]
                if rows:
                    part = pltpu.roll(part, (-4 * rows) % 16, 0) * masks[0 if rows > 0 else 1]
                if columns:
                    part = pltpu.roll(part, -columns % 16, 0) * masks[2 if columns > 0 else 3]
                made[source, rows, columns] = part
            return made[source, rows, columns]

        moved = []
        for tap in range(9):
            down, across = tap // 3 - 1, tap % 3 - 1
            blocks = [of(0, down, across)]
            for a in range(2):
                for b in range(2):
                    na, nb = a + down, b + across
                    blocks.append(of(1 + na % 2 * 2 + nb % 2, na // 2, nb // 2))
            moved.append(blocks)
        return moved

    def wrap(a4, d):
        return (a4 + d) % 4, (a4 + d) // 4

    def shared(rows, weight, dims=NN):
        return None, None, rows, weight, dims

    def summed(ref, place, left, right):
        return ref, place, left, right, TN

    def attend(slot, grid):
        fine = fine_of(grid)
        alive = live_images[first_grid + grid]
        x = ordered(tokens, slot)
        yield
        raised = ordered(cotangent, slot)
        yield
        unit1, scale1 = normalise(x)
        unit1_s[slot] = unit1
        scale1_s[slot] = scale1
        yield
        normed = (unit1 * gain(0) + shift_by(0)).astype(BF)
        normed_s[slot] = normed
        yield
        reduced = []
        for g in range(2):
            reduced.append((yield shared(patches_of(slot, g), reduce_low[rows_of[g], :])))
        queries_s[slot] = mm(normed, entry[0]).astype(BF)
        yield
        cells = [normalise(reduced[g]) for g in range(2)]
        yield
        row16 = lax.broadcasted_iota(jnp.int32, (16, 128), 0)
        within = (row16 // 8) * 4 + (row16 % 4) // 2
        live = jnp.stack(
            [
                jnp.where(
                    jnp.where(fine == 1, within + (q // 2) * 8 + (q % 2) * 2, q) < alive, 1.0, 0.0
                )
                for q in range(4)
            ],
            0,
        )
        up_s[slot] = (raised.reshape(16, 4, 16, 128) * live[None]).reshape(1024, 128).astype(BF)
        yield
        acts = []
        for g in range(2):
            unit, scale = cells[g]
            act, slope = gelu_pair(unit * gain(1 + g) + shift_by(1 + g))
            cells_f[g][slot, 0] = unit
            cells_f[g][slot, 1] = slope
            cells_f[g][slot, 2] = act
            cells_scale[g][slot] = scale
            acts.append(act.astype(BF))
        yield
        pairs = []
        for g in range(2):
            pairs.append((yield shared(acts[g], key_value_w[g])))
        keys = [pair[:, :128].astype(BF) for pair in pairs]
        values = [pair[:, 128:] for pair in pairs]
        keys_all = [
            jnp.concatenate([keys[0][q * 16 : q * 16 + 16], of_quadrant(keys[1], q, 4)], 0)
            for q in range(4)
        ]
        values_all = jnp.concatenate(
            [
                jnp.concatenate(
                    [values[0][q * 16 : q * 16 + 16], of_quadrant(values[1], q, 4)], 0
                )
                for q in range(4)
            ],
            1,
        )
        values_s[slot] = values_all
        yield
        moved = cell_moves(values_all, fine)
        taps4 = jnp.concatenate([value_filter[...]] * 4, 1)
        yield
        enhanced = []
        for block in range(5):
            total = values_all[block * 16 : block * 16 + 16]
            for tap in range(9):
                total = total + moved[tap][block] * taps4[tap : tap + 1]
            enhanced.append(total)
        enhanced = jnp.concatenate(enhanced, 0).astype(BF)
        yield

        def both_heads(rows):
            return jnp.concatenate(
                [jnp.where(lane80 < 64, rows, zero80), jnp.where(lane80 < 64, zero80, rows)], 0
            )

        queries = queries_s[slot]
        scores = []
        for q in range(4):
            keys_s[slot, q] = both_heads(keys_all[q])
            enhanced_s[slot, q] = both_heads(enhanced[:, q * 128 : q * 128 + 128])
            scores.append(mm(keys_s[slot, q], of_quadrant(queries, q, 16), NT))
        yield
        for q in range(4):
            biased = scores[q] * scaling + fine.astype(F32) * bias[...]
            for lo, hi in segments:
                part = biased[lo:hi]
                part = jnp.exp(part - jnp.max(part, 0, keepdims=True))
                probs[slot, q, lo:hi, :] = part * (1.0 / jnp.sum(part, 0, keepdims=True))
        yield
        mixed_parts = [
            mm(probs[slot, q].astype(BF), enhanced_s[slot, q], TN) for q in range(4)
        ]
        yield
        mixed = of_quadrants(mixed_parts, 16).astype(BF)
        mixed_s[slot] = mixed
        middle = x + mm(mixed, mixing_t[...], NT)
        middle_s[slot] = middle
        yield
        unit2, scale2 = normalise(middle)
        unit2_s[slot] = unit2
        scale2_s[slot] = scale2
        second_low = (unit2 * gain(3) + shift_by(3)).astype(BF)
        second_f = second_low.astype(F32)
        yield
        moved_blocks = {}

        def neighbour(block, down, across):
            a4, b4 = place_of(block)
            na, wa = wrap(a4, down)
            nb, wb = wrap(b4, across)
            key = (block_of(na, nb), wa, wb)
            if key not in moved_blocks:
                rows = second_f[key[0] * 64 : key[0] * 64 + 64]
                moved_blocks[key] = move(rows, fine, wa, wb) if wa or wb else rows
            return moved_blocks[key]

        for block in range(8):
            for column in range(3):
                above, first, second = [neighbour(block, d, column - 1) for d in (-1, 0, 1)]
                below = neighbour(block + 8, 1, column - 1)
                for n, part in enumerate(
                    (above - second, first + second, second - first, below - first)
                ):
                    rows_in[
                        n,
                        slot * 512 + block * 64 : slot * 512 + block * 64 + 64,
                        column * 128 : column * 128 + 128,
                    ] = part.astype(BF)
            yield
    def feed():
        def halves(ref):
            return [
                jnp.concatenate([ref[k, h * 512 : h * 512 + 512, :] for k in range(PAIR)], 0)
                for h in range(2)
            ]

        totals, ups = halves(middle_s), halves(up_s)
        wide = 256
        held = None
        for c in range(0, ff + wide, wide):
            if c < ff:
                cols = slice(c, c + wide)
                m = [mm(rows_in[n], conv_w[n, :, cols]) for n in range(4)]
                hidden = (m[1] + m[0] + m[2], m[1] - m[2] + m[3])
                grads = [mm(ups[h], shrink_t[:, cols]) for h in range(2)]
            if c == 0:
                for n in range(4):
                    for column in range(3):
                        rows = slice(column * 128, column * 128 + 128)
                        rows_in_t[n, rows, :] = rows_in[n, :, rows].T
                ups_t = [ups[h].T for h in range(2)]
            if held:
                before, acts, backs = held
                for h in range(2):
                    totals[h] = totals[h] + mm(acts[h], shrink_t[:, before], NT)
                d_shrink_t[:, before] += mm(ups_t[0], acts[0]) + mm(ups_t[1], acts[1])
                for n in range(4):
                    m_sum[n, :, before] += mm(rows_in_t[n], backs[n])
            if c < ff:
                acts, gs = [], []
                for h in range(2):
                    act, slope = scaled_gelu_pair(hidden[h])
                    acts.append(act.astype(BF))
                    gs.append(grads[h] * slope)
                backs = [
                    v.astype(BF) for v in (gs[0], gs[0] + gs[1], gs[0] - gs[1], gs[1])
                ]
                for n in range(4):
                    g_low[n, :, cols] = backs[n]
                held = (cols, acts, backs)
        for n in range(4):
            folds[n] = mm(g_low[n], conv_w[n], NT)
        for k in range(PAIR):
            total = jnp.concatenate([totals[h][k * 512 : k * 512 + 512] for h in range(2)], 0)
            restore(total.astype(BF), out, k)

    def gather_folds(slot, grid):
        fine = fine_of(grid)
        sums = {}
        for block in range(8):
            for column in range(3):
                for down, other, terms in (
                    (-1, block, ((0, 1),)),
                    (0, block, ((1, 1), (2, -1), (3, -1))),
                    (1, block, ((1, 1), (2, 1), (0, -1))),
                    (1, block + 8, ((3, 1),)),
                ):
                    a4, b4 = place_of(other)
                    na, wa = wrap(a4, down)
                    nb, wb = wrap(b4, column - 1)
                    key = (block_of(na, nb), wa, wb)
                    sums.setdefault(key, []).extend((block, column, n, sign) for n, sign in terms)
        for block in range(16):
            total = None
            for (source, wa, wb), terms in sums.items():
                if source != block:
                    continue
                part = None
                for other, column, n, sign in terms:
                    term = folds[
                        n,
                        slot * 512 + other * 64 : slot * 512 + other * 64 + 64,
                        column * 128 : column * 128 + 128,
                    ]
                    if part is None:
                        part = term if sign > 0 else -term
                    else:
                        part = part + term if sign > 0 else part - term
                if wa or wb:
                    part = move(part, fine, -wa, -wb)
                total = part if total is None else total + part
            second_grad_s[slot, block * 64 : block * 64 + 64, :] = total

    def back(slot, grid):
        fine = fine_of(grid)
        second_grad = second_grad_s[slot]
        unit2 = unit2_s[slot]
        add_norm(3, second_grad, unit2)
        middle_grad = up_s[slot].astype(F32) + normalise_back(
            second_grad * gain(3), unit2, scale2_s[slot]
        )
        middle_low = middle_grad.astype(BF)
        yield
        mixed_grad = mm(middle_low, mixing_t[...]).astype(BF)
        queries = queries_s[slot]
        yield
        d_mixing_t[...] += mm(middle_low, mixed_s[slot], TN)
        yield
        out_grads = [of_quadrant(mixed_grad, q, 16) for q in range(4)]
        prob_grads = [mm(enhanced_s[slot, q], out_grads[q], NT) for q in range(4)]
        yield
        enhanced_parts = []
        for q in range(4):
            full = mm(probs[slot, q].astype(BF), out_grads[q])
            enhanced_parts.append(jnp.where(lane80 < 64, full[:80], full[80:]).astype(BF))
        yield
        score_lows = []
        for q in range(4):
            weights = probs[slot, q]
            product = weights * prob_grads[q]
            score_grad = []
            for lo, hi in segments:
                score_grad.append(
                    product[lo:hi] - weights[lo:hi] * jnp.sum(product[lo:hi], 0, keepdims=True)
                )
            score_lows.append((scaling * jnp.concatenate(score_grad, 0)).astype(BF))
        yield
        query_parts = [mm(score_lows[q], keys_s[slot, q], TN) for q in range(4)]
        yield
        key_parts = []
        for q in range(4):
            full = mm(score_lows[q], of_quadrant(queries, q, 16))
            key_parts.append(jnp.where(lane80 < 64, full[:80], full[80:]).astype(BF))
        yield
        query_low = of_quadrants(query_parts, 16).astype(BF)
        enhanced_grad = jnp.concatenate(enhanced_parts, 1)
        yield
        enhanced_grad = enhanced_grad.astype(F32)
        moved = cell_moves(enhanced_grad, fine)
        taps4 = jnp.concatenate([value_filter[...]] * 4, 1)
        yield
        value_grad = []
        for block in range(5):
            total = enhanced_grad[block * 16 : block * 16 + 16]
            for tap in range(9):
                total = total + moved[8 - tap][block] * taps4[tap : tap + 1]
            value_grad.append(total)
        value_grad = jnp.concatenate(value_grad, 0).astype(BF)
        yield
        values_all = values_s[slot]
        for tap in range(9):
            part = None
            for block in range(5):
                product = moved[8 - tap][block] * values_all[block * 16 : block * 16 + 16]
                part = product if part is None else part + product
            part = part[:, :128] + part[:, 128:256] + part[:, 256:384] + part[:, 384:]
            d_value[tap : tap + 1, :] += jnp.sum(part, 0, keepdims=True)
        value_parts = [value_grad[:, q * 128 : q * 128 + 128] for q in range(4)]
        yield
        narrow = [jnp.concatenate([p[:16] for p in parts], 0) for parts in (key_parts, value_parts)]
        wide = [of_quadrants([p[16:] for p in parts], 4) for parts in (key_parts, value_parts)]
        pairs = [jnp.concatenate(sides, 1) for sides in (narrow, wide)]
        cell_grads = []
        for g in range(2):
            cell_grads.append((yield shared(pairs[g], key_value_w[g], NT)))
        normed_grad = mm(query_low, entry[0], NT)
        yield
        reduced_lows = []
        for g in range(2):
            unit, slope = cells_f[g][slot, 0], cells_f[g][slot, 1]
            cell_grad = cell_grads[g] * slope
            add_norm(1 + g, cell_grad, unit)
            reduced_lows.append(
                normalise_back(cell_grad * gain(1 + g), unit, cells_scale[g][slot]).astype(BF)
            )
        yield
        d_entry[0] += mm(normed_s[slot], query_low, TN)
        yield
        spreads = []
        for g in range(2):
            spreads.append((yield shared(reduced_lows[g], reduce_low[rows_of[g], :], NT)))
        for g in range(2):
            yield summed(d_key_value, g, cells_f[g][slot, 2].astype(BF), pairs[g])
        for g in range(2):
            if g == 0:
                order = [place_of(block) for block in range(16)]
                order = [a4 * 4 + b4 for a4, b4 in order]
            else:
                order = range(4)
            normed_grad = normed_grad + jnp.concatenate(
                [spreads[g][:, t * 128 : t * 128 + 128] for t in order], 0
            )
        yield
        for g in range(2):
            columns = (slice(None), rows_of[g])
            yield summed(d_reduce_t, columns, reduced_lows[g], patches_of(slot, g))
        unit1 = unit1_s[slot]
        add_norm(0, normed_grad, unit1)
        raw = middle_grad + normalise_back(normed_grad * gain(0), unit1, scale1_s[slot])
        restore(raw.astype(BF), input_low, slot, input_grad)
        yield

    def together(*parts):
        answers = [None] * len(parts)
        while True:
            asked = []
            for part, answer in zip(parts, answers):
                try:
                    asked.append(part.send(answer))
                except StopIteration:
                    pass
            if not asked:
                return
            answers = [None] * len(parts)
            if asked[0] is None:
                continue
            ref, place, left, right, dims = asked[0]
            left = jnp.concatenate([ask[2] for ask in asked], 0)
            if ref is None:
                whole = mm(left, right, dims)
                size = whole.shape[0] // len(asked)
                answers = [whole[n * size : (n + 1) * size] for n in range(len(asked))]
            else:
                ref[place] += mm(left, jnp.concatenate([ask[3] for ask in asked], 0), dims)

    first = PAIR * step
    together(*[attend(k, first + k) for k in range(PAIR)])

    feed()
    for k in range(PAIR):
        gather_folds(k, first + k)
    together(*[back(k, first + k) for k in range(PAIR)])

    @pl.when(step == last)
    def finish():
        gains = [hidden_filter[tap : tap + 1, :] * ROOT for tap in range(9)]
        gains[4] = gains[4] + ROOT
        for c in range(0, ff, 128):
            cols = slice(c, c + 128)
            taps = [None] * 9
            for r in range(0, 128, 64):
                weight = expand[r : r + 64, cols]
                total = None
                for column in range(3):
                    rows = slice(column * 128 + r, column * 128 + r + 64)
                    one, two = m_sum[1, rows, cols], m_sum[2, rows, cols]
                    both = (one + two) * 0.5
                    for a in range(3):
                        if a == 1:
                            part = (one - two) * 0.5
                        else:
                            part = m_sum[a // 2 * 3, rows, cols] + both
                        tap = 3 * a + column
                        row = jnp.sum(part * weight, 0, keepdims=True)
                        taps[tap] = row if taps[tap] is None else taps[tap] + row
                        part = part * gains[tap][:, cols]
                        total = part if total is None else total + part
                wide_s[0, r : r + 64, cols] = total
            for tap in range(9):
                hidden_filter[tap : tap + 1, cols] = taps[tap] * ROOT
        wide_s[1] = d_shrink_t[...]
        d_entry[1] = jnp.where(
            first_lanes, d_key_value[0, :, :128], pltpu.roll(d_key_value[0, :, 128:], 32, 1)
        )
        d_entry[2] = jnp.where(
            first_lanes, pltpu.roll(d_key_value[1, :, :128], 96, 1), d_key_value[1, :, 128:]
        )
        is_second = head[0] == 1
        d_reduce = reduce_w
        for n in range(20):
            rows = slice(n * 128, n * 128 + 128)
            d_reduce[rows, :] = d_reduce_t[:, rows].T
        top, chunk = 12 * width, ff // 256
        planes = mine.shape[1]

        def put(d, rows, first, second):
            place = (d // planes, d % planes, rows)
            mine[place] = jnp.where(is_second, second, first)
            theirs[place] = jnp.where(is_second, first, second).astype(BF)

        for d in range(devices):
            rows = slice(width * d, width * d + width)
            upper = d_reduce[20 * width * d : 20 * width * d + top, :]
            lower = jnp.concatenate(
                [d_reduce[20 * width * d + top : 20 * width * (d + 1), :]]
                + [d_entry[e, rows, :] for e in range(3)]
                + [d_mixing_t[rows, :]],
                0,
            )
            firsts = [jnp.where(left(top), upper, pltpu.roll(lower, 64, 1))]
            seconds = [jnp.where(left(top), pltpu.roll(upper, 64, 1), lower)]
            for n in range(2):
                for h, parts in enumerate((firsts, seconds)):
                    for u in range(chunk):
                        cols = slice((h * chunk + u) * 128, (h * chunk + u + 1) * 128)
                        parts.append(wide_s[n, rows, cols])
            pad = mine.shape[2] - 20 * width
            if pad:
                firsts.append(jnp.zeros((pad, 128), F32))
                seconds.append(jnp.zeros((pad, 128), F32))
            put(d, slice(None), jnp.concatenate(firsts, 0), jnp.concatenate(seconds, 0))
        count = jnp.int32(0)
        for n in range(steps):
            side = resolution[head[0] * steps + n]
            count = count + side * side * live_images[head[0] * steps + n]
        halves = [
            jnp.concatenate(
                [
                    hidden_filter[:, (h * chunk + u) * 128 : (h * chunk + u + 1) * 128]
                    for u in range(chunk)
                ],
                0,
            )
            for h in range(2)
        ]
        for ref, flip in ((small_mine, False), (small_theirs, True)):
            ref[...] = jnp.zeros_like(ref)
            ref[:8, :] = d_norm[...]
            ref[8:17, :] = d_value[...]
            ref[17:18, :] = jnp.full((1, 128), count, jnp.int32).astype(F32)
            second = jnp.logical_not(is_second) if flip else is_second
            ref[18 : 18 + 9 * chunk, :] = jnp.where(second, halves[1], halves[0])


def run_block(resolution, live_images, head, tokens, cotangent, packed, filters, norms):
    steps = tokens.shape[0] // 2
    devices, rows = packed.shape[0] // 2, packed.shape[1] - 16
    ff = 2 * (filters.shape[2] - 128)
    lines = line_of(devices)
    consts = [
        jnp.asarray(order_matrix(), BF),
        jnp.asarray(order_matrix().T, BF),
        jnp.asarray(score_bias(), F32),
        jnp.asarray(shift_masks(), F32),
    ]
    whole = [packed, filters, norms] + consts

    def all_of(a):
        return pl.BlockSpec(a.shape, lambda i, *_, n=a.ndim: (0,) * n)

    grid_in = pl.BlockSpec(
        (PAIR, 32, 32, 128), lambda i, res, live, head: (head[0] * (steps // PAIR) + i, 0, 0, 0)
    )
    grid_out = pl.BlockSpec((PAIR, 32, 32, 128), lambda i, *_: (i, 0, 0, 0))
    out_shape = [
        jax.ShapeDtypeStruct((2 * steps, 32, 32, 128), BF),
        jax.ShapeDtypeStruct((2 * steps, 32, 32, 128), F32),
        jax.ShapeDtypeStruct((steps, 32, 32, 128), BF),
        jax.ShapeDtypeStruct((lines, devices // lines, rows, 128), F32),
        jax.ShapeDtypeStruct((lines, devices // lines, rows, 128), BF),
        jax.ShapeDtypeStruct((SMALL, 128), F32),
        jax.ShapeDtypeStruct((SMALL, 128), F32),
    ]

    def kernel(*refs):
        block_kernel(*refs, steps=steps)

    return pl.pallas_call(
        kernel,
        out_shape=out_shape,
        grid_spec=pltpu.PrefetchScalarGridSpec(
            num_scalar_prefetch=3,
            grid=(steps // PAIR,),
            in_specs=[grid_in, grid_in] + [all_of(a) for a in whole],
            out_specs=[grid_in, grid_in, grid_out] + [all_of(a) for a in out_shape[3:]],
            scratch_shapes=[
                pltpu.VMEM((3, 128, 128), BF),
                pltpu.VMEM((128, 128), BF),
                pltpu.VMEM((128, ff), F32),
                pltpu.VMEM((128, ff), BF),
                pltpu.VMEM((2560, 128), F32),
                pltpu.VMEM((9, 128), F32),
                pltpu.VMEM((9, ff), F32),
                pltpu.VMEM((2, 128, ff), F32),
                pltpu.VMEM((4, 128, 128), F32),
                pltpu.VMEM((3, 128, 128), F32),
                pltpu.VMEM((128, 128), F32),
                pltpu.VMEM((128, ff), F32),
                pltpu.VMEM((128, 2560), F32),
                pltpu.VMEM((8, 128), F32),
                pltpu.VMEM((9, 128), F32),
                pltpu.VMEM((4, 384, ff), BF),
                pltpu.VMEM((2, 128, 256), BF),
                pltpu.VMEM((4, PAIR * 512, ff), BF),
                pltpu.VMEM((4, 384, ff), F32),
                pltpu.VMEM((4, PAIR * 512, 384), F32),
                pltpu.VMEM((2, 128, 256), F32),
                pltpu.VMEM((2560, 128), BF),
                pltpu.VMEM((4, PAIR * 512, 384), BF),
                pltpu.VMEM((4, 384, PAIR * 512), BF),
                pltpu.VMEM((2, 1024, 128), F32),
                pltpu.VMEM((2, 1024, 128), BF),
                pltpu.VMEM((2, 1024, 128), F32),
                pltpu.VMEM((2, 1024, 1), F32),
                pltpu.VMEM((2, 1024, 128), F32),
                pltpu.VMEM((2, 1024, 1), F32),
                pltpu.VMEM((2, 1024, 128), BF),
                pltpu.VMEM((2, 1024, 128), BF),
                pltpu.VMEM((2, 1024, 128), BF),
                pltpu.VMEM((2, 4, 160, 256), F32),
                pltpu.VMEM((2, 4, 160, 128), BF),
                pltpu.VMEM((2, 4, 160, 128), BF),
                pltpu.VMEM((2, 80, 512), F32),
                pltpu.VMEM((2, 3, 64, 128), F32),
                pltpu.VMEM((2, 64, 1), F32),
                pltpu.VMEM((2, 3, 256, 128), F32),
                pltpu.VMEM((2, 256, 1), F32),
                pltpu.VMEM((2, 1024, 128), F32),
                pltpu.VMEM((1, 128), F32),
            ],
        ),
        compiler_params=pltpu.CompilerParams(
            dimension_semantics=("arbitrary",), vmem_limit_bytes=LIMIT
        ),
        name="block",
    )(resolution, live_images, head, tokens, cotangent, *whole)


def line_of(devices):
    return 4 if devices % 4 == 0 else 1


def rows_of_block(devices):
    return -(-20 * (128 // devices) // 16) * 16


def pack(
    head,
    resolution,
    live_images,
    entry,
    mixing_t,
    expand,
    shrink_t,
    reduce_t,
    values,
    hidden,
    block,
    filters,
    held,
):
    width, ff = expand.shape
    top, chunk = 12 * width, ff // 128
    held[...] = jnp.zeros_like(held)
    rows = reduce_t[...].T
    held[:top, :64] = rows[:top, :]
    held[: 8 * width, 64:] = rows[top:, :]
    for e in range(3):
        held[(8 + e) * width : (9 + e) * width, 64:] = entry[e]
    held[11 * width : top, 64:] = mixing_t[...]
    for u in range(chunk):
        cols = slice(u * 128, (u + 1) * 128)
        held[top + u * width : top + (u + 1) * width, :] = expand[:, cols]
        held[top + (chunk + u) * width : top + (chunk + u + 1) * width, :] = shrink_t[:, cols]
    half = live_images.shape[0] // 2
    count = jnp.int32(0)
    for n in range(half):
        side = resolution[head * half + n]
        count = count + side * side * live_images[head * half + n]
    count = count // 64
    last = held.shape[0] - 16
    held[last : last + 1, :] = jnp.full((1, 128), count % 256, jnp.int32).astype(F32)
    held[last + 1 : last + 2, :] = jnp.full((1, 128), count // 256, jnp.int32).astype(F32)
    block[...] = held[...].astype(BF)
    filters[...] = jnp.zeros_like(filters)
    filters[:9, :ff] = hidden[...]
    for g in range(2):
        filters[:9, ff + 32 * g : ff + 32 * g + 32] = values[:, g]


def greet(peers, meanwhile=None):
    barrier = pltpu.get_barrier_semaphore()
    for peer in peers:
        pl.semaphore_signal(barrier, inc=1, device_id=peer, device_id_type=MESH)
    if meanwhile is not None:
        meanwhile()
    pl.semaphore_wait(barrier, len(peers))


def places(devices):
    lines = line_of(devices)
    planes = devices // lines
    me, head = lax.axis_index("dp"), lax.axis_index("head")
    z, p = me // planes, me % planes
    line_peers = [((z + k) % lines) for k in range(1, lines)]
    plane_peers = [((p + k) % planes) for k in range(1, planes)]
    return lines, planes, z, p, head, line_peers, plane_peers


def gather_kernel(
    devices,
    resolution,
    live_images,
    entry,
    mixing_t,
    expand,
    shrink_t,
    reduce_t,
    values,
    hidden,
    blocks,
    both,
    block,
    filters,
    held,
    send_sem,
    recv_sem,
    filter_sem,
    local_sem,
):
    lines, planes, z, p, head, line_peers, plane_peers = places(devices)

    def slot(line, plane, core):
        return (line * planes + plane) * 2 + core

    def at(line, plane, core):
        return (line * planes + plane, core)

    sibling = at(z, p, 1 - head)
    greet(
        [at(k, p, head) for k in line_peers] + [at(z, k, head) for k in plane_peers] + [sibling],
        lambda: pack(
            head,
            resolution,
            live_images,
            entry,
            mixing_t,
            expand,
            shrink_t,
            reduce_t,
            values,
            hidden,
            block,
            filters,
            held,
        ),
    )
    sends = []

    def send(source, index, target):
        copy = pltpu.make_async_remote_copy(
            src_ref=source,
            dst_ref=blocks.at[index],
            send_sem=send_sem.at[len(sends)],
            recv_sem=recv_sem.at[index],
            device_id=target,
            device_id_type=MESH,
        )
        copy.start()
        sends.append(copy)

    def arrived(index):
        pltpu.make_async_remote_copy(
            src_ref=block,
            dst_ref=blocks.at[index],
            send_sem=send_sem.at[0],
            recv_sem=recv_sem.at[index],
            device_id=sibling,
            device_id_type=MESH,
        ).wait_recv()

    own = slot(z, p, head)
    for k in line_peers:
        send(block, own, at(k, p, head))
    for k in plane_peers:
        send(block, own, at(z, k, head))
    send(block, own, sibling)
    swap = pltpu.make_async_remote_copy(
        src_ref=filters,
        dst_ref=both.at[head],
        send_sem=filter_sem.at[0],
        recv_sem=filter_sem.at[1],
        device_id=sibling,
        device_id_type=MESH,
    )
    swap.start()
    keep = [
        pltpu.make_async_copy(block, blocks.at[own], local_sem.at[0]),
        pltpu.make_async_copy(filters, both.at[head], local_sem.at[1]),
    ]
    for copy in keep:
        copy.start()
    for k in line_peers:
        index = slot(k, p, head)
        arrived(index)
        for j in plane_peers:
            send(blocks.at[index], index, at(z, j, head))
        send(blocks.at[index], index, sibling)
    for line in [z] + line_peers:
        for j in plane_peers:
            index = slot(line, j, head)
            arrived(index)
            send(blocks.at[index], index, sibling)
    for line in [z] + line_peers:
        for j in [p] + plane_peers:
            arrived(slot(line, j, 1 - head))
    for copy in sends:
        copy.wait_send()
    swap.wait_send()
    pltpu.make_async_remote_copy(
        src_ref=filters,
        dst_ref=both.at[1 - head],
        send_sem=filter_sem.at[0],
        recv_sem=filter_sem.at[1],
        device_id=sibling,
        device_id_type=MESH,
    ).wait_recv()
    for copy in keep:
        copy.wait()


def run_gather(devices, resolution, live_images, *weights):
    lines = line_of(devices)
    planes = devices // lines
    copies = (lines - 1) + lines * (planes - 1) + lines * planes
    rows = rows_of_block(devices) + 16
    filters = (16, weights[-1].shape[1] + 128)
    smem = pl.BlockSpec(memory_space=pltpu.SMEM)
    vmem = pl.BlockSpec(memory_space=pltpu.VMEM)

    def kernel(*refs):
        gather_kernel(devices, *refs)

    return pl.pallas_call(
        kernel,
        out_shape=[
            jax.ShapeDtypeStruct((2 * devices, rows, 128), BF),
            jax.ShapeDtypeStruct((2,) + filters, F32),
        ],
        in_specs=[smem] * 2 + [vmem] * len(weights),
        out_specs=[pl.BlockSpec(memory_space=pl.ANY)] * 2,
        scratch_shapes=[
            pltpu.VMEM((rows, 128), BF),
            pltpu.VMEM(filters, F32),
            pltpu.VMEM((rows, 128), F32),
            pltpu.SemaphoreType.DMA((copies,)),
            pltpu.SemaphoreType.DMA((2 * devices,)),
            pltpu.SemaphoreType.DMA((2,)),
            pltpu.SemaphoreType.DMA((2,)),
        ],
        compiler_params=pltpu.CompilerParams(
            collective_id=0, has_side_effects=True, vmem_limit_bytes=LIMIT
        ),
        name="gather",
    )(resolution, live_images, *weights)


def reduce_kernel(
    devices,
    mine_far,
    theirs,
    small_mine,
    small_theirs,
    out_half,
    input_half,
    grad,
    small,
    out_other,
    input_other,
    mine,
    core_in,
    core_small,
    plane_out,
    plane_in,
    plane_small,
    line_out,
    line_in,
    line_small,
    core_send,
    core_recv,
    plane_send,
    plane_recv,
    line_send,
    line_recv,
    local_sem,
):
    lines, planes, z, p, head, line_peers, plane_peers = places(devices)
    half = input_half.shape[0]
    fetch = pltpu.make_async_copy(mine_far, mine, local_sem.at[0])
    fetch.start()

    def at(line, plane, core):
        return (line * planes + plane, core)

    sibling = at(z, p, 1 - head)
    greet(
        [at(k, p, head) for k in line_peers] + [at(z, k, head) for k in plane_peers] + [sibling]
    )

    def remote(source, target, send, recv, device):
        return pltpu.make_async_remote_copy(
            src_ref=source,
            dst_ref=target,
            send_sem=send,
            recv_sem=recv,
            device_id=device,
            device_id_type=MESH,
        )

    started = []

    def go(*args):
        copy = remote(*args)
        copy.start()
        started.append(copy)

    order = line_peers + [z]
    go(small_theirs, core_small, core_send.at[lines], core_recv.at[lines], sibling)
    for a in order:
        go(theirs.at[a], core_in.at[a], core_send.at[a], core_recv.at[a], sibling)
    remote(
        small_theirs, core_small, core_send.at[lines], core_recv.at[lines], sibling
    ).wait_recv()
    plane_small[pl.ds(p, 1)] = (small_mine[...] + core_small[...])[None]
    for n, k in enumerate(plane_peers):
        go(
            plane_small.at[p],
            plane_small.at[p],
            plane_send.at[lines * (planes - 1) + n],
            plane_recv.at[lines * planes + p],
            at(z, k, head),
        )
    fetch.wait()
    for m, a in enumerate(order):
        remote(
            theirs.at[a], core_in.at[a], core_send.at[a], core_recv.at[a], sibling
        ).wait_recv()
        both = mine[pl.ds(a, 1)] + core_in[pl.ds(a, 1)].astype(F32)
        plane_out[pl.ds(a, 1)] = both.astype(BF)
        for n, k in enumerate(plane_peers):
            go(
                plane_out.at[a, k],
                plane_in.at[a, p],
                plane_send.at[m * (planes - 1) + n],
                plane_recv.at[a * planes + p],
                at(z, k, head),
            )
    own_out = out_half.at[pl.ds(head * half, half)]
    go(own_out, out_other, core_send.at[lines + 1], core_recv.at[lines + 1], sibling)
    go(input_half, input_other, core_send.at[lines + 2], core_recv.at[lines + 2], sibling)
    for k in plane_peers:
        remote(
            plane_small.at[p],
            plane_small.at[k],
            plane_send.at[0],
            plane_recv.at[lines * planes + k],
            sibling,
        ).wait_recv()
    part = plane_small[0]
    for k in range(1, planes):
        part = part + plane_small[k]
    line_small[pl.ds(z, 1)] = part[None]
    for n, k in enumerate(line_peers):
        go(
            line_small.at[z],
            line_small.at[z],
            line_send.at[lines + n],
            line_recv.at[lines + z],
            at(k, p, head),
        )
    own = None
    for m, a in enumerate(order):
        total = (
            mine[pl.ds(a, 1), pl.ds(p, 1)] + core_in[pl.ds(a, 1), pl.ds(p, 1)].astype(F32)
        )[0, 0]
        for k in plane_peers:
            remote(
                plane_out.at[a, k],
                plane_in.at[a, k],
                plane_send.at[0],
                plane_recv.at[a * planes + k],
                sibling,
            ).wait_recv()
            total = total + plane_in[pl.ds(a, 1), pl.ds(k, 1)][0, 0].astype(F32)
        if m < lines - 1:
            line_out[pl.ds(a, 1)] = total.astype(BF)[None]
            go(line_out.at[a], line_in.at[z], line_send.at[m], line_recv.at[z], at(a, p, head))
        else:
            own = total
    for k in line_peers:
        remote(
            line_out.at[k], line_in.at[k], line_send.at[0], line_recv.at[k], sibling
        ).wait_recv()
        own = own + line_in[pl.ds(k, 1)][0].astype(F32)
    grad[...] = own
    for k in line_peers:
        remote(
            line_small.at[z],
            line_small.at[k],
            line_send.at[0],
            line_recv.at[lines + k],
            sibling,
        ).wait_recv()
    part = line_small[0]
    for k in range(1, lines):
        part = part + line_small[k]
    small[...] = part
    remote(
        own_out, out_other, core_send.at[lines + 1], core_recv.at[lines + 1], sibling
    ).wait_recv()
    remote(
        input_half, input_other, core_send.at[lines + 2], core_recv.at[lines + 2], sibling
    ).wait_recv()
    for copy in started:
        copy.wait_send()


def run_reduce(devices, mine, theirs, small_mine, small_theirs, out_half, input_half):
    lines, planes, rows = mine.shape[:3]
    anywhere = pl.BlockSpec(memory_space=pl.ANY)
    vmem = pl.BlockSpec(memory_space=pltpu.VMEM)
    sem = pltpu.SemaphoreType.DMA

    def kernel(*refs):
        reduce_kernel(devices, *refs)

    return pl.pallas_call(
        kernel,
        out_shape=[
            jax.ShapeDtypeStruct((rows, 128), F32),
            jax.ShapeDtypeStruct((SMALL, 128), F32),
            jax.ShapeDtypeStruct(input_half.shape, BF),
            jax.ShapeDtypeStruct(input_half.shape, BF),
        ],
        in_specs=[anywhere] * 2 + [vmem] * 2 + [anywhere] * 2,
        out_specs=[vmem] * 2 + [anywhere] * 2,
        scratch_shapes=[
            pltpu.VMEM((lines, planes, rows, 128), F32),
            pltpu.VMEM((lines, planes, rows, 128), BF),
            pltpu.VMEM((SMALL, 128), F32),
            pltpu.VMEM((lines, planes, rows, 128), BF),
            pltpu.VMEM((lines, planes, rows, 128), BF),
            pltpu.VMEM((planes, SMALL, 128), F32),
            pltpu.VMEM((lines, rows, 128), BF),
            pltpu.VMEM((lines, rows, 128), BF),
            pltpu.VMEM((lines, SMALL, 128), F32),
            sem((lines + 3,)),
            sem((lines + 3,)),
            sem((lines * (planes - 1) + planes,)),
            sem((lines * planes + planes,)),
            sem((2 * lines,)),
            sem((2 * lines,)),
            sem((1,)),
        ],
        compiler_params=pltpu.CompilerParams(
            collective_id=1, has_side_effects=True, vmem_limit_bytes=LIMIT
        ),
        name="reduce",
    )(mine, theirs, small_mine, small_theirs, out_half, input_half)


def advance(weight, moment, average, gradient, step_rate, weight_decay):
    gradient = gradient + weight_decay * weight
    moment = 0.9 * moment + gradient
    weight = weight - step_rate * (gradient + 0.9 * moment)
    return (moment, weight, 0.8 * average + 0.2 * weight)


RATES = (0.3, 0.12, 0.12, 0.03, 0.1, 0.2, 0.4, 0.5)


def update_kernel(head, *refs, tokens_all):
    out_other, in_other, grad, small = refs[:4]
    state = refs[6:30]
    output, input_grad = refs[30:32]
    results = refs[32:]
    step = pl.program_id(0)
    factor = tokens_all / small[17:18, :]
    output[...] = out_other[...]
    input_grad[...] = in_other[...].astype(F32) * factor

    @pl.when(step == 0)
    def update():
        width, ff = state[6].shape
        top, chunk = 12 * width, ff // 128
        rate_unit = tokens_all**-0.5

        def apply(n, place, raw, scale):
            new = advance(
                state[3 * n][place],
                state[3 * n + 1][place],
                state[3 * n + 2][place],
                scale * raw,
                RATES[n] * rate_unit,
                0.0 if n == 5 else 0.05,
            )
            for k in range(3):
                results[3 * n + k][place] = new[k]

        scale = factor[:, :64]
        for e in range(3):
            apply(0, e, grad[(8 + e) * width : (9 + e) * width, 64:], scale)
        apply(1, Ellipsis, grad[11 * width : top, 64:], scale)
        for u in range(chunk):
            cols = slice(u * 128, (u + 1) * 128)
            apply(2, (slice(None), cols), grad[top + u * width : top + (u + 1) * width, :], factor)
            apply(
                3,
                (slice(None), cols),
                grad[top + (chunk + u) * width : top + (chunk + u + 1) * width, :],
                factor,
            )
        turned = grad[:top, :].T
        apply(4, (slice(None), slice(0, top)), turned[:64, :], factor[:, :1])
        apply(4, (slice(None), slice(top, 20 * width)), turned[64:, : 8 * width], factor[:, :1])
        for n in range(2):
            apply(5, n, small[4 * n : 4 * n + 4, :], factor)
        values = small[8:17, :]
        values = jnp.where(head[0] == 1, pltpu.roll(values, 64, 1), values)
        for g in range(2):
            apply(6, (slice(None), g), values[:, 32 * g : 32 * g + 32], factor[:, :32])
        for u in range(chunk):
            apply(
                7,
                (slice(None), slice(u * 128, (u + 1) * 128)),
                small[18 + 9 * u : 27 + 9 * u, :],
                factor,
            )


def run_update(tokens_all, head, output, input_grad, out_other, in_other, grad, small, state):
    half = out_other.shape[0]
    steps = 2

    def all_of(a):
        return pl.BlockSpec(a.shape, lambda i, *_, n=a.ndim: (0,) * n)

    block = (half // steps,) + out_other.shape[1:]
    other = pl.BlockSpec(block, lambda i, *_: (i, 0, 0, 0))
    final = pl.BlockSpec(block, lambda i, head: ((1 - head[0]) * steps + i, 0, 0, 0))
    anywhere = pl.BlockSpec(memory_space=pl.ANY)

    def kernel(*refs):
        update_kernel(*refs, tokens_all=tokens_all)

    return pl.pallas_call(
        kernel,
        out_shape=[jax.ShapeDtypeStruct(a.shape, a.dtype) for a in (output, input_grad, *state)],
        grid_spec=pltpu.PrefetchScalarGridSpec(
            num_scalar_prefetch=1,
            grid=(steps,),
            in_specs=[other, other, all_of(grad), all_of(small), anywhere, anywhere]
            + [all_of(a) for a in state],
            out_specs=[final, final] + [all_of(a) for a in state],
        ),
        input_output_aliases={5: 0, 6: 1},
        compiler_params=pltpu.CompilerParams(
            dimension_semantics=("arbitrary",), vmem_limit_bytes=LIMIT
        ),
        name="update",
    )(head, out_other, in_other, grad, small, output, input_grad, *state)


def per_device(
    tokens,
    cotangent,
    resolution,
    live_images,
    entry_weight,
    entry_momentum,
    entry_average,
    mixing_weight,
    mixing_momentum,
    mixing_average,
    expand_weight,
    expand_momentum,
    expand_average,
    shrink_weight,
    shrink_momentum,
    shrink_average,
    reduce_weight,
    reduce_momentum,
    reduce_average,
    norm_params,
    norm_momentum,
    norm_average,
    value_filter,
    value_momentum,
    value_average,
    hidden_filter,
    hidden_momentum,
    hidden_average,
):
    devices = lax.axis_size("dp")
    head = lax.axis_index("head").reshape(1).astype(jnp.int32)
    turns = ((1, 0), (1, 0), (1, 0), (1, 0, 2))
    mixing, shrink, reduced, values = [
        tuple(a.transpose(turn) for a in arrays)
        for turn, arrays in zip(
            turns,
            (
                (mixing_weight, mixing_momentum, mixing_average),
                (shrink_weight, shrink_momentum, shrink_average),
                (reduce_weight, reduce_momentum, reduce_average),
                (value_filter, value_momentum, value_average),
            ),
        )
    ]
    blocks, filters = run_gather(
        devices,
        resolution,
        live_images,
        entry_weight,
        mixing[0],
        expand_weight,
        shrink[0],
        reduced[0],
        values[0],
        hidden_filter,
    )
    output, input_grad, input_low, mine, theirs, small_mine, small_theirs = run_block(
        resolution, live_images, head, tokens, cotangent, blocks, filters, norm_params
    )
    grad, small, out_other, input_other = run_reduce(
        devices, mine, theirs, small_mine, small_theirs, output, input_low
    )
    state = (
        entry_weight,
        entry_momentum,
        entry_average,
        *mixing,
        expand_weight,
        expand_momentum,
        expand_average,
        *shrink,
        *reduced,
        norm_params,
        norm_momentum,
        norm_average,
        *values,
        hidden_filter,
        hidden_momentum,
        hidden_average,
    )
    tokens_all = devices * tokens.shape[0] * tokens.shape[1] * tokens.shape[2]
    results = list(
        run_update(
            tokens_all, head, output, input_grad, out_other, input_other, grad, small, state
        )
    )
    for n, turn in zip((1, 3, 4, 6), turns):
        for k in range(2 + 3 * n, 5 + 3 * n):
            results[k] = results[k].transpose(turn)
    return tuple(results)


def solution(mesh):
    in_specs = (
        P("dp", None, None, None),
        P("dp", None, None, None),
        P("dp"),
        P("dp"),
        P(None, "dp", "head"),
        P(None, "dp", "head"),
        P(None, "dp", "head"),
        P("head", "dp"),
        P("head", "dp"),
        P("head", "dp"),
        P("dp", "head"),
        P("dp", "head"),
        P("dp", "head"),
        P("head", "dp"),
        P("head", "dp"),
        P("head", "dp"),
        P("dp", "head"),
        P("dp", "head"),
        P("dp", "head"),
        P(),
        P(),
        P(),
        P(None, None, "head"),
        P(None, None, "head"),
        P(None, None, "head"),
        P(None, "head"),
        P(None, "head"),
        P(None, "head"),
    )
    out_specs = (
        P("dp", None, None, None),
        P("dp", None, None, None),
        P(None, "dp", "head"),
        P(None, "dp", "head"),
        P(None, "dp", "head"),
        P("head", "dp"),
        P("head", "dp"),
        P("head", "dp"),
        P("dp", "head"),
        P("dp", "head"),
        P("dp", "head"),
        P("head", "dp"),
        P("head", "dp"),
        P("head", "dp"),
        P("dp", "head"),
        P("dp", "head"),
        P("dp", "head"),
        P(),
        P(),
        P(),
        P(None, None, "head"),
        P(None, None, "head"),
        P(None, None, "head"),
        P(None, "head"),
        P(None, "head"),
        P(None, "head"),
    )
    return jax.shard_map(
        per_device, mesh=mesh, in_specs=in_specs, out_specs=out_specs, check_vma=False
    )
```

```python
import math

import jax
import jax.numpy as jnp
import numpy as np
from jax import lax
from jax.experimental import pallas as pl
from jax.experimental.pallas import tpu as pltpu
from jax.sharding import PartitionSpec as P

BF = jnp.bfloat16
F32 = jnp.float32
EPSILON = 1e-06
HALF = 16
MASKED = -1e9
NN = (((1,), (0,)), ((), ()))
NT = (((1,), (1,)), ((), ()))
TN = (((0,), (0,)), ((), ()))
MESH = pl.DeviceIdType.MESH
SMALL = 64
PAIR = 2
LIMIT = 60 * 1024 * 1024
ROOT = math.sqrt(0.5)


def mm(a, b, dims=NN):
    return lax.dot_general(a, b, dims, preferred_element_type=F32)


def block_of(a4, b4):
    return (a4 % 2) * 8 + (b4 % 2) * 4 + (a4 // 2) * 2 + b4 // 2


def place_of(block):
    return ((block >> 1) & 1) * 2 + (block >> 3), (block & 1) * 2 + ((block >> 2) & 1)


def order_matrix():
    perm = np.zeros((256, 256), np.float32)
    for block in range(16):
        a4, b4 = place_of(block)
        for ci in range(4):
            for ck in range(4):
                perm[block * 16 + ci * 4 + ck, (4 * ci + a4) * HALF + 4 * ck + b4] = 1
    return perm


def score_bias():
    rows = np.array([(n % 16) for _ in range(2) for n in list(range(16)) + list(range(64))])
    cols = np.arange(256) % 16

    def image(n):
        return (n // 8) * 2 + (n % 4) // 2

    return np.where(image(rows)[:, None] == image(cols)[None, :], 0.0, MASKED).astype(np.float32)


def shift_masks():
    masks = np.zeros((2, 4, 16, 128), np.float32)
    for fine in range(2):
        for ci in range(4):
            for ck in range(4):
                row = ci * 4 + ck
                for n, (d, e) in enumerate(((1, 0), (-1, 0), (0, 1), (0, -1))):
                    ni, nk = ci + d, ck + e
                    ok = 0 <= ni < 4 and 0 <= nk < 4
                    if fine:
                        ok = ok and ni // 2 == ci // 2 and nk // 2 == ck // 2
                    masks[fine, n, row] = ok
    return masks


def normalise(x):
    centred = x - jnp.mean(x, -1, keepdims=True)
    scale = lax.rsqrt(jnp.mean(centred * centred, -1, keepdims=True) + EPSILON)
    return centred * scale, scale


def normalise_back(grad, unit, scale):
    return scale * (
        grad
        - jnp.mean(grad, -1, keepdims=True)
        - unit * jnp.mean(grad * unit, -1, keepdims=True)
    )


def gelu_pair(h):
    below = 0.5 + 0.5 * lax.erf(h * math.sqrt(0.5))
    density = jnp.exp2(h * h * (-0.5 * math.log2(math.e)))
    return h * below, below + h * density * (1.0 / math.sqrt(2 * math.pi))


def scaled_gelu_pair(u):
    below = math.sqrt(0.5) + math.sqrt(0.5) * lax.erf(u)
    density = jnp.exp2(u * u * (-math.log2(math.e)))
    return u * below, below + u * density * (2.0 / math.sqrt(2 * math.pi))


def block_kernel(
    resolution,
    live_images,
    head,
    tokens,
    cotangent,
    packed,
    filters,
    norms,
    perm,
    perm_t,
    bias,
    edge,
    out,
    input_grad,
    input_low,
    mine,
    theirs,
    small_mine,
    small_theirs,
    factor,
    entry,
    mixing_t,
    expand,
    shrink_t,
    reduce_w,
    value_filter,
    hidden_filter,
    wide_s,
    square_s,
    d_entry,
    d_mixing_t,
    d_shrink_t,
    d_reduce_t,
    d_norm,
    d_value,
    conv_w,
    key_value_w,
    g_low,
    m_sum,
    folds,
    d_key_value,
    reduce_low,
    rows_in,
    rows_in_t,
    middle_s,
    up_s,
    unit1_s,
    scale1_s,
    unit2_s,
    scale2_s,
    normed_s,
    queries_s,
    mixed_s,
    probs,
    keys_s,
    enhanced_s,
    values_s,
    wide_cells,
    wide_scale,
    narrow_cells,
    narrow_scale,
    second_grad_s,
    factor_s,
    *,
    steps,
):
    step = pl.program_id(0)
    last = pl.num_programs(0) - 1
    first_grid = head[0] * steps
    devices = packed.shape[0] // 2
    width = 128 // devices
    ff = expand.shape[1]
    lane = lax.broadcasted_iota(jnp.int32, (128, 128), 1)
    first_lanes = lane % 64 < 32

    def left(rows):
        return lax.broadcasted_iota(jnp.int32, (rows, 128), 1) < 64

    @pl.when(step == 0)
    def prepare():
        top, chunk = 12 * width, ff // 256
        counts = jnp.zeros((1, 128), F32)
        last_rows = packed.shape[1] - 16
        for n in range(2 * devices):
            pair = packed[n, last_rows : last_rows + 16, :].astype(F32)
            counts = counts + (pair[:1] + 256.0 * pair[1:2])
        factor_s[...] = (devices * 2 * steps * 1024 / 64) / counts
        factor[...] = jnp.broadcast_to(factor_s[...], factor.shape)
        for d in range(devices):
            one, two = [packed[2 * d + h].astype(F32) for h in range(2)]
            mask = left(top)
            reduce_w[20 * width * d : 20 * width * d + top, :] = jnp.where(
                mask, one[:top], pltpu.roll(two[:top], 64, 1)
            )
            rest = jnp.where(mask, pltpu.roll(one[:top], 64, 1), two[:top])
            reduce_w[20 * width * d + top : 20 * width * (d + 1), :] = rest[: 8 * width]
            rows = slice(width * d, width * d + width)
            for e in range(4):
                square_s[e, rows, :] = rest[(8 + e) * width : (9 + e) * width]
            for h, part in enumerate((one, two)):
                for u in range(chunk):
                    cols = slice((h * chunk + u) * 128, (h * chunk + u + 1) * 128)
                    wide_s[0, rows, cols] = part[top + u * width : top + (u + 1) * width]
                    wide_s[1, rows, cols] = part[
                        top + (chunk + u) * width : top + (chunk + u + 1) * width
                    ]
        reduce_low[...] = reduce_w[...].astype(BF)
        entry[...] = square_s[:3].astype(BF)
        mixing_t[...] = square_s[3].astype(BF)
        expand[...] = wide_s[0]
        shrink_t[...] = wide_s[1].astype(BF)
        for h in range(2):
            hidden_filter[:, h * (ff // 2) : (h + 1) * (ff // 2)] = filters[h, :9, : ff // 2]
        value_filter[...] = jnp.where(
            left(9),
            filters[0, :9, ff // 2 :],
            pltpu.roll(filters[1, :9, ff // 2 :], 64, 1),
        )
        for column in range(3):
            top, mid, low = [
                hidden_filter[3 * a + column : 3 * a + column + 1, :] * ROOT for a in range(3)
            ]
            if column == 1:
                mid = mid + ROOT
            rows = slice(column * 128, column * 128 + 128)
            for n, gain in enumerate(
                (top, 0.5 * (top + mid + low), 0.5 * (top - mid + low), low)
            ):
                conv_w[n, rows, :] = (expand[...] * gain).astype(BF)
        for g in range(2):
            w = entry[1 + g].astype(F32)
            if g == 0:
                keys, vals = w, pltpu.roll(w, 96, 1)
                keep = first_lanes
            else:
                keys, vals = pltpu.roll(w, 32, 1), w
                keep = jnp.logical_not(first_lanes)
            key_value_w[g, :, :128] = jnp.where(keep, keys, 0.0).astype(BF)
            key_value_w[g, :, 128:] = jnp.where(keep, vals, 0.0).astype(BF)
        for ref in (d_entry, d_mixing_t, d_shrink_t, d_reduce_t, d_norm, d_value, m_sum, d_key_value):
            ref[...] = jnp.zeros_like(ref)

    def ordered(ref, place):
        parts = [
            ref[place, a * 16 : a * 16 + 16, b * 16 : b * 16 + 16, :].reshape(256, 128)
            for a in range(2)
            for b in range(2)
        ]
        rows = mm(perm[...], jnp.concatenate(parts, 1))
        return jnp.stack(
            [rows[:, q * 128 : q * 128 + 128].reshape(16, 16, 128) for q in range(4)], 1
        ).reshape(1024, 128)

    def restore(value, ref, place, wide=None):
        blocks = value.reshape(16, 4, 16, 128)
        rows = mm(
            perm_t[...],
            jnp.concatenate([blocks[:, q].reshape(256, 128) for q in range(4)], 1),
        )
        for q in range(4):
            a, b = q // 2, q % 2
            index = (pl.ds(place, 1), slice(a * 16, a * 16 + 16), slice(b * 16, b * 16 + 16))
            part = rows[:, q * 128 : q * 128 + 128]
            ref[index] = part.astype(BF).reshape(1, 16, 16, 128)
            if wide is not None:
                wide[index] = (part * factor_s[...]).reshape(1, 16, 16, 128)

    def of_quadrant(value, q, blocks):
        return value.reshape(blocks, 4, 16, 128)[:, q].reshape(blocks * 16, 128)

    def of_quadrants(parts, blocks):
        return jnp.stack([p.reshape(blocks, 16, 128) for p in parts], 1).reshape(
            blocks * 64, 128
        )

    def gain(n):
        return norms[0, n : n + 1, :]

    def shift_by(n):
        return norms[1, n : n + 1, :]

    def add_norm(n, grad, unit):
        d_norm[n : n + 1, :] += jnp.sum(grad * unit, 0, keepdims=True)
        d_norm[4 + n : 5 + n, :] += jnp.sum(grad, 0, keepdims=True)

    lane80 = lax.broadcasted_iota(jnp.int32, (80, 128), 1)
    zero80 = jnp.zeros((80, 128), BF)
    segments = ((0, 16), (16, 80), (80, 96), (96, 160))
    scaling = 32**-0.5
    rows_of = (slice(0, 2048), slice(2048, 2560))
    cells_f = (wide_cells, narrow_cells)
    cells_scale = (wide_scale, narrow_scale)

    def fine_of(grid):
        return (resolution[first_grid + grid] == 8).astype(jnp.int32)

    def patches_of(slot, g):
        if g == 0:
            blocks = [block_of(t // 4, t % 4) for t in range(16)]
            parts = [normed_s[slot, b * 64 : b * 64 + 64, :] for b in blocks]
        else:
            parts = [normed_s[slot, t * 256 : t * 256 + 256, :] for t in range(4)]
        return jnp.concatenate(parts, 1)

    def move(value, fine, rows, columns):
        size = value.shape[0]
        if rows:
            n = 0 if rows > 0 else 1
            value = pltpu.roll(value, (-4 * rows) % size, 0)
            value = (
                value.reshape(size // 16, 16, 128) * edge[pl.ds(fine, 1), n : n + 1][0]
            ).reshape(size, 128)
        if columns:
            n = 2 if columns > 0 else 3
            value = pltpu.roll(value, (-columns) % size, 0)
            value = (
                value.reshape(size // 16, 16, 128) * edge[pl.ds(fine, 1), n : n + 1][0]
            ).reshape(size, 128)
        return value

    def cell_moves(value, fine):
        masks = [
            jnp.concatenate([edge[pl.ds(fine, 1), n : n + 1][0, 0]] * 4, 1) for n in range(4)
        ]
        made = {}

        def of(source, rows, columns):
            if (source, rows, columns) not in made:
                part = value[source * 16 : source * 16 + 16]
                if rows:
                    part = pltpu.roll(part, (-4 * rows) % 16, 0) * masks[0 if rows > 0 else 1]
                if columns:
                    part = pltpu.roll(part, -columns % 16, 0) * masks[2 if columns > 0 else 3]
                made[source, rows, columns] = part
            return made[source, rows, columns]

        moved = []
        for tap in range(9):
            down, across = tap // 3 - 1, tap % 3 - 1
            blocks = [of(0, down, across)]
            for a in range(2):
                for b in range(2):
                    na, nb = a + down, b + across
                    blocks.append(of(1 + na % 2 * 2 + nb % 2, na // 2, nb // 2))
            moved.append(blocks)
        return moved

    def wrap(a4, d):
        return (a4 + d) % 4, (a4 + d) // 4

    def shared(rows, weight, dims=NN):
        return None, None, rows, weight, dims

    def summed(ref, place, left, right):
        return ref, place, left, right, TN

    def attend(slot, grid):
        fine = fine_of(grid)
        alive = live_images[first_grid + grid]
        x = ordered(tokens, slot)
        yield
        raised = ordered(cotangent, slot)
        yield
        unit1, scale1 = normalise(x)
        unit1_s[slot] = unit1
        scale1_s[slot] = scale1
        yield
        normed = (unit1 * gain(0) + shift_by(0)).astype(BF)
        normed_s[slot] = normed
        yield
        reduced = []
        for g in range(2):
            reduced.append((yield shared(patches_of(slot, g), reduce_low[rows_of[g], :])))
        queries_s[slot] = mm(normed, entry[0]).astype(BF)
        yield
        cells = [normalise(reduced[g]) for g in range(2)]
        yield
        row16 = lax.broadcasted_iota(jnp.int32, (16, 128), 0)
        within = (row16 // 8) * 4 + (row16 % 4) // 2
        live = jnp.stack(
            [
                jnp.where(
                    jnp.where(fine == 1, within + (q // 2) * 8 + (q % 2) * 2, q) < alive, 1.0, 0.0
                )
                for q in range(4)
            ],
            0,
        )
        up_s[slot] = (raised.reshape(16, 4, 16, 128) * live[None]).reshape(1024, 128).astype(BF)
        yield
        acts = []
        for g in range(2):
            unit, scale = cells[g]
            act, slope = gelu_pair(unit * gain(1 + g) + shift_by(1 + g))
            cells_f[g][slot, 0] = unit
            cells_f[g][slot, 1] = slope
            cells_f[g][slot, 2] = act
            cells_scale[g][slot] = scale
            acts.append(act.astype(BF))
        yield
        pairs = []
        for g in range(2):
            pairs.append((yield shared(acts[g], key_value_w[g])))
        keys = [pair[:, :128].astype(BF) for pair in pairs]
        values = [pair[:, 128:] for pair in pairs]
        keys_all = [
            jnp.concatenate([keys[0][q * 16 : q * 16 + 16], of_quadrant(keys[1], q, 4)], 0)
            for q in range(4)
        ]
        values_all = jnp.concatenate(
            [
                jnp.concatenate(
                    [values[0][q * 16 : q * 16 + 16], of_quadrant(values[1], q, 4)], 0
                )
                for q in range(4)
            ],
            1,
        )
        values_s[slot] = values_all
        yield
        moved = cell_moves(values_all, fine)
        taps4 = jnp.concatenate([value_filter[...]] * 4, 1)
        yield
        enhanced = []
        for block in range(5):
            total = values_all[block * 16 : block * 16 + 16]
            for tap in range(9):
                total = total + moved[tap][block] * taps4[tap : tap + 1]
            enhanced.append(total)
        enhanced = jnp.concatenate(enhanced, 0).astype(BF)
        yield

        def both_heads(rows):
            return jnp.concatenate(
                [jnp.where(lane80 < 64, rows, zero80), jnp.where(lane80 < 64, zero80, rows)], 0
            )

        queries = queries_s[slot]
        scores = []
        for q in range(4):
            keys_s[slot, q] = both_heads(keys_all[q])
            enhanced_s[slot, q] = both_heads(enhanced[:, q * 128 : q * 128 + 128])
            scores.append(mm(keys_s[slot, q], of_quadrant(queries, q, 16), NT))
        yield
        offset = fine.astype(F32) * bias[...]
        for q in range(4):
            biased = scores[q] * (scaling * math.log2(math.e)) + offset
            for lo, hi in segments:
                part = biased[lo:hi]
                part = jnp.exp2(part - jnp.max(part, 0, keepdims=True))
                probs[slot, q, lo:hi, :] = part * (1.0 / jnp.sum(part, 0, keepdims=True))
        yield
        mixed_parts = [
            mm(probs[slot, q].astype(BF), enhanced_s[slot, q], TN) for q in range(4)
        ]
        yield
        mixed = of_quadrants(mixed_parts, 16).astype(BF)
        mixed_s[slot] = mixed
        middle = x + mm(mixed, mixing_t[...], NT)
        middle_s[slot] = middle
        yield
        unit2, scale2 = normalise(middle)
        unit2_s[slot] = unit2
        scale2_s[slot] = scale2
        second_low = (unit2 * gain(3) + shift_by(3)).astype(BF)
        second_f = second_low.astype(F32)
        yield
        moved_blocks = {}

        def neighbour(block, down, across):
            a4, b4 = place_of(block)
            na, wa = wrap(a4, down)
            nb, wb = wrap(b4, across)
            key = (block_of(na, nb), wa, wb)
            if key not in moved_blocks:
                rows = second_f[key[0] * 64 : key[0] * 64 + 64]
                moved_blocks[key] = move(rows, fine, wa, wb) if wa or wb else rows
            return moved_blocks[key]

        for block in range(8):
            for column in range(3):
                above, first, second = [neighbour(block, d, column - 1) for d in (-1, 0, 1)]
                below = neighbour(block + 8, 1, column - 1)
                for n, part in enumerate(
                    (above - second, first + second, second - first, below - first)
                ):
                    rows_in[
                        n,
                        slot * 512 + block * 64 : slot * 512 + block * 64 + 64,
                        column * 128 : column * 128 + 128,
                    ] = part.astype(BF)
            yield
    def feed():
        def halves(ref):
            return [
                jnp.concatenate([ref[k, h * 512 : h * 512 + 512, :] for k in range(PAIR)], 0)
                for h in range(2)
            ]

        totals, ups = halves(middle_s), halves(up_s)
        wide = 256
        held = None
        for c in range(0, ff + wide, wide):
            if c < ff:
                cols = slice(c, c + wide)
                m = [mm(rows_in[n], conv_w[n, :, cols]) for n in range(4)]
                hidden = (m[1] + m[0] + m[2], m[1] - m[2] + m[3])
                grads = [mm(ups[h], shrink_t[:, cols]) for h in range(2)]
            if c == 0:
                for n in range(4):
                    for column in range(3):
                        rows = slice(column * 128, column * 128 + 128)
                        rows_in_t[n, rows, :] = rows_in[n, :, rows].T
                ups_t = [ups[h].T for h in range(2)]
            if held:
                before, acts, backs = held
                for h in range(2):
                    totals[h] = totals[h] + mm(acts[h], shrink_t[:, before], NT)
                d_shrink_t[:, before] += mm(ups_t[0], acts[0]) + mm(ups_t[1], acts[1])
                for n in range(4):
                    m_sum[n, :, before] += mm(rows_in_t[n], backs[n])
            if c < ff:
                acts, gs = [], []
                for h in range(2):
                    act, slope = scaled_gelu_pair(hidden[h])
                    acts.append(act.astype(BF))
                    gs.append(grads[h] * slope)
                backs = [
                    v.astype(BF) for v in (gs[0], gs[0] + gs[1], gs[0] - gs[1], gs[1])
                ]
                for n in range(4):
                    g_low[n, :, cols] = backs[n]
                held = (cols, acts, backs)
        for n in range(4):
            folds[n] = mm(g_low[n], conv_w[n], NT)
        for k in range(PAIR):
            total = jnp.concatenate([totals[h][k * 512 : k * 512 + 512] for h in range(2)], 0)
            restore(total.astype(BF), out, k)

    def gather_folds(slot, grid):
        fine = fine_of(grid)
        sums = {}
        for block in range(8):
            for column in range(3):
                for down, other, terms in (
                    (-1, block, ((0, 1),)),
                    (0, block, ((1, 1), (2, -1), (3, -1))),
                    (1, block, ((1, 1), (2, 1), (0, -1))),
                    (1, block + 8, ((3, 1),)),
                ):
                    a4, b4 = place_of(other)
                    na, wa = wrap(a4, down)
                    nb, wb = wrap(b4, column - 1)
                    key = (block_of(na, nb), wa, wb)
                    sums.setdefault(key, []).extend((block, column, n, sign) for n, sign in terms)
        for block in range(16):
            total = None
            for (source, wa, wb), terms in sums.items():
                if source != block:
                    continue
                part = None
                for other, column, n, sign in terms:
                    term = folds[
                        n,
                        slot * 512 + other * 64 : slot * 512 + other * 64 + 64,
                        column * 128 : column * 128 + 128,
                    ]
                    if part is None:
                        part = term if sign > 0 else -term
                    else:
                        part = part + term if sign > 0 else part - term
                if wa or wb:
                    part = move(part, fine, -wa, -wb)
                total = part if total is None else total + part
            second_grad_s[slot, block * 64 : block * 64 + 64, :] = total

    def back(slot, grid):
        fine = fine_of(grid)
        second_grad = second_grad_s[slot]
        unit2 = unit2_s[slot]
        add_norm(3, second_grad, unit2)
        middle_grad = up_s[slot].astype(F32) + normalise_back(
            second_grad * gain(3), unit2, scale2_s[slot]
        )
        middle_low = middle_grad.astype(BF)
        yield
        mixed_grad = mm(middle_low, mixing_t[...]).astype(BF)
        queries = queries_s[slot]
        yield
        d_mixing_t[...] += mm(middle_low, mixed_s[slot], TN)
        yield
        out_grads = [of_quadrant(mixed_grad, q, 16) for q in range(4)]
        prob_grads = [mm(enhanced_s[slot, q], out_grads[q], NT) for q in range(4)]
        yield
        enhanced_parts = []
        for q in range(4):
            full = mm(probs[slot, q].astype(BF), out_grads[q])
            enhanced_parts.append(jnp.where(lane80 < 64, full[:80], full[80:]).astype(BF))
        yield
        score_lows = []
        for q in range(4):
            weights = probs[slot, q]
            product = weights * prob_grads[q]
            score_grad = []
            for lo, hi in segments:
                score_grad.append(
                    product[lo:hi] - weights[lo:hi] * jnp.sum(product[lo:hi], 0, keepdims=True)
                )
            score_lows.append((scaling * jnp.concatenate(score_grad, 0)).astype(BF))
        yield
        query_parts = [mm(score_lows[q], keys_s[slot, q], TN) for q in range(4)]
        yield
        key_parts = []
        for q in range(4):
            full = mm(score_lows[q], of_quadrant(queries, q, 16))
            key_parts.append(jnp.where(lane80 < 64, full[:80], full[80:]).astype(BF))
        yield
        query_low = of_quadrants(query_parts, 16).astype(BF)
        enhanced_grad = jnp.concatenate(enhanced_parts, 1)
        yield
        enhanced_grad = enhanced_grad.astype(F32)
        moved = cell_moves(enhanced_grad, fine)
        taps4 = jnp.concatenate([value_filter[...]] * 4, 1)
        yield
        value_grad = []
        for block in range(5):
            total = enhanced_grad[block * 16 : block * 16 + 16]
            for tap in range(9):
                total = total + moved[8 - tap][block] * taps4[tap : tap + 1]
            value_grad.append(total)
        value_grad = jnp.concatenate(value_grad, 0).astype(BF)
        yield
        values_all = values_s[slot]
        for tap in range(9):
            part = None
            for block in range(5):
                product = moved[8 - tap][block] * values_all[block * 16 : block * 16 + 16]
                part = product if part is None else part + product
            part = part[:, :128] + part[:, 128:256] + part[:, 256:384] + part[:, 384:]
            d_value[tap : tap + 1, :] += jnp.sum(part, 0, keepdims=True)
        value_parts = [value_grad[:, q * 128 : q * 128 + 128] for q in range(4)]
        yield
        narrow = [jnp.concatenate([p[:16] for p in parts], 0) for parts in (key_parts, value_parts)]
        wide = [of_quadrants([p[16:] for p in parts], 4) for parts in (key_parts, value_parts)]
        pairs = [jnp.concatenate(sides, 1) for sides in (narrow, wide)]
        cell_grads = []
        for g in range(2):
            cell_grads.append((yield shared(pairs[g], key_value_w[g], NT)))
        normed_grad = mm(query_low, entry[0], NT)
        yield
        reduced_lows = []
        for g in range(2):
            unit, slope = cells_f[g][slot, 0], cells_f[g][slot, 1]
            cell_grad = cell_grads[g] * slope
            add_norm(1 + g, cell_grad, unit)
            reduced_lows.append(
                normalise_back(cell_grad * gain(1 + g), unit, cells_scale[g][slot]).astype(BF)
            )
        yield
        d_entry[0] += mm(normed_s[slot], query_low, TN)
        yield
        spreads = []
        for g in range(2):
            spreads.append((yield shared(reduced_lows[g], reduce_low[rows_of[g], :], NT)))
        for g in range(2):
            yield summed(d_key_value, g, cells_f[g][slot, 2].astype(BF), pairs[g])
        for g in range(2):
            if g == 0:
                order = [place_of(block) for block in range(16)]
                order = [a4 * 4 + b4 for a4, b4 in order]
            else:
                order = range(4)
            normed_grad = normed_grad + jnp.concatenate(
                [spreads[g][:, t * 128 : t * 128 + 128] for t in order], 0
            )
        yield
        for g in range(2):
            columns = (slice(None), rows_of[g])
            yield summed(d_reduce_t, columns, reduced_lows[g], patches_of(slot, g))
        unit1 = unit1_s[slot]
        add_norm(0, normed_grad, unit1)
        raw = middle_grad + normalise_back(normed_grad * gain(0), unit1, scale1_s[slot])
        restore(raw.astype(BF), input_low, slot, input_grad)
        yield

    def together(*parts):
        answers = [None] * len(parts)
        while True:
            asked = []
            for part, answer in zip(parts, answers):
                try:
                    asked.append(part.send(answer))
                except StopIteration:
                    pass
            if not asked:
                return
            answers = [None] * len(parts)
            if asked[0] is None:
                continue
            ref, place, left, right, dims = asked[0]
            left = jnp.concatenate([ask[2] for ask in asked], 0)
            if ref is None:
                whole = mm(left, right, dims)
                size = whole.shape[0] // len(asked)
                answers = [whole[n * size : (n + 1) * size] for n in range(len(asked))]
            else:
                ref[place] += mm(left, jnp.concatenate([ask[3] for ask in asked], 0), dims)

    first = PAIR * step
    together(*[attend(k, first + k) for k in range(PAIR)])

    feed()
    for k in range(PAIR):
        gather_folds(k, first + k)
    together(*[back(k, first + k) for k in range(PAIR)])

    @pl.when(step == last)
    def finish():
        gains = [hidden_filter[tap : tap + 1, :] * ROOT for tap in range(9)]
        gains[4] = gains[4] + ROOT
        for c in range(0, ff, 128):
            cols = slice(c, c + 128)
            taps = [None] * 9
            for r in range(0, 128, 64):
                weight = expand[r : r + 64, cols]
                total = None
                for column in range(3):
                    rows = slice(column * 128 + r, column * 128 + r + 64)
                    one, two = m_sum[1, rows, cols], m_sum[2, rows, cols]
                    both = (one + two) * 0.5
                    for a in range(3):
                        if a == 1:
                            part = (one - two) * 0.5
                        else:
                            part = m_sum[a // 2 * 3, rows, cols] + both
                        tap = 3 * a + column
                        row = jnp.sum(part * weight, 0, keepdims=True)
                        taps[tap] = row if taps[tap] is None else taps[tap] + row
                        part = part * gains[tap][:, cols]
                        total = part if total is None else total + part
                wide_s[0, r : r + 64, cols] = total
            for tap in range(9):
                hidden_filter[tap : tap + 1, cols] = taps[tap] * ROOT
        wide_s[1] = d_shrink_t[...]
        d_entry[1] = jnp.where(
            first_lanes, d_key_value[0, :, :128], pltpu.roll(d_key_value[0, :, 128:], 32, 1)
        )
        d_entry[2] = jnp.where(
            first_lanes, pltpu.roll(d_key_value[1, :, :128], 96, 1), d_key_value[1, :, 128:]
        )
        is_second = head[0] == 1
        d_reduce = reduce_w
        for n in range(20):
            rows = slice(n * 128, n * 128 + 128)
            d_reduce[rows, :] = d_reduce_t[:, rows].T
        top, chunk = 12 * width, ff // 256
        planes = mine.shape[1]

        def put(d, rows, first, second):
            place = (d // planes, d % planes, rows)
            mine[place] = jnp.where(is_second, second, first)
            theirs[place] = jnp.where(is_second, first, second).astype(BF)

        for d in range(devices):
            rows = slice(width * d, width * d + width)
            upper = d_reduce[20 * width * d : 20 * width * d + top, :]
            lower = jnp.concatenate(
                [d_reduce[20 * width * d + top : 20 * width * (d + 1), :]]
                + [d_entry[e, rows, :] for e in range(3)]
                + [d_mixing_t[rows, :]],
                0,
            )
            firsts = [jnp.where(left(top), upper, pltpu.roll(lower, 64, 1))]
            seconds = [jnp.where(left(top), pltpu.roll(upper, 64, 1), lower)]
            for n in range(2):
                for h, parts in enumerate((firsts, seconds)):
                    for u in range(chunk):
                        cols = slice((h * chunk + u) * 128, (h * chunk + u + 1) * 128)
                        parts.append(wide_s[n, rows, cols])
            pad = mine.shape[2] - 20 * width
            if pad:
                firsts.append(jnp.zeros((pad, 128), F32))
                seconds.append(jnp.zeros((pad, 128), F32))
            put(d, slice(None), jnp.concatenate(firsts, 0), jnp.concatenate(seconds, 0))
        count = jnp.int32(0)
        for n in range(steps):
            side = resolution[head[0] * steps + n]
            count = count + side * side * live_images[head[0] * steps + n]
        halves = [
            jnp.concatenate(
                [
                    hidden_filter[:, (h * chunk + u) * 128 : (h * chunk + u + 1) * 128]
                    for u in range(chunk)
                ],
                0,
            )
            for h in range(2)
        ]
        for ref, flip in ((small_mine, False), (small_theirs, True)):
            ref[...] = jnp.zeros_like(ref)
            ref[:8, :] = d_norm[...]
            ref[8:17, :] = d_value[...]
            ref[17:18, :] = jnp.full((1, 128), count, jnp.int32).astype(F32)
            second = jnp.logical_not(is_second) if flip else is_second
            ref[18 : 18 + 9 * chunk, :] = jnp.where(second, halves[1], halves[0])


def run_block(resolution, live_images, head, tokens, cotangent, packed, filters, norms):
    steps = tokens.shape[0] // 2
    devices, rows = packed.shape[0] // 2, packed.shape[1] - 16
    ff = 2 * (filters.shape[2] - 128)
    lines = line_of(devices)
    consts = [
        jnp.asarray(order_matrix(), BF),
        jnp.asarray(order_matrix().T, BF),
        jnp.asarray(score_bias(), F32),
        jnp.asarray(shift_masks(), F32),
    ]
    whole = [packed, filters, norms] + consts

    def all_of(a):
        return pl.BlockSpec(a.shape, lambda i, *_, n=a.ndim: (0,) * n)

    grid_in = pl.BlockSpec(
        (PAIR, 32, 32, 128), lambda i, res, live, head: (head[0] * (steps // PAIR) + i, 0, 0, 0)
    )
    grid_out = pl.BlockSpec((PAIR, 32, 32, 128), lambda i, *_: (i, 0, 0, 0))
    out_shape = [
        jax.ShapeDtypeStruct((2 * steps, 32, 32, 128), BF),
        jax.ShapeDtypeStruct((2 * steps, 32, 32, 128), F32),
        jax.ShapeDtypeStruct((steps, 32, 32, 128), BF),
        jax.ShapeDtypeStruct((lines, devices // lines, rows, 128), F32),
        jax.ShapeDtypeStruct((lines, devices // lines, rows, 128), BF),
        jax.ShapeDtypeStruct((SMALL, 128), F32),
        jax.ShapeDtypeStruct((SMALL, 128), F32),
        jax.ShapeDtypeStruct((8, 128), F32),
    ]

    def kernel(*refs):
        block_kernel(*refs, steps=steps)

    return pl.pallas_call(
        kernel,
        out_shape=out_shape,
        grid_spec=pltpu.PrefetchScalarGridSpec(
            num_scalar_prefetch=3,
            grid=(steps // PAIR,),
            in_specs=[grid_in, grid_in] + [all_of(a) for a in whole],
            out_specs=[grid_in, grid_in, grid_out] + [all_of(a) for a in out_shape[3:]],
            scratch_shapes=[
                pltpu.VMEM((3, 128, 128), BF),
                pltpu.VMEM((128, 128), BF),
                pltpu.VMEM((128, ff), F32),
                pltpu.VMEM((128, ff), BF),
                pltpu.VMEM((2560, 128), F32),
                pltpu.VMEM((9, 128), F32),
                pltpu.VMEM((9, ff), F32),
                pltpu.VMEM((2, 128, ff), F32),
                pltpu.VMEM((4, 128, 128), F32),
                pltpu.VMEM((3, 128, 128), F32),
                pltpu.VMEM((128, 128), F32),
                pltpu.VMEM((128, ff), F32),
                pltpu.VMEM((128, 2560), F32),
                pltpu.VMEM((8, 128), F32),
                pltpu.VMEM((9, 128), F32),
                pltpu.VMEM((4, 384, ff), BF),
                pltpu.VMEM((2, 128, 256), BF),
                pltpu.VMEM((4, PAIR * 512, ff), BF),
                pltpu.VMEM((4, 384, ff), F32),
                pltpu.VMEM((4, PAIR * 512, 384), F32),
                pltpu.VMEM((2, 128, 256), F32),
                pltpu.VMEM((2560, 128), BF),
                pltpu.VMEM((4, PAIR * 512, 384), BF),
                pltpu.VMEM((4, 384, PAIR * 512), BF),
                pltpu.VMEM((2, 1024, 128), F32),
                pltpu.VMEM((2, 1024, 128), BF),
                pltpu.VMEM((2, 1024, 128), F32),
                pltpu.VMEM((2, 1024, 1), F32),
                pltpu.VMEM((2, 1024, 128), F32),
                pltpu.VMEM((2, 1024, 1), F32),
                pltpu.VMEM((2, 1024, 128), BF),
                pltpu.VMEM((2, 1024, 128), BF),
                pltpu.VMEM((2, 1024, 128), BF),
                pltpu.VMEM((2, 4, 160, 256), F32),
                pltpu.VMEM((2, 4, 160, 128), BF),
                pltpu.VMEM((2, 4, 160, 128), BF),
                pltpu.VMEM((2, 80, 512), F32),
                pltpu.VMEM((2, 3, 64, 128), F32),
                pltpu.VMEM((2, 64, 1), F32),
                pltpu.VMEM((2, 3, 256, 128), F32),
                pltpu.VMEM((2, 256, 1), F32),
                pltpu.VMEM((2, 1024, 128), F32),
                pltpu.VMEM((1, 128), F32),
            ],
        ),
        compiler_params=pltpu.CompilerParams(
            dimension_semantics=("arbitrary",), vmem_limit_bytes=LIMIT
        ),
        name="block",
    )(resolution, live_images, head, tokens, cotangent, *whole)


def line_of(devices):
    return 4 if devices % 4 == 0 else 1


def rows_of_block(devices):
    return -(-20 * (128 // devices) // 16) * 16


def pack(
    head,
    resolution,
    live_images,
    entry,
    mixing_t,
    expand,
    shrink_t,
    reduce_t,
    values,
    hidden,
    block,
    filters,
    held,
):
    width, ff = expand.shape
    top, chunk = 12 * width, ff // 128
    held[...] = jnp.zeros_like(held)
    rows = reduce_t[...].T
    held[:top, :64] = rows[:top, :]
    held[: 8 * width, 64:] = rows[top:, :]
    for e in range(3):
        held[(8 + e) * width : (9 + e) * width, 64:] = entry[e]
    held[11 * width : top, 64:] = mixing_t[...]
    for u in range(chunk):
        cols = slice(u * 128, (u + 1) * 128)
        held[top + u * width : top + (u + 1) * width, :] = expand[:, cols]
        held[top + (chunk + u) * width : top + (chunk + u + 1) * width, :] = shrink_t[:, cols]
    half = live_images.shape[0] // 2
    count = jnp.int32(0)
    for n in range(half):
        side = resolution[head * half + n]
        count = count + side * side * live_images[head * half + n]
    count = count // 64
    last = held.shape[0] - 16
    held[last : last + 1, :] = jnp.full((1, 128), count % 256, jnp.int32).astype(F32)
    held[last + 1 : last + 2, :] = jnp.full((1, 128), count // 256, jnp.int32).astype(F32)
    block[...] = held[...].astype(BF)
    filters[...] = jnp.zeros_like(filters)
    filters[:9, :ff] = hidden[...]
    for g in range(2):
        filters[:9, ff + 32 * g : ff + 32 * g + 32] = values[:, g]


def greet(peers, meanwhile=None):
    barrier = pltpu.get_barrier_semaphore()
    for peer in peers:
        pl.semaphore_signal(barrier, inc=1, device_id=peer, device_id_type=MESH)
    if meanwhile is not None:
        meanwhile()
    pl.semaphore_wait(barrier, len(peers))


def places(devices):
    lines = line_of(devices)
    planes = devices // lines
    me, head = lax.axis_index("dp"), lax.axis_index("head")
    z, p = me // planes, me % planes
    line_peers = [((z + k) % lines) for k in range(1, lines)]
    plane_peers = [((p + k) % planes) for k in range(1, planes)]
    return lines, planes, z, p, head, line_peers, plane_peers


def gather_kernel(
    devices,
    resolution,
    live_images,
    entry,
    mixing_t,
    expand,
    shrink_t,
    reduce_t,
    values,
    hidden,
    blocks,
    both,
    block,
    filters,
    held,
    send_sem,
    recv_sem,
    filter_sem,
    local_sem,
):
    lines, planes, z, p, head, line_peers, plane_peers = places(devices)

    def slot(line, plane, core):
        return (line * planes + plane) * 2 + core

    def at(line, plane, core):
        return (line * planes + plane, core)

    sibling = at(z, p, 1 - head)
    greet(
        [at(k, p, head) for k in line_peers] + [at(z, k, head) for k in plane_peers] + [sibling],
        lambda: pack(
            head,
            resolution,
            live_images,
            entry,
            mixing_t,
            expand,
            shrink_t,
            reduce_t,
            values,
            hidden,
            block,
            filters,
            held,
        ),
    )
    sends = []

    def send(source, index, target):
        copy = pltpu.make_async_remote_copy(
            src_ref=source,
            dst_ref=blocks.at[index],
            send_sem=send_sem.at[len(sends)],
            recv_sem=recv_sem.at[index],
            device_id=target,
            device_id_type=MESH,
        )
        copy.start()
        sends.append(copy)

    def arrived(index):
        pltpu.make_async_remote_copy(
            src_ref=block,
            dst_ref=blocks.at[index],
            send_sem=send_sem.at[0],
            recv_sem=recv_sem.at[index],
            device_id=sibling,
            device_id_type=MESH,
        ).wait_recv()

    own = slot(z, p, head)
    for k in line_peers:
        send(block, own, at(k, p, head))
    for k in plane_peers:
        send(block, own, at(z, k, head))
    send(block, own, sibling)
    swap = pltpu.make_async_remote_copy(
        src_ref=filters,
        dst_ref=both.at[head],
        send_sem=filter_sem.at[0],
        recv_sem=filter_sem.at[1],
        device_id=sibling,
        device_id_type=MESH,
    )
    swap.start()
    keep = [
        pltpu.make_async_copy(block, blocks.at[own], local_sem.at[0]),
        pltpu.make_async_copy(filters, both.at[head], local_sem.at[1]),
    ]
    for copy in keep:
        copy.start()
    for k in line_peers:
        index = slot(k, p, head)
        arrived(index)
        for j in plane_peers:
            send(blocks.at[index], index, at(z, j, head))
        send(blocks.at[index], index, sibling)
    for line in [z] + line_peers:
        for j in plane_peers:
            index = slot(line, j, head)
            arrived(index)
            send(blocks.at[index], index, sibling)
    for line in [z] + line_peers:
        for j in [p] + plane_peers:
            arrived(slot(line, j, 1 - head))
    for copy in sends:
        copy.wait_send()
    swap.wait_send()
    pltpu.make_async_remote_copy(
        src_ref=filters,
        dst_ref=both.at[1 - head],
        send_sem=filter_sem.at[0],
        recv_sem=filter_sem.at[1],
        device_id=sibling,
        device_id_type=MESH,
    ).wait_recv()
    for copy in keep:
        copy.wait()


def run_gather(devices, resolution, live_images, *weights):
    lines = line_of(devices)
    planes = devices // lines
    copies = (lines - 1) + lines * (planes - 1) + lines * planes
    rows = rows_of_block(devices) + 16
    filters = (16, weights[-1].shape[1] + 128)
    smem = pl.BlockSpec(memory_space=pltpu.SMEM)
    vmem = pl.BlockSpec(memory_space=pltpu.VMEM)

    def kernel(*refs):
        gather_kernel(devices, *refs)

    return pl.pallas_call(
        kernel,
        out_shape=[
            jax.ShapeDtypeStruct((2 * devices, rows, 128), BF),
            jax.ShapeDtypeStruct((2,) + filters, F32),
        ],
        in_specs=[smem] * 2 + [vmem] * len(weights),
        out_specs=[pl.BlockSpec(memory_space=pl.ANY)] * 2,
        scratch_shapes=[
            pltpu.VMEM((rows, 128), BF),
            pltpu.VMEM(filters, F32),
            pltpu.VMEM((rows, 128), F32),
            pltpu.SemaphoreType.DMA((copies,)),
            pltpu.SemaphoreType.DMA((2 * devices,)),
            pltpu.SemaphoreType.DMA((2,)),
            pltpu.SemaphoreType.DMA((2,)),
        ],
        compiler_params=pltpu.CompilerParams(
            collective_id=0, has_side_effects=True, vmem_limit_bytes=LIMIT
        ),
        name="gather",
    )(resolution, live_images, *weights)


def reduce_kernel(
    devices,
    mine_far,
    theirs,
    small_mine,
    small_theirs,
    out_half,
    input_half,
    grad,
    small,
    out_other,
    input_other,
    mine,
    core_in,
    core_small,
    plane_out,
    plane_in,
    plane_small,
    line_out,
    line_in,
    line_small,
    core_send,
    core_recv,
    plane_send,
    plane_recv,
    line_send,
    line_recv,
    local_sem,
):
    lines, planes, z, p, head, line_peers, plane_peers = places(devices)
    half = input_half.shape[0]
    fetch = pltpu.make_async_copy(mine_far, mine, local_sem.at[0])
    fetch.start()

    def at(line, plane, core):
        return (line * planes + plane, core)

    sibling = at(z, p, 1 - head)
    greet(
        [at(k, p, head) for k in line_peers] + [at(z, k, head) for k in plane_peers] + [sibling]
    )

    def remote(source, target, send, recv, device):
        return pltpu.make_async_remote_copy(
            src_ref=source,
            dst_ref=target,
            send_sem=send,
            recv_sem=recv,
            device_id=device,
            device_id_type=MESH,
        )

    started = []

    def go(*args):
        copy = remote(*args)
        copy.start()
        started.append(copy)

    order = line_peers + [z]
    go(small_theirs, core_small, core_send.at[lines], core_recv.at[lines], sibling)
    for a in order:
        go(theirs.at[a], core_in.at[a], core_send.at[a], core_recv.at[a], sibling)
    remote(
        small_theirs, core_small, core_send.at[lines], core_recv.at[lines], sibling
    ).wait_recv()
    plane_small[pl.ds(p, 1)] = (small_mine[...] + core_small[...]).astype(BF)[None]
    for n, k in enumerate(plane_peers):
        go(
            plane_small.at[p],
            plane_small.at[p],
            plane_send.at[lines * (planes - 1) + n],
            plane_recv.at[lines * planes + p],
            at(z, k, head),
        )
    fetch.wait()
    for m, a in enumerate(order):
        remote(
            theirs.at[a], core_in.at[a], core_send.at[a], core_recv.at[a], sibling
        ).wait_recv()
        both = mine[pl.ds(a, 1)] + core_in[pl.ds(a, 1)].astype(F32)
        plane_out[pl.ds(a, 1)] = both.astype(BF)
        for n, k in enumerate(plane_peers):
            go(
                plane_out.at[a, k],
                plane_in.at[a, p],
                plane_send.at[m * (planes - 1) + n],
                plane_recv.at[a * planes + p],
                at(z, k, head),
            )
    own_out = out_half.at[pl.ds(head * half, half)]
    go(own_out, out_other, core_send.at[lines + 1], core_recv.at[lines + 1], sibling)
    go(input_half, input_other, core_send.at[lines + 2], core_recv.at[lines + 2], sibling)
    for k in plane_peers:
        remote(
            plane_small.at[p],
            plane_small.at[k],
            plane_send.at[0],
            plane_recv.at[lines * planes + k],
            sibling,
        ).wait_recv()
    part = plane_small[0].astype(F32)
    for k in range(1, planes):
        part = part + plane_small[k].astype(F32)
    line_small[pl.ds(z, 1)] = part.astype(BF)[None]
    for n, k in enumerate(line_peers):
        go(
            line_small.at[z],
            line_small.at[z],
            line_send.at[lines + n],
            line_recv.at[lines + z],
            at(k, p, head),
        )
    own = None
    for m, a in enumerate(order):
        total = (
            mine[pl.ds(a, 1), pl.ds(p, 1)] + core_in[pl.ds(a, 1), pl.ds(p, 1)].astype(F32)
        )[0, 0]
        for k in plane_peers:
            remote(
                plane_out.at[a, k],
                plane_in.at[a, k],
                plane_send.at[0],
                plane_recv.at[a * planes + k],
                sibling,
            ).wait_recv()
            total = total + plane_in[pl.ds(a, 1), pl.ds(k, 1)][0, 0].astype(F32)
        if m < lines - 1:
            line_out[pl.ds(a, 1)] = total.astype(BF)[None]
            go(line_out.at[a], line_in.at[z], line_send.at[m], line_recv.at[z], at(a, p, head))
        else:
            own = total
    for k in line_peers:
        remote(
            line_out.at[k], line_in.at[k], line_send.at[0], line_recv.at[k], sibling
        ).wait_recv()
        own = own + line_in[pl.ds(k, 1)][0].astype(F32)
    grad[...] = own
    for k in line_peers:
        remote(
            line_small.at[z],
            line_small.at[k],
            line_send.at[0],
            line_recv.at[lines + k],
            sibling,
        ).wait_recv()
    part = line_small[0].astype(F32)
    for k in range(1, lines):
        part = part + line_small[k].astype(F32)
    small[...] = part
    remote(
        own_out, out_other, core_send.at[lines + 1], core_recv.at[lines + 1], sibling
    ).wait_recv()
    remote(
        input_half, input_other, core_send.at[lines + 2], core_recv.at[lines + 2], sibling
    ).wait_recv()
    for copy in started:
        copy.wait_send()


def run_reduce(devices, mine, theirs, small_mine, small_theirs, out_half, input_half):
    lines, planes, rows = mine.shape[:3]
    anywhere = pl.BlockSpec(memory_space=pl.ANY)
    vmem = pl.BlockSpec(memory_space=pltpu.VMEM)
    sem = pltpu.SemaphoreType.DMA

    def kernel(*refs):
        reduce_kernel(devices, *refs)

    return pl.pallas_call(
        kernel,
        out_shape=[
            jax.ShapeDtypeStruct((rows, 128), F32),
            jax.ShapeDtypeStruct((SMALL, 128), F32),
            jax.ShapeDtypeStruct(input_half.shape, BF),
            jax.ShapeDtypeStruct(input_half.shape, BF),
        ],
        in_specs=[anywhere] * 2 + [vmem] * 2 + [anywhere] * 2,
        out_specs=[vmem] * 2 + [anywhere] * 2,
        scratch_shapes=[
            pltpu.VMEM((lines, planes, rows, 128), F32),
            pltpu.VMEM((lines, planes, rows, 128), BF),
            pltpu.VMEM((SMALL, 128), F32),
            pltpu.VMEM((lines, planes, rows, 128), BF),
            pltpu.VMEM((lines, planes, rows, 128), BF),
            pltpu.VMEM((planes, SMALL, 128), BF),
            pltpu.VMEM((lines, rows, 128), BF),
            pltpu.VMEM((lines, rows, 128), BF),
            pltpu.VMEM((lines, SMALL, 128), BF),
            sem((lines + 3,)),
            sem((lines + 3,)),
            sem((lines * (planes - 1) + planes,)),
            sem((lines * planes + planes,)),
            sem((2 * lines,)),
            sem((2 * lines,)),
            sem((1,)),
        ],
        compiler_params=pltpu.CompilerParams(
            collective_id=1, has_side_effects=True, vmem_limit_bytes=LIMIT
        ),
        name="reduce",
    )(mine, theirs, small_mine, small_theirs, out_half, input_half)


def advance(weight, moment, average, gradient, step_rate, weight_decay):
    gradient = gradient + weight_decay * weight
    moment = 0.9 * moment + gradient
    weight = weight - step_rate * (gradient + 0.9 * moment)
    return (moment, weight, 0.8 * average + 0.2 * weight)


RATES = (0.3, 0.12, 0.12, 0.03, 0.1, 0.2, 0.4, 0.5)


def update_kernel(head, *refs, tokens_all):
    out_other, in_other, grad, small, scales = refs[:5]
    state = refs[7:31]
    output, input_grad = refs[31:33]
    results = refs[33:]
    step = pl.program_id(0)
    factor = scales[:1, :]
    output[...] = out_other[...]
    input_grad[...] = in_other[...].astype(F32) * factor

    @pl.when(step == 0)
    def update():
        width, ff = state[6].shape
        top, chunk = 12 * width, ff // 128
        rate_unit = tokens_all**-0.5

        def apply(n, place, raw, scale):
            new = advance(
                state[3 * n][place],
                state[3 * n + 1][place],
                state[3 * n + 2][place],
                scale * raw,
                RATES[n] * rate_unit,
                0.0 if n == 5 else 0.05,
            )
            for k in range(3):
                results[3 * n + k][place] = new[k]

        scale = factor[:, :64]
        for e in range(3):
            apply(0, e, grad[(8 + e) * width : (9 + e) * width, 64:], scale)
        apply(1, Ellipsis, grad[11 * width : top, 64:], scale)
        for u in range(chunk):
            cols = slice(u * 128, (u + 1) * 128)
            apply(2, (slice(None), cols), grad[top + u * width : top + (u + 1) * width, :], factor)
            apply(
                3,
                (slice(None), cols),
                grad[top + (chunk + u) * width : top + (chunk + u + 1) * width, :],
                factor,
            )
        turned = grad[:top, :].T
        apply(4, (slice(None), slice(0, top)), turned[:64, :], factor[:, :1])
        apply(4, (slice(None), slice(top, 20 * width)), turned[64:, : 8 * width], factor[:, :1])
        for n in range(2):
            apply(5, n, small[4 * n : 4 * n + 4, :], factor)
        values = small[8:17, :]
        values = jnp.where(head[0] == 1, pltpu.roll(values, 64, 1), values)
        for g in range(2):
            apply(6, (slice(None), g), values[:, 32 * g : 32 * g + 32], factor[:, :32])
        for u in range(chunk):
            apply(
                7,
                (slice(None), slice(u * 128, (u + 1) * 128)),
                small[18 + 9 * u : 27 + 9 * u, :],
                factor,
            )


def run_update(tokens_all, head, output, input_grad, out_other, in_other, grad, small, factor, state):
    half = out_other.shape[0]
    steps = 2

    def all_of(a):
        return pl.BlockSpec(a.shape, lambda i, *_, n=a.ndim: (0,) * n)

    block = (half // steps,) + out_other.shape[1:]
    other = pl.BlockSpec(block, lambda i, *_: (i, 0, 0, 0))
    final = pl.BlockSpec(block, lambda i, head: ((1 - head[0]) * steps + i, 0, 0, 0))
    anywhere = pl.BlockSpec(memory_space=pl.ANY)

    def kernel(*refs):
        update_kernel(*refs, tokens_all=tokens_all)

    return pl.pallas_call(
        kernel,
        out_shape=[jax.ShapeDtypeStruct(a.shape, a.dtype) for a in (output, input_grad, *state)],
        grid_spec=pltpu.PrefetchScalarGridSpec(
            num_scalar_prefetch=1,
            grid=(steps,),
            in_specs=[other, other, all_of(grad), all_of(small), all_of(factor), anywhere, anywhere]
            + [all_of(a) for a in state],
            out_specs=[final, final] + [all_of(a) for a in state],
        ),
        input_output_aliases={6: 0, 7: 1},
        compiler_params=pltpu.CompilerParams(
            dimension_semantics=("arbitrary",), vmem_limit_bytes=LIMIT
        ),
        name="update",
    )(head, out_other, in_other, grad, small, factor, output, input_grad, *state)


def per_device(
    tokens,
    cotangent,
    resolution,
    live_images,
    entry_weight,
    entry_momentum,
    entry_average,
    mixing_weight,
    mixing_momentum,
    mixing_average,
    expand_weight,
    expand_momentum,
    expand_average,
    shrink_weight,
    shrink_momentum,
    shrink_average,
    reduce_weight,
    reduce_momentum,
    reduce_average,
    norm_params,
    norm_momentum,
    norm_average,
    value_filter,
    value_momentum,
    value_average,
    hidden_filter,
    hidden_momentum,
    hidden_average,
):
    devices = lax.axis_size("dp")
    head = lax.axis_index("head").reshape(1).astype(jnp.int32)
    turns = ((1, 0), (1, 0), (1, 0), (1, 0, 2))
    mixing, shrink, reduced, values = [
        tuple(a.transpose(turn) for a in arrays)
        for turn, arrays in zip(
            turns,
            (
                (mixing_weight, mixing_momentum, mixing_average),
                (shrink_weight, shrink_momentum, shrink_average),
                (reduce_weight, reduce_momentum, reduce_average),
                (value_filter, value_momentum, value_average),
            ),
        )
    ]
    blocks, filters = run_gather(
        devices,
        resolution,
        live_images,
        entry_weight,
        mixing[0],
        expand_weight,
        shrink[0],
        reduced[0],
        values[0],
        hidden_filter,
    )
    output, input_grad, input_low, mine, theirs, small_mine, small_theirs, factor = run_block(
        resolution, live_images, head, tokens, cotangent, blocks, filters, norm_params
    )
    grad, small, out_other, input_other = run_reduce(
        devices, mine, theirs, small_mine, small_theirs, output, input_low
    )
    state = (
        entry_weight,
        entry_momentum,
        entry_average,
        *mixing,
        expand_weight,
        expand_momentum,
        expand_average,
        *shrink,
        *reduced,
        norm_params,
        norm_momentum,
        norm_average,
        *values,
        hidden_filter,
        hidden_momentum,
        hidden_average,
    )
    tokens_all = devices * tokens.shape[0] * tokens.shape[1] * tokens.shape[2]
    results = list(
        run_update(
            tokens_all,
            head,
            output,
            input_grad,
            out_other,
            input_other,
            grad,
            small,
            factor,
            state,
        )
    )
    for n, turn in zip((1, 3, 4, 6), turns):
        for k in range(2 + 3 * n, 5 + 3 * n):
            results[k] = results[k].transpose(turn)
    return tuple(results)


def solution(mesh):
    in_specs = (
        P("dp", None, None, None),
        P("dp", None, None, None),
        P("dp"),
        P("dp"),
        P(None, "dp", "head"),
        P(None, "dp", "head"),
        P(None, "dp", "head"),
        P("head", "dp"),
        P("head", "dp"),
        P("head", "dp"),
        P("dp", "head"),
        P("dp", "head"),
        P("dp", "head"),
        P("head", "dp"),
        P("head", "dp"),
        P("head", "dp"),
        P("dp", "head"),
        P("dp", "head"),
        P("dp", "head"),
        P(),
        P(),
        P(),
        P(None, None, "head"),
        P(None, None, "head"),
        P(None, None, "head"),
        P(None, "head"),
        P(None, "head"),
        P(None, "head"),
    )
    out_specs = (
        P("dp", None, None, None),
        P("dp", None, None, None),
        P(None, "dp", "head"),
        P(None, "dp", "head"),
        P(None, "dp", "head"),
        P("head", "dp"),
        P("head", "dp"),
        P("head", "dp"),
        P("dp", "head"),
        P("dp", "head"),
        P("dp", "head"),
        P("head", "dp"),
        P("head", "dp"),
        P("head", "dp"),
        P("dp", "head"),
        P("dp", "head"),
        P("dp", "head"),
        P(),
        P(),
        P(),
        P(None, None, "head"),
        P(None, None, "head"),
        P(None, None, "head"),
        P(None, "head"),
        P(None, "head"),
        P(None, "head"),
    )
    return jax.shard_map(
        per_device, mesh=mesh, in_specs=in_specs, out_specs=out_specs, check_vma=False
    )
```
